32 devices in a mesh: gx: 2 (over x), gy: 4 (over y, core), gz: 4 (over z).
Axes of the slice: x: 2, y: 2, z: 4, core: 2. Of those that a mesh axis runs over, the one named last changes fastest.
Arguments:
- basis: float32 [6, 4, 4, 8, 8, 512], P(None, None, None, 'gx', 'gy', 'gz'), may hold values from -15 to 15
- inverse_rows: bfloat16 [4, 8, 8, 192, 512], P(None, 'gx', 'gy', None, 'gz'), may hold values from -1 to 3
- block_diag: float32 [4, 4, 8, 8, 512], P(None, None, 'gx', 'gy', 'gz'), may hold values from -6 to 6
- couple: float32 [6, 4, 8, 8, 512], P(None, None, 'gx', 'gy', 'gz'), may hold values from 0.2 to 2
- coarse_basis: float32 [16, 4, 8, 8, 512], P(None, None, 'gx', 'gy', 'gz'), may hold values from -0.09375 to 0.09375
- coarse_factor: float32 [512, 512], P(('gx', 'gy', 'gz')), may hold values from -1 to 5, as said below
Outputs:
- krylov_next: float32 [4, 4, 8, 8, 512], P(None, None, 'gx', 'gy', 'gz')
- preconditioned: float32 [4, 4, 8, 8, 512], P(None, None, 'gx', 'gy', 'gz')
- hessenberg: float32 [4, 7], replicated
The draws below stay inside these ranges and needn't reach their ends.
Inputs may be any that keep to these rules, and one draw needn't show every extreme that they name: coarse_factor is zero above its diagonal.
All inputs are finite; a program needn't handle non-finite values.
Results may differ from the reference program's by a relative error of at most 0.0026.
Values may be sent and summed in bfloat16 or wider, within the bound.
No kernel may reach another device: no remote copies, remote signals or barrier semaphores. Data moves between devices by JAX's collectives and lax.ppermute only.
A program may use at most 64 MiB of HBM per device.

```python
import math
import jax
import jax.numpy as jnp
from jax import lax

C = 4
CX = 4
CY = 2
CZ = 128
S = 4
M = 6
K = 16
NX = 8
NY = 8
NZ = 512
ECOLS = 192
NC = 512
N_GX = 2
N_GY = 4
N_GZ = 4


def draw_basis(key, part):
    common_key, private_key, mixing_key = jax.random.split(jax.random.fold_in(key, 17), 3)
    x_position = jnp.arange(NX, dtype=jnp.float32) / (NX - 1)
    common = jax.random.truncated_normal(common_key, -3.0, 3.0, (S, C, NX, NY, NZ), jnp.float32)
    mixing = jax.random.uniform(mixing_key, (M, 1, 1, 1, 1, 1), jnp.float32, 0.3, 0.7)
    profile = (1.0 + 2.0 * x_position)[:, None, None] * jnp.ones((1, 1, NZ), jnp.float32)
    private = jax.random.truncated_normal(private_key, -3.0, 3.0, (M, S, C, NX, NY, NZ), jnp.float32)
    return mixing * profile * common + private


def draw_inverse_rows(key, part):
    off_key, diagonal_key = jax.random.split(jax.random.fold_in(key, 23), 2)
    component = jnp.arange(C, dtype=jnp.int32)[:, None, None, None, None]
    x_local = (jnp.arange(NX, dtype=jnp.int32) % CX)[None, :, None, None, None]
    y_local = (jnp.arange(NY, dtype=jnp.int32) % CY)[None, None, :, None, None]
    column = jnp.arange(ECOLS, dtype=jnp.int32)[None, None, None, :, None]
    on_diagonal = column == component * ((CX + 4) * (CY + 4)) + (x_local + 2) * (CY + 4) + y_local + 2
    off_values = jax.random.truncated_normal(off_key, -4.0, 4.0, (C, NX, NY, ECOLS, NZ), jnp.float32) * (0.6 / jnp.sqrt(jnp.float32(ECOLS)))
    diagonal = jax.random.uniform(diagonal_key, (C, NX, NY, 1, NZ), jnp.float32, 1.0, 2.0)
    return jnp.where(on_diagonal, diagonal, off_values).astype(jnp.bfloat16)


def draw_coarse_factor(key, part):
    off_key, diagonal_key = jax.random.split(jax.random.fold_in(key, 31), 2)
    row_index = jnp.arange(NC, dtype=jnp.int32)[:, None]
    column_index = jnp.arange(NC, dtype=jnp.int32)[None, :]
    off_values = jax.random.truncated_normal(off_key, -4.0, 4.0, (NC, NC), jnp.float32) * (2.0 / jnp.sqrt(jnp.float32(NC)))
    diagonal = jax.random.uniform(diagonal_key, (NC, 1), jnp.float32, 2.0, 4.0)
    below = jnp.where(column_index < row_index, off_values, 0.0)
    return below + jnp.where(column_index == row_index, diagonal, 0.0)


def shard_levels(rng, shape, cuts, low, top_value):
    def one(axis_at, shards_of):
        draws = jax.random.uniform(jax.random.fold_in(jax.random.fold_in(rng, 6), axis_at), (shards_of,), jnp.float32, low / len(cuts), top_value / len(cuts))
        return jnp.repeat(jnp.exp(draws), shape[axis_at] // shards_of).reshape((-1,) + (1,) * (len(shape) - axis_at - 1))

    factor_of = one(*cuts[0])
    for cut in cuts[1:]:
        factor_of = factor_of * one(*cut)
    return factor_of


def noise(key, extent, scale, bound, cuts=(), kind=jnp.bfloat16):
    drawn = jax.random.normal(key, extent, jnp.float32) * scale
    if len(cuts) > 0:
        drawn = shard_levels(key, extent, cuts, -0.22, 0.18) * drawn
    return jnp.clip(drawn, min=-bound, max=bound).astype(kind)


def setup_inputs(seed: int = 0) -> dict:
    streams_of = jax.random.split(jax.random.key(seed), 7)
    return {
        "basis": draw_basis(jax.random.fold_in(streams_of[6], 71), 0),
        "inverse_rows": draw_inverse_rows(jax.random.fold_in(streams_of[6], 71), 0),
        "block_diag": noise(streams_of[2], (C, C, NX, NY, NZ), 1.0, 6.0, ((2, 2), (3, 4), (4, 4)), jnp.float32),
        "couple": jnp.clip(jnp.exp(math.log(2.0) - 2.3025851 * jax.random.uniform(streams_of[3], (6, C, NX, NY, NZ), jnp.float32) ** shard_levels(streams_of[3], (6, C, NX, NY, NZ), ((2, 2), (3, 4), (4, 4)), -0.2, 0.2)), 0.2, 2.0),
        "coarse_basis": noise(streams_of[4], (K, C, NX, NY, NZ), (C * CX * CY * CZ) ** -0.5, 0.09375, ((2, 2), (3, 4), (4, 4)), jnp.float32),
        "coarse_factor": draw_coarse_factor(jax.random.fold_in(streams_of[6], 71), 0),
    }


def solve_layers(rounded, inverse_rows):
    padded = jnp.pad(rounded, ((0, 0), (0, 0), (2, 2), (2, 2), (0, 0)))
    x_index = (jnp.arange(N_GX, dtype=jnp.int32)[:, None] * CX + jnp.arange(CX + 4, dtype=jnp.int32)[None, :]).reshape(-1)
    y_index = (jnp.arange(N_GY, dtype=jnp.int32)[:, None] * CY + jnp.arange(CY + 4, dtype=jnp.int32)[None, :]).reshape(-1)
    extended = jnp.take(padded, x_index, axis=2)
    extended = jnp.take(extended, y_index, axis=3)
    extended = extended.reshape(S, C, N_GX, CX + 4, N_GY, CY + 4, NZ)

    def one_depth(depth_block):
        offset = (depth_block * CZ).astype(jnp.int32)
        inverse_part = lax.dynamic_slice_in_dim(inverse_rows, offset, CZ, 4).astype(jnp.float32)
        inverse_part = inverse_part.reshape(C, N_GX, CX, N_GY, CY, C, CX + 4, CY + 4, CZ)
        extended_part = lax.dynamic_slice_in_dim(extended, offset, CZ, 6).astype(jnp.float32)
        return jnp.einsum('caxbydefz,sdaebfz->scaxbyz', inverse_part, extended_part, precision=lax.Precision.HIGHEST)
    layers = lax.map(one_depth, jnp.arange(N_GZ, dtype=jnp.int32))
    layers = jnp.transpose(layers, (1, 2, 3, 4, 5, 6, 0, 7))
    return layers.reshape(S, C, NX, NY, NZ)

def reference(basis, inverse_rows, block_diag, couple, coarse_basis, coarse_factor):
    highest = lax.Precision.HIGHEST
    vector = basis[M - 1]
    rounded = vector.astype(jnp.bfloat16)
    local_part = solve_layers(rounded, inverse_rows)
    shaped_basis = coarse_basis.reshape(K, C, N_GX, CX, N_GY, CY, N_GZ, CZ)
    shaped_vector = vector.reshape(S, C, N_GX, CX, N_GY, CY, N_GZ, CZ)
    coarse_rhs = jnp.einsum('kcaxbygw,scaxbygw->abgks', shaped_basis, shaped_vector, precision=highest).reshape(NC, S)
    factor_image = jnp.dot(coarse_factor, coarse_rhs, precision=highest)
    coarse_coef = jnp.dot(coarse_factor.T, factor_image, precision=highest)
    shaped_coef = coarse_coef.reshape(N_GX, N_GY, N_GZ, K, S)
    correction = jnp.einsum('kcaxbygw,abgks->scaxbygw', shaped_basis, shaped_coef, precision=highest).reshape(S, C, NX, NY, NZ)
    preconditioned = local_part + correction
    padded = jnp.pad(preconditioned, ((0, 0), (0, 0), (1, 1), (1, 1), (1, 1)))
    applied = jnp.einsum('cdxyz,sdxyz->scxyz', block_diag, preconditioned, precision=highest)
    applied = applied - couple[0] * padded[:, :, :-2, 1:-1, 1:-1] - couple[1] * padded[:, :, 2:, 1:-1, 1:-1]
    applied = applied - couple[2] * padded[:, :, 1:-1, :-2, 1:-1] - couple[3] * padded[:, :, 1:-1, 2:, 1:-1]
    applied = applied - couple[4] * padded[:, :, 1:-1, 1:-1, :-2] - couple[5] * padded[:, :, 1:-1, 1:-1, 2:]
    unknowns = C * NX * NY * NZ
    projections = jnp.einsum('mscxyz,scxyz->sm', basis, applied, precision=highest) / unknowns
    remainder = applied - jnp.einsum('sm,mscxyz->scxyz', projections, basis, precision=highest)
    norm_scale = jnp.sqrt(lax.optimization_barrier(jnp.sum(remainder * remainder, axis=(1, 2, 3, 4))) / unknowns + 1e-06)
    krylov_next = remainder / norm_scale[:, None, None, None, None]
    hessenberg = jnp.concatenate([projections, norm_scale[:, None]], axis=1)
    return (krylov_next, preconditioned, hessenberg)
```

```python
import jax
import jax.numpy as jnp
from jax import lax
from jax.sharding import PartitionSpec as P

C = 4
CX = 4
CY = 2
CZ = 128
S = 4
M = 6
AXES = ("gx", "gy", "gz")

epsilon = 1e-06


def swap_rounds(axis, low_side, high_side):
    count = lax.axis_size(axis)
    odd = lax.axis_index(axis) % 2 == 1
    first = [(i, i + 1) for i in range(0, count - 1, 2)]
    second = [(i, i + 1) for i in range(1, count - 1, 2)]

    def both(pairs):
        return pairs + [(j, i) for i, j in pairs]

    got_first = lax.ppermute(jnp.where(odd, low_side, high_side), axis, both(first))
    if second:
        got_second = lax.ppermute(jnp.where(odd, high_side, low_side), axis, both(second))
    else:
        got_second = jnp.zeros_like(got_first)
    return jnp.where(odd, got_first, got_second), jnp.where(odd, got_second, got_first)


def padded_2(cells, sides, width):
    for axis, dim in sides:
        head = lax.slice_in_dim(cells, 0, width, axis=dim)
        tail = lax.slice_in_dim(cells, cells.shape[dim] - width, cells.shape[dim], axis=dim)
        below, above = swap_rounds(axis, head, tail)
        cells = jnp.concatenate([below, cells, above], axis=dim)
    return cells


def gathered(row, devices):
    sent = jnp.broadcast_to(row.reshape(1, 1, -1), (devices, 1, row.size))
    return lax.all_to_all(sent, AXES, 0, 0, tiled=True)


def total(row, devices):
    return jnp.sum(gathered(row, devices), axis=(0, 1))


def on_device(basis, inverse_rows, block_diag, couple, coarse_basis, coarse_factor):
    highest = lax.Precision.HIGHEST
    devices = lax.axis_size("gx") * lax.axis_size("gy") * lax.axis_size("gz")
    kinds = coarse_basis.shape[0]
    vector = basis[M - 1]
    rounded = vector.astype(jnp.bfloat16)
    extended = padded_2(rounded, (("gx", 2), ("gy", 3)), 2)
    columns = extended.reshape(S, C * (CX + 4) * (CY + 4), CZ)
    local_part = jnp.einsum(
        "cxyjz,sjz->scxyz", inverse_rows, columns, preferred_element_type=jnp.float32
    )
    coarse_rhs = jnp.einsum("kcxyz,scxyz->ks", coarse_basis, vector, precision=highest)
    all_rhs = gathered(coarse_rhs, devices).reshape(devices * kinds, S)
    factor_image = jnp.dot(coarse_factor, all_rhs, precision=highest)
    shares = jnp.dot(coarse_factor.T, factor_image, precision=highest)
    shares = lax.all_to_all(
        shares.reshape(devices, 1, kinds * S), AXES, 0, 0, tiled=True
    )
    coarse_coef = jnp.sum(shares, axis=(0, 1)).reshape(kinds, S)
    correction = jnp.einsum("kcxyz,ks->scxyz", coarse_basis, coarse_coef, precision=highest)
    preconditioned = local_part + correction
    p = preconditioned
    x_low, x_high = swap_rounds("gx", p[:, :, :1], p[:, :, -1:])
    y_low, y_high = swap_rounds("gy", p[:, :, :, :1], p[:, :, :, -1:])
    z_low, z_high = swap_rounds("gz", p[..., :1], p[..., -1:])
    px = jnp.concatenate([x_low, p, x_high], axis=2)
    py = jnp.concatenate([y_low, p, y_high], axis=3)
    pz = jnp.concatenate([z_low, p, z_high], axis=4)
    applied = sum(block_diag[:, d] * p[:, d : d + 1] for d in range(C))
    applied = applied - couple[0] * px[:, :, :-2] - couple[1] * px[:, :, 2:]
    applied = applied - couple[2] * py[:, :, :, :-2] - couple[3] * py[:, :, :, 2:]
    applied = applied - couple[4] * pz[..., :-2] - couple[5] * pz[..., 2:]
    unknowns = float(C * CX * CY * CZ * devices)
    local_products = jnp.einsum("mscxyz,scxyz->sm", basis, applied, precision=highest)
    projections = total(local_products, devices).reshape(S, M) / unknowns
    remainder = applied - jnp.einsum("sm,mscxyz->scxyz", projections, basis, precision=highest)
    squares = total(jnp.sum(remainder * remainder, axis=(1, 2, 3, 4)), devices)
    norm_scale = jnp.sqrt(squares / unknowns + epsilon)
    krylov_next = remainder / norm_scale[:, None, None, None, None]
    hessenberg = jnp.concatenate([projections, norm_scale[:, None]], axis=1)
    return (krylov_next, preconditioned, hessenberg)


def solution(mesh):
    return jax.shard_map(
        on_device,
        mesh=mesh,
        in_specs=(
            P(None, None, None, "gx", "gy", "gz"),
            P(None, "gx", "gy", None, "gz"),
            P(None, None, "gx", "gy", "gz"),
            P(None, None, "gx", "gy", "gz"),
            P(None, None, "gx", "gy", "gz"),
            P(AXES, None),
        ),
        out_specs=(P(None, None, "gx", "gy", "gz"), P(None, None, "gx", "gy", "gz"), P()),
        check_vma=False,
    )
```

```python
import functools

import jax
import jax.numpy as jnp
import numpy as np
from jax import lax
from jax.experimental import pallas as pl
from jax.experimental.pallas import tpu as pltpu
from jax.sharding import PartitionSpec as P

C = 4
CX = 4
CY = 2
CZ = 128
S = 4
M = 6
K = 16
XY = CX * CY
ROWS = C * (CX + 4) * (CY + 4)
AXES = ("gx", "gy", "gz")
PAIRS = [(m, n) for m in range(M) for n in range(m, M)]
BASE = 88
CANCEL = 1e-2

epsilon = 1e-06

VMEM = pl.BlockSpec(memory_space=pltpu.VMEM)
F32 = jnp.float32


def call(body, outs, operands, flops, scratch=()):
    size = sum(x.size * x.dtype.itemsize for x in list(operands) + list(outs))
    return pl.pallas_call(
        body,
        out_shape=tuple(outs),
        in_specs=[VMEM] * len(operands),
        out_specs=tuple([VMEM] * len(outs)),
        scratch_shapes=list(scratch),
        compiler_params=pltpu.CompilerParams(vmem_limit_bytes=24 * 1024 * 1024),
        cost_estimate=pl.CostEstimate(flops=flops, bytes_accessed=size, transcendentals=0),
    )(*operands)


def shape(*dims, dtype=F32):
    return jax.ShapeDtypeStruct(dims, dtype)


def iota(axis):
    return lax.broadcasted_iota(jnp.int32, (8, 128), axis)


def rolled(x, shift, axis):
    return pltpu.roll(x, shift % x.shape[axis], axis)


def row_sums(blocks):
    sub = iota(0)
    for bit in (4, 2, 1):
        low = (sub & bit) == 0
        half = len(blocks) // 2
        blocks = [
            jnp.where(
                low,
                blocks[i] + rolled(blocks[i], -bit, 0),
                blocks[i + half] + rolled(blocks[i + half], bit, 0),
            )
            for i in range(half)
        ]
    return blocks[0]


def across(left, right):
    return lax.dot_general(
        left,
        right,
        (((1,), (1,)), ((), ())),
        precision=lax.Precision.HIGHEST,
        preferred_element_type=F32,
    )


def all_rows(x, t):
    return jnp.broadcast_to(x[t : t + 1, :], (8, 128))


def splat(x, lane):
    return jnp.broadcast_to(x[:, lane : lane + 1], (8, 128))


def ends():
    sub, lane = iota(0), iota(1)
    pick = ((sub == 0) & (lane == 0)) | ((sub == 1) & (lane == CZ - 1))
    return jnp.where(pick, 1.0, 0.0).astype(F32)


def place():
    x, y, z = (lax.axis_index(a) for a in AXES)
    ny, nz = lax.axis_size("gy"), lax.axis_size("gz")
    return (x * ny + y) * nz + z, z > 0, z < nz - 1


def rhs_body(basis, phi, out):
    n = out.shape[0]
    rows = []
    for s in range(S):
        v = [basis[M - 1, s * C + c] for c in range(C)]
        prods = [sum(phi[k * C + c] * v[c] for c in range(C)) for k in range(K)]
        rows.append(row_sums(prods[:8]))
        rows.append(row_sums(prods[8:]))
    rows.append(jnp.zeros((64, 128), F32))
    rhs = across(jnp.ones((8, 128), F32), jnp.concatenate(rows, 0))
    faces = across(ends(), phi[...].reshape(K * C * XY, CZ))
    sub = iota(0)
    base = jnp.where(sub == 0, rhs, 0.0)
    out[...] = jnp.broadcast_to(base[None], (n, 8, 128))

    def with_face(side):
        block = base
        for r in range(4):
            block = jnp.where(sub == r + 1, all_rows(faces[:, 128 * r : 128 * r + 128], side), block)
        return block

    me, below, above = place()

    @pl.when(below)
    def _():
        out[me - 1] = with_face(0)

    @pl.when(above)
    def _():
        out[me + 1] = with_face(1)


def local_body(two_x, inv, cols, phi, basis, loc, locz, gram, *sends):
    def one(c, carry):
        total = [[jnp.zeros((8, 128), F32) for _ in range(XY)] for _ in range(S)]
        for j in range(0, ROWS, 16):
            seen = [cols[s, j : j + 16, :].astype(F32) for s in range(S)]
            for i in range(XY):
                w = inv[c, i, j : j + 16, :].astype(F32)
                for s in range(S):
                    part = w * seen[s]
                    total[s][i] = total[s][i] + part[:8] + part[8:]
        for s in range(S):
            loc[s * C + c] = row_sums(total[s])
        return carry

    lax.fori_loop(0, C, one, 0)
    locz[...] = across(ends(), loc[...].reshape(S * C * XY, CZ))

    rows = []
    for m, n in PAIRS:
        for s in range(S):
            rows.append(sum(basis[m, s * C + c] * basis[n, s * C + c] for c in range(C)))
    rows += [jnp.zeros((8, 128), F32)] * (BASE - len(rows))
    for g in range(0, BASE, 8):
        gram[g : g + 8, :] = row_sums(rows[g : g + 8])

    odd_y = lax.axis_index("gy") % 2 == 1
    odd_x = lax.axis_index("gx") % 2 == 1
    sub = iota(0)
    even = (sub & 1) == 0

    def block(half, of, i):
        share, own = K * C // of, S * C // of
        return phi[half * share + i] if i < share else loc[half * own + i - share]

    for i in range((K + S) * C // 2):
        a, b = block(0, 2, i), block(1, 2, i)
        low = jnp.where(even, a, rolled(b, 1, 0))
        high = jnp.where(even, rolled(a, -1, 0), b)
        sends[0][i] = jnp.where(odd_y, low, high)
        sends[1][i] = jnp.where(odd_y, high, low)
    for i in range((K + S) * C // 4):
        low = high = None
        for g in range(4):
            a = block(g, 4, i)
            to_low, to_high = rolled(a, 2 * g, 0), rolled(a, 2 * g - 6, 0)
            low = to_low if low is None else jnp.where((sub >> 1) == g, to_low, low)
            high = to_high if high is None else jnp.where((sub >> 1) == g, to_high, high)
        sends[2][i] = jnp.where(odd_x, low, high)
        if two_x:
            sends[3][i] = jnp.where(odd_x, high, low)


def periodic(x):
    for shift in (16, 32, 64):
        x = x + rolled(x, shift, 1)
    return x


def slots(two_x):
    return ["own", "ylo", "yhi"] + (["xlo", "xhi"] if two_x else ["x"]) + ["zlo", "zhi"]


def factor_body(two_x, got, locz, factor, out):
    n = factor.shape[1] // K
    stride = out.shape[0] // n
    sub, lane = iota(0), iota(1)
    diag = (lane >> 4) == sub
    image = [jnp.zeros((K, 128), F32) for _ in range(S)]
    for b in range(n // 8):
        rhs = got[pl.ds(64 * b, 8, stride=8), :]
        rows = factor[:, 128 * b : 128 * b + 128]
        for s in range(S):
            mine = jnp.where(diag, periodic(jnp.where((lane >> 4) == s, rhs, 0.0)), 0.0)
            image[s] = image[s] + rows * jnp.sum(mine, axis=0, keepdims=True)
    image = [jnp.sum(x, axis=1, keepdims=True) for x in image]
    shares = []
    for b in range(n // 8):
        rows = factor[:, 128 * b : 128 * b + 128]
        block = jnp.zeros((8, 128), F32)
        for s in range(S):
            part = jnp.sum(rows * image[s], axis=0, keepdims=True)
            mine = periodic(jnp.where(diag, part, 0.0))
            block = jnp.where((lane >> 4) == s, mine, block)
        shares.append(block)
    shares = jnp.concatenate(shares, 0)
    nz = lax.axis_size("gz")
    plane = lax.axis_size("gy") * nz
    shift = {"own": 0, "ylo": nz, "yhi": -nz, "x": plane, "xlo": plane, "xhi": -plane, "zlo": 1, "zhi": -1}
    names = slots(two_x)
    for t in range(0, len(names), 2):
        pair = [rolled(shares, shift[x], 0) if shift[x] else shares for x in names[t : t + 2]]
        row = pair[0] if len(pair) == 1 else pair[0] + rolled(pair[1], 64, 1)
        out[pl.ds(t // 2, n, stride=stride), :] = row
    face = (len(names) + 1) // 2
    for t in range(face, stride):
        out[pl.ds(t, n, stride=stride), :] = jnp.zeros((n, 128), F32)
    me, below, above = place()

    @pl.when(below)
    def _():
        out[pl.ds((me - 1) * stride + face, 1), :] = locz[0:1, :]

    @pl.when(above)
    def _():
        out[pl.ds((me + 1) * stride + face, 1), :] = locz[1:2, :]


def image_body(two_x, loc, phi, diagonal, couple, basis, gram, coarse, got, *rest):
    faces, (pre, image, sent) = rest[:-3], rest[-3:]
    n = sent.shape[0]
    stride = coarse.shape[0] // n
    sub, lane = iota(0), iota(1)
    even = (sub & 1) == 0
    total = coarse[0:8, :]
    for b in range(1, coarse.shape[0] // 8):
        total = total + coarse[8 * b : 8 * b + 8, :]
    if stride == 4:
        total = total + rolled(total, 4, 0)
    names = slots(two_x)

    def coefs(name):
        at = names.index(name)
        return rolled(all_rows(total, at // 2), -64 * (at % 2), 1)

    own = coefs("own")
    p = [loc[i] for i in range(S * C)]
    for s in range(S):
        for k in range(K):
            w = splat(own, s * K + k)
            for c in range(C):
                p[s * C + c] = p[s * C + c] + w * phi[k * C + c]

    odd_y = lax.axis_index("gy") % 2 == 1
    odd_x = lax.axis_index("gx") % 2 == 1

    def y_side(face, coef):
        sums = []
        for s in range(S):
            mine = even if s < 2 else ~even
            part = [jnp.where(mine, face[32 + (s % 2) * C + c], 0.0) for c in range(C)]
            for k in range(K // 2):
                w = jnp.where(even, splat(coef, s * K + k), splat(coef, s * K + k + K // 2))
                for c in range(C):
                    part[c] = part[c] + w * face[k * C + c]
            sums += part
        return sums

    def x_side(face, coef):
        sums = []
        for s in range(S):
            part = [jnp.where((sub >> 1) == s, face[16 + c], 0.0) for c in range(C)]
            for k in range(K // 4):
                w = splat(coef, s * K + k)
                for g in range(1, 4):
                    w = jnp.where((sub >> 1) == g, splat(coef, s * K + k + 4 * g), w)
                for c in range(C):
                    part[c] = part[c] + w * face[k * C + c]
            for x in part:
                x = x + rolled(x, 2, 0)
                sums.append(x + rolled(x, 4, 0))
        return sums

    ylo, yhi = coefs("ylo"), coefs("yhi")
    y_first = y_side(faces[0], jnp.where(odd_y, ylo, yhi))
    y_second = y_side(faces[1], jnp.where(odd_y, yhi, ylo))
    if two_x:
        xlo, xhi = coefs("xlo"), coefs("xhi")
        x_first = x_side(faces[2], jnp.where(odd_x, xlo, xhi))
        x_second = x_side(faces[3], jnp.where(odd_x, xhi, xlo))
    else:
        x_first = x_side(faces[2], coefs("x"))
        x_second = [jnp.zeros((8, 128), F32)] * (S * C)

    me, below, above = place()

    def z_side(there, neighbour, coef):
        at = jnp.where(there, neighbour, me)
        parts = got[pl.ds(pl.multiple_of(at * 8, 8), 8), :]
        parts = jnp.where((sub >= 1) & (sub <= 4), parts, 0.0)
        row = jnp.broadcast_to(coarse[pl.ds(at * stride + (len(names) + 1) // 2, 1), :], (8, 128))
        for s in range(S):
            w = jnp.zeros((8, 128), F32)
            for k in range(K):
                w = jnp.where((sub == 1 + k // 4) & ((lane >> 5) == k % 4), splat(coef, s * K + k), w)
            part = parts * w
            for shift in (4, 2, 1):
                part = part + rolled(part, shift, 0)
            for shift in (32, 64):
                part = part + rolled(part, shift, 1)
            row = row + jnp.where((lane >> 5) == s, part, 0.0)
        return jnp.where(there, row, 0.0)

    zlo = z_side(below, me - 1, coefs("zlo"))
    zhi = z_side(above, me + 1, coefs("zhi"))
    columns = jnp.transpose(jnp.where(sub == 0, zlo, zhi))

    for s in range(S):
        sides = []
        for c in range(C):
            i = s * C + c
            x = p[i]
            pre[i] = x
            zl = jnp.broadcast_to(columns[i * XY : (i + 1) * XY, 0:1], (8, 128))
            zh = jnp.broadcast_to(columns[i * XY : (i + 1) * XY, 1:2], (8, 128))
            y_low = jnp.where(odd_y, y_first[i], y_second[i])
            y_high = jnp.where(odd_y, y_second[i], y_first[i])
            x_low = jnp.where(odd_x, x_first[i], x_second[i])
            x_high = jnp.where(odd_x, x_second[i], x_first[i])
            y_low = y_low + rolled(y_low, -1, 0)
            y_high = y_high + rolled(y_high, 1, 0)
            sides = [
                jnp.where(sub < CY, x_low, rolled(x, CY, 0)),
                jnp.where(sub >= XY - CY, x_high, rolled(x, -CY, 0)),
                jnp.where(even, y_low, rolled(x, 1, 0)),
                jnp.where(even, rolled(x, -1, 0), y_high),
                jnp.where(lane == 0, zl, rolled(x, 1, 1)),
                jnp.where(lane == CZ - 1, zh, rolled(x, -1, 1)),
            ]
            a = sum(diagonal[c * C + d] * p[s * C + d] for d in range(C))
            for d, side in enumerate(sides):
                a = a - couple[d * C + c] * side
            image[i] = a

    rows = []
    for m in range(M):
        for s in range(S):
            rows.append(sum(basis[m, s * C + c] * image[s * C + c] for c in range(C)))
    for s in range(S):
        rows.append(sum(image[s * C + c] * image[s * C + c] for c in range(C)))
    rows += [jnp.zeros((8, 128), F32)] * 4
    sums = [row_sums(rows[g : g + 8]) for g in range(0, 32, 8)]
    sums = jnp.concatenate([gram[...]] + sums + [jnp.zeros((8, 128), F32)], 0)
    row = across(jnp.ones((8, 128), F32), sums)
    sent[...] = jnp.broadcast_to(row[None], (n // 8, 8, 128)).reshape(n, 128)


def tables():
    first = np.zeros((128, 128), np.float32)
    second = np.zeros((128, 128), np.float32)
    out = np.zeros((128, 128), np.float32)
    fixed = np.zeros((8, 128), np.float32)
    for s in range(S):
        for at, (m, n) in enumerate(PAIRS):
            first[BASE + 4 * m + s, 4 * at + s] = 1
            second[BASE + 4 * n + s, 4 * at + s] = 1
            fixed[2, 4 * at + s] = 1 if m == n else 2
        for m in range(M):
            lane = BASE + 4 * m + s
            first[lane, lane] = 1
            fixed[1, lane] = 1
            fixed[2, lane] = -2
        lane = BASE + 4 * M + s
        fixed[0, lane] = fixed[1, lane] = fixed[2, lane] = 1
        for i in range(M + 1):
            out[BASE + 4 * i + s, i] = 1
    return np.stack([first, second, out]), fixed


def finish_body(unknowns, got, image, basis, maps, fixed, krylov, hessenberg, flag):
    sub, lane = iota(0), iota(1)
    total = got[0:8, :]
    for b in range(1, got.shape[0] // 8):
        total = total + got[8 * b : 8 * b + 8, :]
    for shift in (4, 2, 1):
        total = total + rolled(total, shift, 0)
    h = total / unknowns

    def times(x, table):
        return jnp.dot(x, table, precision=lax.Precision.HIGHEST, preferred_element_type=F32)

    terms = total * all_rows(fixed, 2)
    terms = terms * (times(h, maps[0]) + all_rows(fixed, 0)) * (times(h, maps[1]) + all_rows(fixed, 1))
    size = jnp.abs(terms)
    for shift in (4, 8, 16, 32, 64):
        terms = terms + rolled(terms, shift, 1)
        size = size + rolled(size, shift, 1)
    norm = jnp.sqrt(jnp.maximum(terms, 0.0) / unknowns + epsilon)
    scale = 1.0 / norm
    flag[...] = jnp.where(terms < CANCEL * size, 1.0, 0.0)
    for s in range(S):
        w = [splat(h, BASE + 4 * m + s) for m in range(M)]
        f = splat(scale, s)
        for c in range(C):
            i = s * C + c
            krylov[i] = (image[i] - sum(w[m] * basis[m, i] for m in range(M))) * f
    values = jnp.where(lane >= BASE + 4 * M, norm, h)
    values = jnp.where((lane & 3) == sub, values, 0.0)
    hessenberg[...] = times(values, maps[2])[:S, : M + 1]


def pairs_of(axis):
    count = lax.axis_size(axis)
    rounds = [[(i, i + 1) for i in range(start, count - 1, 2)] for start in (0, 1)]
    return [r + [(j, i) for i, j in r] for r in rounds if r]


def swap_rounds(axis, low_side, high_side):
    odd = lax.axis_index(axis) % 2 == 1
    rounds = pairs_of(axis)
    got_first = lax.ppermute(jnp.where(odd, low_side, high_side), axis, rounds[0])
    if len(rounds) == 2:
        got_second = lax.ppermute(jnp.where(odd, high_side, low_side), axis, rounds[1])
    else:
        got_second = jnp.zeros_like(got_first)
    return jnp.where(odd, got_first, got_second), jnp.where(odd, got_second, got_first)


def exchange(rows, n):
    sent = rows.reshape(n, -1, 128)
    return lax.all_to_all(sent, AXES, 0, 0, tiled=True)


def on_device(basis, inverse_rows, block_diag, couple, coarse_basis, coarse_factor):
    n = lax.axis_size("gx") * lax.axis_size("gy") * lax.axis_size("gz")
    unknowns = float(C * XY * CZ * n)
    two_x = lax.axis_size("gx") > 2
    vectors = basis.reshape(M, S * C, XY, CZ)
    phi = coarse_basis.reshape(K * C, XY, CZ)

    rounded = basis[M - 1].astype(jnp.bfloat16)
    y_low, y_high = swap_rounds("gy", rounded, rounded)
    (rhs,) = call(rhs_body, [shape(n, 8, 128)], (vectors, phi), 2 * K * S * C * XY * CZ)
    got = exchange(rhs, n).reshape(n * 8, 128)

    extended = jnp.concatenate([y_low, rounded, y_high], axis=3)
    x_low, x_high = swap_rounds("gx", extended[:, :, :2], extended[:, :, -2:])
    extended = jnp.concatenate([x_low, extended, x_high], axis=2)
    columns = extended.reshape(S, ROWS, CZ)
    half, quarter = (K + S) * C // 2, (K + S) * C // 4
    sends = [shape(half, 8, 128)] * 2 + [shape(quarter, 8, 128)] * (2 if two_x else 1)
    loc, locz, gram, *sends = call(
        functools.partial(local_body, two_x),
        [shape(S * C, XY, CZ), shape(8, 128), shape(BASE, 128)] + sends,
        (inverse_rows.reshape(C, XY, ROWS, CZ), columns, phi, vectors),
        2 * S * C * XY * ROWS * CZ,
    )
    faces = [lax.ppermute(x, "gy", pairs) for x, pairs in zip(sends, pairs_of("gy"))]
    faces += [lax.ppermute(x, "gx", pairs) for x, pairs in zip(sends[2:], pairs_of("gx"))]

    stride = 8 if two_x else 4
    (shares,) = call(
        functools.partial(factor_body, two_x),
        [shape(n * stride, 128)],
        (got, locz, coarse_factor),
        4 * S * K * K * n,
    )
    coarse = exchange(shares, n).reshape(n * stride, 128)
    pre, image, sent = call(
        functools.partial(image_body, two_x),
        [shape(S * C, XY, CZ), shape(S * C, XY, CZ), shape(n, 128)],
        (
            loc,
            phi,
            block_diag.reshape(C * C, XY, CZ),
            couple.reshape(6 * C, XY, CZ),
            vectors,
            gram,
            coarse,
            got,
            *faces,
        ),
        2 * S * C * XY * CZ * 40,
    )
    products = exchange(sent, n).reshape(n, 128)
    maps, fixed = tables()
    krylov, hessenberg, flag = call(
        functools.partial(finish_body, unknowns),
        [shape(S * C, XY, CZ), shape(S, M + 1), shape(8, 128)],
        (products, image, vectors, jnp.asarray(maps), jnp.asarray(fixed)),
        2 * S * C * XY * CZ * 8,
    )

    def exact(image, vectors, krylov, hessenberg):
        h = hessenberg[:, :M]
        left = image.reshape(S, C, XY, CZ) - jnp.sum(
            h.T[:, :, None, None, None] * vectors.reshape(M, S, C, XY, CZ), axis=0
        )
        squares = jnp.zeros((1, 128), F32).at[0, :S].set(jnp.sum(left * left, axis=(1, 2, 3)))
        squares = jnp.sum(exchange(jnp.broadcast_to(squares, (n, 128)), n), axis=(0, 1))[:S]
        norm = jnp.sqrt(squares / unknowns + epsilon)
        return (
            (left / norm[:, None, None, None]).reshape(S * C, XY, CZ),
            jnp.concatenate([h, norm[:, None]], axis=1),
        )

    def as_is(image, vectors, krylov, hessenberg):
        return krylov, hessenberg

    krylov, hessenberg = lax.cond(
        jnp.max(flag) > 0.0, exact, as_is, image, vectors, krylov, hessenberg
    )
    cells = (S, C, CX, CY, CZ)
    return krylov.reshape(cells), pre.reshape(cells), hessenberg


def solution(mesh):
    return jax.shard_map(
        on_device,
        mesh=mesh,
        in_specs=(
            P(None, None, None, "gx", "gy", "gz"),
            P(None, "gx", "gy", None, "gz"),
            P(None, None, "gx", "gy", "gz"),
            P(None, None, "gx", "gy", "gz"),
            P(None, None, "gx", "gy", "gz"),
            P(AXES, None),
        ),
        out_specs=(P(None, None, "gx", "gy", "gz"), P(None, None, "gx", "gy", "gz"), P()),
        check_vma=False,
    )
```

```python
import functools

import jax
import jax.numpy as jnp
import numpy as np
from jax import lax
from jax.experimental import pallas as pl
from jax.experimental.pallas import tpu as pltpu
from jax.sharding import PartitionSpec as P

C = 4
CX = 4
CY = 2
CZ = 128
S = 4
M = 6
K = 16
XY = CX * CY
ROWS = C * (CX + 4) * (CY + 4)
AXES = ("gx", "gy", "gz")
PAIRS = [(m, n) for m in range(M) for n in range(m, M)]
BASE = 88
CANCEL = 1e-2

epsilon = 1e-06

VMEM = pl.BlockSpec(memory_space=pltpu.VMEM)
F32 = jnp.float32


def call(body, outs, operands, flops, in_specs=None, out_specs=None, scratch=()):
    size = sum(int(np.prod(x.shape)) * x.dtype.itemsize for x in list(operands) + list(outs))
    return pl.pallas_call(
        body,
        out_shape=tuple(outs),
        in_specs=in_specs or [VMEM] * len(operands),
        out_specs=tuple(out_specs or [VMEM] * len(outs)),
        scratch_shapes=list(scratch),
        compiler_params=pltpu.CompilerParams(vmem_limit_bytes=24 * 1024 * 1024),
        cost_estimate=pl.CostEstimate(flops=flops, bytes_accessed=size, transcendentals=0),
    )(*operands)


def shape(*dims, dtype=F32):
    return jax.ShapeDtypeStruct(dims, dtype)


def kept(*dims, dtype=F32):
    return pltpu.VMEM(dims, dtype)


def in_hbm(x):
    return pltpu.with_memory_space_constraint(x, pltpu.HBM)


def iota(axis):
    return lax.broadcasted_iota(jnp.int32, (8, 128), axis)


def rolled(x, shift, axis):
    return pltpu.roll(x, shift % x.shape[axis], axis)


def row_sums(blocks):
    sub = iota(0)
    for bit in (4, 2, 1):
        low = (sub & bit) == 0
        half = len(blocks) // 2
        blocks = [
            jnp.where(
                low,
                blocks[i] + rolled(blocks[i], -bit, 0),
                blocks[i + half] + rolled(blocks[i + half], bit, 0),
            )
            for i in range(half)
        ]
    return blocks[0]


def across(left, right):
    return lax.dot_general(
        left,
        right,
        (((1,), (1,)), ((), ())),
        precision=lax.Precision.HIGHEST,
        preferred_element_type=F32,
    )


def all_rows(x, t):
    return jnp.broadcast_to(x[t : t + 1, :], (8, 128))


def splat(x, lane):
    return jnp.broadcast_to(x[:, lane : lane + 1], (8, 128))


def ends():
    sub, lane = iota(0), iota(1)
    pick = ((sub == 0) & (lane == 0)) | ((sub == 1) & (lane == CZ - 1))
    return jnp.where(pick, 1.0, 0.0).astype(F32)


def both_sides(axis):
    at = lax.axis_index(axis)
    return at > 0, at < lax.axis_size(axis) - 1


def place():
    x, y, z = (lax.axis_index(a) for a in AXES)
    ny, nz = lax.axis_size("gy"), lax.axis_size("gz")
    return (x * ny + y) * nz + z, z > 0, z < nz - 1


def load_body(basis, phi, vector, rounded, phi_kept, sems):
    first = pltpu.make_async_copy(basis.at[M - 1], vector, sems.at[0])
    second = pltpu.make_async_copy(phi, phi_kept, sems.at[1])
    first.start()
    second.start()
    first.wait()
    rounded[...] = vector[...].astype(jnp.bfloat16)
    second.wait()


def rhs_body(vector, phi, out):
    n = out.shape[0]
    rows = []
    for s in range(S):
        v = [vector[s * C + c] for c in range(C)]
        prods = [sum(phi[k * C + c] * v[c] for c in range(C)) for k in range(K)]
        rows.append(row_sums(prods[:8]))
        rows.append(row_sums(prods[8:]))
    rows.append(jnp.zeros((64, 128), F32))
    rhs = across(jnp.ones((8, 128), F32), jnp.concatenate(rows, 0))
    faces = across(ends(), phi[...].reshape(K * C * XY, CZ))
    sub = iota(0)
    base = jnp.where(sub == 0, rhs, 0.0)
    out[...] = jnp.broadcast_to(base[None], (n, 8, 128))

    def with_face(side):
        block = base
        for r in range(4):
            block = jnp.where(sub == r + 1, all_rows(faces[:, 128 * r : 128 * r + 128], side), block)
        return block

    me, below, above = place()

    @pl.when(below)
    def _():
        out[me - 1] = with_face(0)

    @pl.when(above)
    def _():
        out[me + 1] = with_face(1)


def local_body(two_x, inv, cols, phi, basis, loc, locz, gram, *sends):
    def one(c, carry):
        total = [[jnp.zeros((8, 128), F32) for _ in range(XY)] for _ in range(S)]
        for j in range(0, ROWS, 16):
            seen = [cols[s, j : j + 16, :].astype(F32) for s in range(S)]
            for i in range(XY):
                w = inv[c, i, j : j + 16, :].astype(F32)
                for s in range(S):
                    part = w * seen[s]
                    total[s][i] = total[s][i] + part[:8] + part[8:]
        for s in range(S):
            loc[s * C + c] = row_sums(total[s])
        return carry

    lax.fori_loop(0, C, one, 0)
    locz[...] = across(ends(), loc[...].reshape(S * C * XY, CZ))

    rows = []
    for m, n in PAIRS:
        for s in range(S):
            rows.append(sum(basis[m, s * C + c] * basis[n, s * C + c] for c in range(C)))
    rows += [jnp.zeros((8, 128), F32)] * (BASE - len(rows))
    for g in range(0, BASE, 8):
        gram[g : g + 8, :] = row_sums(rows[g : g + 8])

    odd_y = lax.axis_index("gy") % 2 == 1
    odd_x = lax.axis_index("gx") % 2 == 1
    sub = iota(0)
    even = (sub & 1) == 0

    def block(half, of, i):
        share, own = K * C // of, S * C // of
        return phi[half * share + i] if i < share else loc[half * own + i - share]

    for i in range((K + S) * C // 2):
        a, b = block(0, 2, i), block(1, 2, i)
        low = jnp.where(even, a, rolled(b, 1, 0))
        high = jnp.where(even, rolled(a, -1, 0), b)
        sends[0][i] = jnp.where(odd_y, low, high)
        sends[1][i] = jnp.where(odd_y, high, low)
    for i in range((K + S) * C // 4):
        low = high = None
        for g in range(4):
            a = block(g, 4, i)
            to_low, to_high = rolled(a, 2 * g, 0), rolled(a, 2 * g - 6, 0)
            low = to_low if low is None else jnp.where((sub >> 1) == g, to_low, low)
            high = to_high if high is None else jnp.where((sub >> 1) == g, to_high, high)
        sends[2][i] = jnp.where(odd_x, low, high)
        if two_x:
            sends[3][i] = jnp.where(odd_x, high, low)


def periodic(x):
    for shift in (16, 32, 64):
        x = x + rolled(x, shift, 1)
    return x


def slots(two_x):
    return ["own", "ylo", "yhi"] + (["xlo", "xhi"] if two_x else ["x"]) + ["zlo", "zhi"]


def factor_body(two_x, got, locz, factor, out):
    n = factor.shape[1] // K
    stride = out.shape[0] // n
    sub, lane = iota(0), iota(1)
    diag = (lane >> 4) == sub
    image = [jnp.zeros((K, 128), F32) for _ in range(S)]
    for b in range(n // 8):
        rhs = got[pl.ds(64 * b, 8, stride=8), :]
        rows = factor[:, 128 * b : 128 * b + 128]
        for s in range(S):
            mine = jnp.where(diag, periodic(jnp.where((lane >> 4) == s, rhs, 0.0)), 0.0)
            image[s] = image[s] + rows * jnp.sum(mine, axis=0, keepdims=True)
    image = [jnp.sum(x, axis=1, keepdims=True) for x in image]
    shares = []
    for b in range(n // 8):
        rows = factor[:, 128 * b : 128 * b + 128]
        block = jnp.zeros((8, 128), F32)
        for s in range(S):
            part = jnp.sum(rows * image[s], axis=0, keepdims=True)
            mine = periodic(jnp.where(diag, part, 0.0))
            block = jnp.where((lane >> 4) == s, mine, block)
        shares.append(block)
    shares = jnp.concatenate(shares, 0)
    nz = lax.axis_size("gz")
    plane = lax.axis_size("gy") * nz
    shift = {"own": 0, "ylo": nz, "yhi": -nz, "x": plane, "xlo": plane, "xhi": -plane, "zlo": 1, "zhi": -1}
    names = slots(two_x)
    for t in range(0, len(names), 2):
        pair = [rolled(shares, shift[x], 0) if shift[x] else shares for x in names[t : t + 2]]
        row = pair[0] if len(pair) == 1 else pair[0] + rolled(pair[1], 64, 1)
        out[pl.ds(t // 2, n, stride=stride), :] = row
    face = (len(names) + 1) // 2
    for t in range(face, stride):
        out[pl.ds(t, n, stride=stride), :] = jnp.zeros((n, 128), F32)
    me, below, above = place()

    @pl.when(below)
    def _():
        out[pl.ds((me - 1) * stride + face, 1), :] = locz[0:1, :]

    @pl.when(above)
    def _():
        out[pl.ds((me + 1) * stride + face, 1), :] = locz[1:2, :]


def image_body(two_x, loc, phi, diagonal, couple, basis, gram, coarse, got, *rest):
    faces, (pre, image, sent) = rest[:-3], rest[-3:]
    n = sent.shape[0]
    stride = coarse.shape[0] // n
    sub, lane = iota(0), iota(1)
    even = (sub & 1) == 0
    total = coarse[0:8, :]
    for b in range(1, coarse.shape[0] // 8):
        total = total + coarse[8 * b : 8 * b + 8, :]
    if stride == 4:
        total = total + rolled(total, 4, 0)
    names = slots(two_x)

    def coefs(name):
        at = names.index(name)
        return rolled(all_rows(total, at // 2), -64 * (at % 2), 1)

    own = coefs("own")
    p = [loc[i] for i in range(S * C)]
    for s in range(S):
        for k in range(K):
            w = splat(own, s * K + k)
            for c in range(C):
                p[s * C + c] = p[s * C + c] + w * phi[k * C + c]

    odd_y = lax.axis_index("gy") % 2 == 1
    odd_x = lax.axis_index("gx") % 2 == 1

    has_y, has_x = both_sides("gy"), both_sides("gx")

    def y_side(face, coef):
        sums = []
        for s in range(S):
            mine = even if s < 2 else ~even
            part = [jnp.where(mine, face[32 + (s % 2) * C + c], 0.0) for c in range(C)]
            for k in range(K // 2):
                w = jnp.where(even, splat(coef, s * K + k), splat(coef, s * K + k + K // 2))
                for c in range(C):
                    part[c] = part[c] + w * face[k * C + c]
            sums += part
        return sums

    def x_side(face, coef):
        sums = []
        for s in range(S):
            part = [jnp.where((sub >> 1) == s, face[16 + c], 0.0) for c in range(C)]
            for k in range(K // 4):
                w = splat(coef, s * K + k)
                for g in range(1, 4):
                    w = jnp.where((sub >> 1) == g, splat(coef, s * K + k + 4 * g), w)
                for c in range(C):
                    part[c] = part[c] + w * face[k * C + c]
            for x in part:
                x = x + rolled(x, 2, 0)
                sums.append(x + rolled(x, 4, 0))
        return sums

    ylo, yhi = coefs("ylo"), coefs("yhi")
    y_first = y_side(faces[0], jnp.where(odd_y, ylo, yhi))
    y_second = y_side(faces[1], jnp.where(odd_y, yhi, ylo))
    if two_x:
        xlo, xhi = coefs("xlo"), coefs("xhi")
        x_first = x_side(faces[2], jnp.where(odd_x, xlo, xhi))
        x_second = x_side(faces[3], jnp.where(odd_x, xhi, xlo))
    else:
        x_first = x_side(faces[2], coefs("x"))
        x_second = x_first

    me, below, above = place()

    def z_side(there, neighbour, coef):
        at = jnp.where(there, neighbour, me)
        parts = got[pl.ds(pl.multiple_of(at * 8, 8), 8), :]
        parts = jnp.where((sub >= 1) & (sub <= 4), parts, 0.0)
        row = jnp.broadcast_to(coarse[pl.ds(at * stride + (len(names) + 1) // 2, 1), :], (8, 128))
        for s in range(S):
            w = jnp.zeros((8, 128), F32)
            for k in range(K):
                w = jnp.where((sub == 1 + k // 4) & ((lane >> 5) == k % 4), splat(coef, s * K + k), w)
            part = parts * w
            for shift in (4, 2, 1):
                part = part + rolled(part, shift, 0)
            for shift in (32, 64):
                part = part + rolled(part, shift, 1)
            row = row + jnp.where((lane >> 5) == s, part, 0.0)
        return jnp.where(there, row, 0.0)

    zlo = z_side(below, me - 1, coefs("zlo"))
    zhi = z_side(above, me + 1, coefs("zhi"))
    columns = jnp.transpose(jnp.where(sub == 0, zlo, zhi))

    for s in range(S):
        sides = []
        for c in range(C):
            i = s * C + c
            x = p[i]
            pre[i] = x
            zl = jnp.broadcast_to(columns[i * XY : (i + 1) * XY, 0:1], (8, 128))
            zh = jnp.broadcast_to(columns[i * XY : (i + 1) * XY, 1:2], (8, 128))
            y_low = jnp.where(odd_y, y_first[i], y_second[i])
            y_high = jnp.where(odd_y, y_second[i], y_first[i])
            x_low = jnp.where(odd_x, x_first[i], x_second[i])
            x_high = jnp.where(odd_x, x_second[i], x_first[i])
            y_low = jnp.where(has_y[0], y_low + rolled(y_low, -1, 0), 0.0)
            y_high = jnp.where(has_y[1], y_high + rolled(y_high, 1, 0), 0.0)
            x_low, x_high = jnp.where(has_x[0], x_low, 0.0), jnp.where(has_x[1], x_high, 0.0)
            sides = [
                jnp.where(sub < CY, x_low, rolled(x, CY, 0)),
                jnp.where(sub >= XY - CY, x_high, rolled(x, -CY, 0)),
                jnp.where(even, y_low, rolled(x, 1, 0)),
                jnp.where(even, rolled(x, -1, 0), y_high),
                jnp.where(lane == 0, zl, rolled(x, 1, 1)),
                jnp.where(lane == CZ - 1, zh, rolled(x, -1, 1)),
            ]
            a = sum(diagonal[c * C + d] * p[s * C + d] for d in range(C))
            for d, side in enumerate(sides):
                a = a - couple[d * C + c] * side
            image[i] = a

    rows = []
    for m in range(M):
        for s in range(S):
            rows.append(sum(basis[m, s * C + c] * image[s * C + c] for c in range(C)))
    for s in range(S):
        rows.append(sum(image[s * C + c] * image[s * C + c] for c in range(C)))
    rows += [jnp.zeros((8, 128), F32)] * 4
    sums = [row_sums(rows[g : g + 8]) for g in range(0, 32, 8)]
    sums = jnp.concatenate([gram[...]] + sums + [jnp.zeros((8, 128), F32)], 0)
    row = across(jnp.ones((8, 128), F32), sums)
    sent[...] = jnp.broadcast_to(row[None], (n // 8, 8, 128)).reshape(n, 128)


def tables():
    first = np.zeros((128, 128), np.float32)
    second = np.zeros((128, 128), np.float32)
    out = np.zeros((128, 128), np.float32)
    fixed = np.zeros((8, 128), np.float32)
    for s in range(S):
        for at, (m, n) in enumerate(PAIRS):
            first[BASE + 4 * m + s, 4 * at + s] = 1
            second[BASE + 4 * n + s, 4 * at + s] = 1
            fixed[2, 4 * at + s] = 1 if m == n else 2
        for m in range(M):
            lane = BASE + 4 * m + s
            first[lane, lane] = 1
            fixed[1, lane] = 1
            fixed[2, lane] = -2
        lane = BASE + 4 * M + s
        fixed[0, lane] = fixed[1, lane] = fixed[2, lane] = 1
        for i in range(M + 1):
            out[BASE + 4 * i + s, i] = 1
    return np.stack([first, second, out]), fixed


def finish_body(unknowns, got, image, basis, maps, fixed, krylov, hessenberg, flag):
    sub, lane = iota(0), iota(1)
    total = got[0:8, :]
    for b in range(1, got.shape[0] // 8):
        total = total + got[8 * b : 8 * b + 8, :]
    for shift in (4, 2, 1):
        total = total + rolled(total, shift, 0)
    h = total / unknowns

    def times(x, table):
        return jnp.dot(x, table, precision=lax.Precision.HIGHEST, preferred_element_type=F32)

    terms = total * all_rows(fixed, 2)
    terms = terms * (times(h, maps[0]) + all_rows(fixed, 0)) * (times(h, maps[1]) + all_rows(fixed, 1))
    size = jnp.abs(terms)
    for shift in (4, 8, 16, 32, 64):
        terms = terms + rolled(terms, shift, 1)
        size = size + rolled(size, shift, 1)
    norm = jnp.sqrt(jnp.maximum(terms, 0.0) / unknowns + epsilon)
    scale = 1.0 / norm
    flag[0] = jnp.max(jnp.where(terms < CANCEL * size, 1, 0))
    for s in range(S):
        w = [splat(h, BASE + 4 * m + s) for m in range(M)]
        f = splat(scale, s)
        for c in range(C):
            i = s * C + c
            krylov[i] = (image[i] - sum(w[m] * basis[m, i] for m in range(M))) * f
    values = jnp.where(lane >= BASE + 4 * M, norm, h)
    values = jnp.where((lane & 3) == sub, values, 0.0)
    hessenberg[...] = times(values, maps[2])[:S, : M + 1]


def pairs_of(axis):
    count = lax.axis_size(axis)
    rounds = [[(i, i + 1) for i in range(0, count, 2)]]
    if count > 2:
        rounds.append([(i, (i + 1) % count) for i in range(1, count, 2)])
    return [r + [(j, i) for i, j in r] for r in rounds]


def swap(axis, low_side, high_side):
    odd = lax.axis_index(axis) % 2 == 1
    rounds = pairs_of(axis)
    sides = [jnp.where(odd, low_side, high_side), jnp.where(odd, high_side, low_side)]
    return [lax.ppermute(x, axis, pairs) for x, pairs in zip(sides, rounds)]


def by_side(axis, got):
    at = lax.axis_index(axis)
    odd = at % 2 == 1
    first, second = got if len(got) == 2 else (got[0], got[0])
    low, high = jnp.where(odd, first, second), jnp.where(odd, second, first)
    none = jnp.zeros_like(first)
    return jnp.where(at > 0, low, none), jnp.where(at < lax.axis_size(axis) - 1, high, none)


def exchange(rows, n):
    sent = rows.reshape(n, -1, 128)
    return lax.all_to_all(sent, AXES, 0, 0, tiled=True)


def on_device(basis, inverse_rows, block_diag, couple, coarse_basis, coarse_factor):
    n = lax.axis_size("gx") * lax.axis_size("gy") * lax.axis_size("gz")
    unknowns = float(C * XY * CZ * n)
    two_x = lax.axis_size("gx") > 2
    vectors = basis.reshape(M, S * C, XY, CZ)
    phi = coarse_basis.reshape(K * C, XY, CZ)

    vector, rounded, phi = call(
        load_body,
        [kept(S * C, XY, CZ), kept(S * C, XY, CZ, dtype=jnp.bfloat16), kept(K * C, XY, CZ)],
        (in_hbm(vectors), in_hbm(phi)),
        S * C * XY * CZ,
        in_specs=[pl.BlockSpec(memory_space=pltpu.HBM)] * 2,
        scratch=[pltpu.SemaphoreType.DMA((2,))],
    )
    rounded = rounded.reshape(S, C, CX, CY, CZ)
    (rhs,) = call(rhs_body, [kept(n, 8, 128)], (vector, phi), 2 * K * S * C * XY * CZ)
    swapped, rhs = lax.optimization_barrier((swap("gy", rounded, rounded), rhs))
    y_low, y_high = by_side("gy", swapped)
    got = exchange(rhs, n).reshape(n * 8, 128)

    extended = jnp.concatenate([y_low, rounded, y_high], axis=3)
    x_low, x_high = by_side("gx", swap("gx", extended[:, :, :2], extended[:, :, -2:]))
    extended = jnp.concatenate([x_low, extended, x_high], axis=2)
    columns = extended.reshape(S, ROWS, CZ)
    half, quarter = (K + S) * C // 2, (K + S) * C // 4
    sends = [shape(half, 8, 128)] * 2 + [shape(quarter, 8, 128)] * (2 if two_x else 1)
    loc, locz, gram, *sends = call(
        functools.partial(local_body, two_x),
        [shape(S * C, XY, CZ), shape(8, 128), shape(BASE, 128)] + sends,
        (inverse_rows.reshape(C, XY, ROWS, CZ), columns, phi, vectors),
        2 * S * C * XY * ROWS * CZ,
    )
    x_faces = [lax.ppermute(x, "gx", pairs) for x, pairs in zip(sends[2:], pairs_of("gx"))]
    faces = [lax.ppermute(x, "gy", pairs) for x, pairs in zip(sends, pairs_of("gy"))]
    faces += x_faces

    stride = 8 if two_x else 4
    (shares,) = call(
        functools.partial(factor_body, two_x),
        [kept(n * stride, 128)],
        (got, locz, coarse_factor),
        4 * S * K * K * n,
    )
    coarse = exchange(shares, n).reshape(n * stride, 128)
    pre, image, sent = call(
        functools.partial(image_body, two_x),
        [shape(S * C, XY, CZ), kept(S * C, XY, CZ), kept(n, 128)],
        (
            loc,
            phi,
            block_diag.reshape(C * C, XY, CZ),
            couple.reshape(6 * C, XY, CZ),
            vectors,
            gram,
            coarse,
            got,
            *faces,
        ),
        2 * S * C * XY * CZ * 40,
    )
    products = exchange(sent, n).reshape(n, 128)
    maps, fixed = tables()
    krylov, hessenberg, flag = call(
        functools.partial(finish_body, unknowns),
        [shape(S * C, XY, CZ), shape(S, M + 1), pltpu.SMEM((1,), jnp.int32)],
        (products, image, vectors, jnp.asarray(maps), jnp.asarray(fixed)),
        2 * S * C * XY * CZ * 8,
        out_specs=[VMEM, VMEM, pl.BlockSpec(memory_space=pltpu.SMEM)],
    )

    def exact(image, vectors, krylov, hessenberg):
        h = hessenberg[:, :M]
        left = image.reshape(S, C, XY, CZ) - jnp.sum(
            h.T[:, :, None, None, None] * vectors.reshape(M, S, C, XY, CZ), axis=0
        )
        squares = jnp.zeros((1, 128), F32).at[0, :S].set(jnp.sum(left * left, axis=(1, 2, 3)))
        squares = jnp.sum(exchange(jnp.broadcast_to(squares, (n, 128)), n), axis=(0, 1))[:S]
        norm = jnp.sqrt(squares / unknowns + epsilon)
        return (
            (left / norm[:, None, None, None]).reshape(S * C, XY, CZ),
            jnp.concatenate([h, norm[:, None]], axis=1),
        )

    def as_is(image, vectors, krylov, hessenberg):
        return krylov, hessenberg

    krylov, hessenberg = lax.cond(
        flag[0] > 0, exact, as_is, image, vectors, krylov, hessenberg
    )
    cells = (S, C, CX, CY, CZ)
    return krylov.reshape(cells), pre.reshape(cells), hessenberg


def solution(mesh):
    return jax.shard_map(
        on_device,
        mesh=mesh,
        in_specs=(
            P(None, None, None, "gx", "gy", "gz"),
            P(None, "gx", "gy", None, "gz"),
            P(None, None, "gx", "gy", "gz"),
            P(None, None, "gx", "gy", "gz"),
            P(None, None, "gx", "gy", "gz"),
            P(AXES, None),
        ),
        out_specs=(P(None, None, "gx", "gy", "gz"), P(None, None, "gx", "gy", "gz"), P()),
        check_vma=False,
    )
```

```python
import functools

import jax
import jax.numpy as jnp
import numpy as np
from jax import lax
from jax.experimental import pallas as pl
from jax.experimental.pallas import tpu as pltpu
from jax.sharding import PartitionSpec as P

C = 4
CX = 4
CY = 2
CZ = 128
S = 4
M = 6
K = 16
XY = CX * CY
ROWS = C * (CX + 4) * (CY + 4)
AXES = ("gx", "gy", "gz")
PAIRS = [(m, n) for m in range(M) for n in range(m, M)]
BASE = 88
CANCEL = 1e-2

epsilon = 1e-06

VMEM = pl.BlockSpec(memory_space=pltpu.VMEM)
F32 = jnp.float32


def call(body, outs, operands, flops, in_specs=None, out_specs=None, scratch=()):
    size = sum(int(np.prod(x.shape)) * x.dtype.itemsize for x in list(operands) + list(outs))
    return pl.pallas_call(
        body,
        out_shape=tuple(outs),
        in_specs=in_specs or [VMEM] * len(operands),
        out_specs=tuple(out_specs or [VMEM] * len(outs)),
        scratch_shapes=list(scratch),
        compiler_params=pltpu.CompilerParams(vmem_limit_bytes=24 * 1024 * 1024),
        cost_estimate=pl.CostEstimate(flops=flops, bytes_accessed=size, transcendentals=0),
    )(*operands)


def shape(*dims, dtype=F32):
    return jax.ShapeDtypeStruct(dims, dtype)


def kept(*dims, dtype=F32):
    return pltpu.VMEM(dims, dtype)


def in_hbm(x):
    return pltpu.with_memory_space_constraint(x, pltpu.HBM)


def iota(axis):
    return lax.broadcasted_iota(jnp.int32, (8, 128), axis)


def rolled(x, shift, axis):
    return pltpu.roll(x, shift % x.shape[axis], axis)


def row_sums(blocks):
    sub = iota(0)
    for bit in (4, 2, 1):
        low = (sub & bit) == 0
        half = len(blocks) // 2
        blocks = [
            jnp.where(
                low,
                blocks[i] + rolled(blocks[i], -bit, 0),
                blocks[i + half] + rolled(blocks[i + half], bit, 0),
            )
            for i in range(half)
        ]
    return blocks[0]


def across(left, right):
    return lax.dot_general(
        left,
        right,
        (((1,), (1,)), ((), ())),
        precision=lax.Precision.HIGHEST,
        preferred_element_type=F32,
    )


def all_rows(x, t):
    return jnp.broadcast_to(x[t : t + 1, :], (8, 128))


def splat(x, lane):
    return jnp.broadcast_to(x[:, lane : lane + 1], (8, 128))


def ends():
    sub, lane = iota(0), iota(1)
    pick = ((sub == 0) & (lane == 0)) | ((sub == 1) & (lane == CZ - 1))
    return jnp.where(pick, 1.0, 0.0).astype(F32)


def both_sides(axis):
    at = lax.axis_index(axis)
    return at > 0, at < lax.axis_size(axis) - 1


def place():
    x, y, z = (lax.axis_index(a) for a in AXES)
    ny, nz = lax.axis_size("gy"), lax.axis_size("gz")
    return (x * ny + y) * nz + z, z > 0, z < nz - 1


def y_faces(first, second):
    even = (iota(0) & 1) == 0
    low = jnp.where(even, first, rolled(second, 1, 0))
    high = jnp.where(even, rolled(first, -1, 0), second)
    return low, high


def load_body(basis, phi, vector, rounded, phi_kept, to_first, to_second, sems):
    copies = [
        pltpu.make_async_copy(basis.at[M - 1], vector, sems.at[0]),
        pltpu.make_async_copy(phi, phi_kept, sems.at[1]),
    ]
    for copy in copies:
        copy.start()
    odd = lax.axis_index("gy") % 2 == 1
    copies[0].wait()
    low = vector[...].astype(jnp.bfloat16)
    rounded[...] = low
    to_first[: S * C] = low.astype(F32)
    to_second[: S * C] = low.astype(F32)
    copies[1].wait()
    half = K * C // 2
    for i in range(half):
        low, high = y_faces(phi_kept[i], phi_kept[half + i])
        to_first[S * C + i] = jnp.where(odd, low, high)
        to_second[S * C + i] = jnp.where(odd, high, low)


def rhs_body(vector, phi, out):
    n = out.shape[0]
    rows = []
    for s in range(S):
        v = [vector[s * C + c] for c in range(C)]
        prods = [sum(phi[k * C + c] * v[c] for c in range(C)) for k in range(K)]
        rows.append(row_sums(prods[:8]))
        rows.append(row_sums(prods[8:]))
    rows.append(jnp.zeros((64, 128), F32))
    rhs = across(jnp.ones((8, 128), F32), jnp.concatenate(rows, 0))
    faces = across(ends(), phi[...].reshape(K * C * XY, CZ))
    sub = iota(0)
    base = jnp.where(sub == 0, rhs, 0.0)
    out[...] = jnp.broadcast_to(base[None], (n, 8, 128))

    def with_face(side):
        block = base
        for r in range(4):
            block = jnp.where(sub == r + 1, all_rows(faces[:, 128 * r : 128 * r + 128], side), block)
        return block

    me, below, above = place()

    @pl.when(below)
    def _():
        out[me - 1] = with_face(0)

    @pl.when(above)
    def _():
        out[me + 1] = with_face(1)


def local_body(two_x, inv, cols, phi, basis, loc, locz, gram, *sends):
    def one(c, carry):
        total = [[jnp.zeros((8, 128), F32) for _ in range(XY)] for _ in range(S)]
        for j in range(0, ROWS, 16):
            seen = [cols[s, j : j + 16, :].astype(F32) for s in range(S)]
            for i in range(XY):
                w = inv[c, i, j : j + 16, :].astype(F32)
                for s in range(S):
                    part = w * seen[s]
                    total[s][i] = total[s][i] + part[:8] + part[8:]
        for s in range(S):
            loc[s * C + c] = row_sums(total[s])
        return carry

    lax.fori_loop(0, C, one, 0)
    locz[...] = across(ends(), loc[...].reshape(S * C * XY, CZ))

    rows = []
    for m, n in PAIRS:
        for s in range(S):
            rows.append(sum(basis[m, s * C + c] * basis[n, s * C + c] for c in range(C)))
    rows += [jnp.zeros((8, 128), F32)] * (BASE - len(rows))
    for g in range(0, BASE, 8):
        gram[g : g + 8, :] = row_sums(rows[g : g + 8])

    odd_y = lax.axis_index("gy") % 2 == 1
    odd_x = lax.axis_index("gx") % 2 == 1
    sub = iota(0)

    def block(half, of, i):
        share, own = K * C // of, S * C // of
        return phi[half * share + i] if i < share else loc[half * own + i - share]

    for i in range(S * C // 2):
        low, high = y_faces(loc[i], loc[S * C // 2 + i])
        sends[0][i] = jnp.where(odd_y, low, high)
        sends[1][i] = jnp.where(odd_y, high, low)
    for i in range((K + S) * C // 4):
        low = high = None
        for g in range(4):
            a = block(g, 4, i)
            to_low, to_high = rolled(a, 2 * g, 0), rolled(a, 2 * g - 6, 0)
            low = to_low if low is None else jnp.where((sub >> 1) == g, to_low, low)
            high = to_high if high is None else jnp.where((sub >> 1) == g, to_high, high)
        sends[2][i] = jnp.where(odd_x, low, high)
        if two_x:
            sends[3][i] = jnp.where(odd_x, high, low)


def periodic(x):
    for shift in (16, 32, 64):
        x = x + rolled(x, shift, 1)
    return x


def slots(two_x):
    return ["own", "ylo", "yhi"] + (["xlo", "xhi"] if two_x else ["x"]) + ["zlo", "zhi"]


def factor_body(two_x, got, locz, factor, out):
    n = factor.shape[1] // K
    stride = out.shape[0] // n
    sub, lane = iota(0), iota(1)
    diag = (lane >> 4) == sub
    image = [jnp.zeros((K, 128), F32) for _ in range(S)]
    for b in range(n // 8):
        rhs = got[pl.ds(64 * b, 8, stride=8), :]
        rows = factor[:, 128 * b : 128 * b + 128]
        for s in range(S):
            mine = jnp.where(diag, periodic(jnp.where((lane >> 4) == s, rhs, 0.0)), 0.0)
            image[s] = image[s] + rows * jnp.sum(mine, axis=0, keepdims=True)
    image = [jnp.sum(x, axis=1, keepdims=True) for x in image]
    shares = []
    for b in range(n // 8):
        rows = factor[:, 128 * b : 128 * b + 128]
        block = jnp.zeros((8, 128), F32)
        for s in range(S):
            part = jnp.sum(rows * image[s], axis=0, keepdims=True)
            mine = periodic(jnp.where(diag, part, 0.0))
            block = jnp.where((lane >> 4) == s, mine, block)
        shares.append(block)
    shares = jnp.concatenate(shares, 0)
    nz = lax.axis_size("gz")
    plane = lax.axis_size("gy") * nz
    shift = {"own": 0, "ylo": nz, "yhi": -nz, "x": plane, "xlo": plane, "xhi": -plane, "zlo": 1, "zhi": -1}
    names = slots(two_x)
    for t in range(0, len(names), 2):
        pair = [rolled(shares, shift[x], 0) if shift[x] else shares for x in names[t : t + 2]]
        row = pair[0] if len(pair) == 1 else pair[0] + rolled(pair[1], 64, 1)
        out[pl.ds(t // 2, n, stride=stride), :] = row
    face = (len(names) + 1) // 2
    for t in range(face, stride):
        out[pl.ds(t, n, stride=stride), :] = jnp.zeros((n, 128), F32)
    me, below, above = place()

    @pl.when(below)
    def _():
        out[pl.ds((me - 1) * stride + face, 1), :] = locz[0:1, :]

    @pl.when(above)
    def _():
        out[pl.ds((me + 1) * stride + face, 1), :] = locz[1:2, :]


def image_body(two_x, loc, phi, diagonal, couple, basis, gram, coarse, got, *rest):
    slabs, faces, (pre, image, sent) = rest[:2], rest[2:-3], rest[-3:]
    n = sent.shape[0]
    stride = coarse.shape[0] // n
    sub, lane = iota(0), iota(1)
    even = (sub & 1) == 0
    total = coarse[0:8, :]
    for b in range(1, coarse.shape[0] // 8):
        total = total + coarse[8 * b : 8 * b + 8, :]
    if stride == 4:
        total = total + rolled(total, 4, 0)
    names = slots(two_x)

    def coefs(name):
        at = names.index(name)
        return rolled(all_rows(total, at // 2), -64 * (at % 2), 1)

    own = coefs("own")
    p = [loc[i] for i in range(S * C)]
    for s in range(S):
        for k in range(K):
            w = splat(own, s * K + k)
            for c in range(C):
                p[s * C + c] = p[s * C + c] + w * phi[k * C + c]

    odd_y = lax.axis_index("gy") % 2 == 1
    odd_x = lax.axis_index("gx") % 2 == 1

    has_y, has_x = both_sides("gy"), both_sides("gx")

    def y_side(slab, face, coef):
        sums = []
        for s in range(S):
            mine = even if s < 2 else ~even
            part = [jnp.where(mine, face[(s % 2) * C + c], 0.0) for c in range(C)]
            for k in range(K // 2):
                w = jnp.where(even, splat(coef, s * K + k), splat(coef, s * K + k + K // 2))
                for c in range(C):
                    part[c] = part[c] + w * slab[S * C + k * C + c]
            sums += part
        return sums

    def x_side(face, coef):
        sums = []
        for s in range(S):
            part = [jnp.where((sub >> 1) == s, face[16 + c], 0.0) for c in range(C)]
            for k in range(K // 4):
                w = splat(coef, s * K + k)
                for g in range(1, 4):
                    w = jnp.where((sub >> 1) == g, splat(coef, s * K + k + 4 * g), w)
                for c in range(C):
                    part[c] = part[c] + w * face[k * C + c]
            for x in part:
                x = x + rolled(x, 2, 0)
                sums.append(x + rolled(x, 4, 0))
        return sums

    ylo, yhi = coefs("ylo"), coefs("yhi")
    y_first = y_side(slabs[0], faces[0], jnp.where(odd_y, ylo, yhi))
    y_second = y_side(slabs[1], faces[1], jnp.where(odd_y, yhi, ylo))
    if two_x:
        xlo, xhi = coefs("xlo"), coefs("xhi")
        x_first = x_side(faces[2], jnp.where(odd_x, xlo, xhi))
        x_second = x_side(faces[3], jnp.where(odd_x, xhi, xlo))
    else:
        x_first = x_side(faces[2], coefs("x"))
        x_second = x_first

    me, below, above = place()

    def z_side(there, neighbour, coef):
        at = jnp.where(there, neighbour, me)
        parts = got[pl.ds(pl.multiple_of(at * 8, 8), 8), :]
        parts = jnp.where((sub >= 1) & (sub <= 4), parts, 0.0)
        row = jnp.broadcast_to(coarse[pl.ds(at * stride + (len(names) + 1) // 2, 1), :], (8, 128))
        for s in range(S):
            w = jnp.zeros((8, 128), F32)
            for k in range(K):
                w = jnp.where((sub == 1 + k // 4) & ((lane >> 5) == k % 4), splat(coef, s * K + k), w)
            part = parts * w
            for shift in (4, 2, 1):
                part = part + rolled(part, shift, 0)
            for shift in (32, 64):
                part = part + rolled(part, shift, 1)
            row = row + jnp.where((lane >> 5) == s, part, 0.0)
        return jnp.where(there, row, 0.0)

    zlo = z_side(below, me - 1, coefs("zlo"))
    zhi = z_side(above, me + 1, coefs("zhi"))
    columns = jnp.transpose(jnp.where(sub == 0, zlo, zhi))

    for s in range(S):
        sides = []
        for c in range(C):
            i = s * C + c
            x = p[i]
            pre[i] = x
            zl = jnp.broadcast_to(columns[i * XY : (i + 1) * XY, 0:1], (8, 128))
            zh = jnp.broadcast_to(columns[i * XY : (i + 1) * XY, 1:2], (8, 128))
            y_low = jnp.where(odd_y, y_first[i], y_second[i])
            y_high = jnp.where(odd_y, y_second[i], y_first[i])
            x_low = jnp.where(odd_x, x_first[i], x_second[i])
            x_high = jnp.where(odd_x, x_second[i], x_first[i])
            y_low = jnp.where(has_y[0], y_low + rolled(y_low, -1, 0), 0.0)
            y_high = jnp.where(has_y[1], y_high + rolled(y_high, 1, 0), 0.0)
            x_low, x_high = jnp.where(has_x[0], x_low, 0.0), jnp.where(has_x[1], x_high, 0.0)
            sides = [
                jnp.where(sub < CY, x_low, rolled(x, CY, 0)),
                jnp.where(sub >= XY - CY, x_high, rolled(x, -CY, 0)),
                jnp.where(even, y_low, rolled(x, 1, 0)),
                jnp.where(even, rolled(x, -1, 0), y_high),
                jnp.where(lane == 0, zl, rolled(x, 1, 1)),
                jnp.where(lane == CZ - 1, zh, rolled(x, -1, 1)),
            ]
            a = sum(diagonal[c * C + d] * p[s * C + d] for d in range(C))
            for d, side in enumerate(sides):
                a = a - couple[d * C + c] * side
            image[i] = a

    rows = []
    for m in range(M):
        for s in range(S):
            rows.append(sum(basis[m, s * C + c] * image[s * C + c] for c in range(C)))
    for s in range(S):
        rows.append(sum(image[s * C + c] * image[s * C + c] for c in range(C)))
    rows += [jnp.zeros((8, 128), F32)] * 4
    sums = [row_sums(rows[g : g + 8]) for g in range(0, 32, 8)]
    sums = jnp.concatenate([gram[...]] + sums + [jnp.zeros((8, 128), F32)], 0)
    row = across(jnp.ones((8, 128), F32), sums)
    sent[...] = jnp.broadcast_to(row[None], (n // 8, 8, 128)).reshape(n, 128)


def tables():
    first = np.zeros((128, 128), np.float32)
    second = np.zeros((128, 128), np.float32)
    out = np.zeros((128, 128), np.float32)
    fixed = np.zeros((8, 128), np.float32)
    for s in range(S):
        for at, (m, n) in enumerate(PAIRS):
            first[BASE + 4 * m + s, 4 * at + s] = 1
            second[BASE + 4 * n + s, 4 * at + s] = 1
            fixed[2, 4 * at + s] = 1 if m == n else 2
        for m in range(M):
            lane = BASE + 4 * m + s
            first[lane, lane] = 1
            fixed[1, lane] = 1
            fixed[2, lane] = -2
        lane = BASE + 4 * M + s
        fixed[0, lane] = fixed[1, lane] = fixed[2, lane] = 1
        for i in range(M + 1):
            out[BASE + 4 * i + s, i] = 1
    return np.stack([first, second, out]), fixed


def finish_body(unknowns, got, image, basis, maps, fixed, krylov, hessenberg, flag):
    sub, lane = iota(0), iota(1)
    total = got[0:8, :]
    for b in range(1, got.shape[0] // 8):
        total = total + got[8 * b : 8 * b + 8, :]
    for shift in (4, 2, 1):
        total = total + rolled(total, shift, 0)
    h = total / unknowns

    def times(x, table):
        return jnp.dot(x, table, precision=lax.Precision.HIGHEST, preferred_element_type=F32)

    terms = total * all_rows(fixed, 2)
    terms = terms * (times(h, maps[0]) + all_rows(fixed, 0)) * (times(h, maps[1]) + all_rows(fixed, 1))
    size = jnp.abs(terms)
    for shift in (4, 8, 16, 32, 64):
        terms = terms + rolled(terms, shift, 1)
        size = size + rolled(size, shift, 1)
    norm = jnp.sqrt(jnp.maximum(terms, 0.0) / unknowns + epsilon)
    scale = 1.0 / norm
    flag[0] = jnp.max(jnp.where(terms < CANCEL * size, 1, 0))
    for s in range(S):
        w = [splat(h, BASE + 4 * m + s) for m in range(M)]
        f = splat(scale, s)
        for c in range(C):
            i = s * C + c
            krylov[i] = (image[i] - sum(w[m] * basis[m, i] for m in range(M))) * f
    values = jnp.where(lane >= BASE + 4 * M, norm, h)
    values = jnp.where((lane & 3) == sub, values, 0.0)
    hessenberg[...] = times(values, maps[2])[:S, : M + 1]


def pairs_of(axis):
    count = lax.axis_size(axis)
    rounds = [[(i, i + 1) for i in range(0, count, 2)]]
    if count > 2:
        rounds.append([(i, (i + 1) % count) for i in range(1, count, 2)])
    return [r + [(j, i) for i, j in r] for r in rounds]


def swap(axis, low_side, high_side):
    odd = lax.axis_index(axis) % 2 == 1
    rounds = pairs_of(axis)
    sides = [jnp.where(odd, low_side, high_side), jnp.where(odd, high_side, low_side)]
    return [lax.ppermute(x, axis, pairs) for x, pairs in zip(sides, rounds)]


def by_side(axis, got):
    at = lax.axis_index(axis)
    odd = at % 2 == 1
    first, second = got if len(got) == 2 else (got[0], got[0])
    low, high = jnp.where(odd, first, second), jnp.where(odd, second, first)
    none = jnp.zeros_like(first)
    return jnp.where(at > 0, low, none), jnp.where(at < lax.axis_size(axis) - 1, high, none)


def exchange(rows, n):
    sent = rows.reshape(n, -1, 128)
    return lax.all_to_all(sent, AXES, 0, 0, tiled=True)


def on_device(basis, inverse_rows, block_diag, couple, coarse_basis, coarse_factor):
    n = lax.axis_size("gx") * lax.axis_size("gy") * lax.axis_size("gz")
    unknowns = float(C * XY * CZ * n)
    two_x = lax.axis_size("gx") > 2
    vectors = basis.reshape(M, S * C, XY, CZ)
    phi = coarse_basis.reshape(K * C, XY, CZ)

    slab = S * C + K * C // 2
    vector, rounded, phi, *slabs = call(
        load_body,
        [
            kept(S * C, XY, CZ),
            kept(S * C, XY, CZ, dtype=jnp.bfloat16),
            kept(K * C, XY, CZ),
            kept(slab, XY, CZ),
            kept(slab, XY, CZ),
        ],
        (in_hbm(vectors), in_hbm(phi)),
        S * C * XY * CZ,
        in_specs=[pl.BlockSpec(memory_space=pltpu.HBM)] * 2,
        scratch=[pltpu.SemaphoreType.DMA((2,))],
    )
    rounded = rounded.reshape(S, C, CX, CY, CZ)
    (rhs,) = call(rhs_body, [kept(n, 8, 128)], (vector, phi), 2 * K * S * C * XY * CZ)
    got = exchange(rhs, n).reshape(n * 8, 128)
    swapped = [lax.ppermute(x, "gy", pairs) for x, pairs in zip(slabs, pairs_of("gy"))]

    always = lax.axis_index("gx") >= 0

    def extend(swapped, rounded):
        parts = [x[: S * C].reshape(S, C, CX, CY, CZ).astype(rounded.dtype) for x in swapped]
        y_low, y_high = by_side("gy", parts)
        extended = jnp.concatenate([y_low, rounded, y_high], axis=3)
        x_low, x_high = by_side("gx", swap("gx", extended[:, :, :2], extended[:, :, -2:]))
        extended = jnp.concatenate([x_low, extended, x_high], axis=2)
        return extended.reshape(S, ROWS, CZ)

    def unused(swapped, rounded):
        return jnp.zeros((S, ROWS, CZ), rounded.dtype)

    columns = lax.cond(always, extend, unused, swapped, rounded)
    half, quarter = S * C // 2, (K + S) * C // 4
    sends = [shape(half, 8, 128)] * 2 + [shape(quarter, 8, 128)] * (2 if two_x else 1)
    loc, locz, gram, *sends = call(
        functools.partial(local_body, two_x),
        [shape(S * C, XY, CZ), shape(8, 128), shape(BASE, 128)] + sends,
        (inverse_rows.reshape(C, XY, ROWS, CZ), columns, phi, vectors),
        20000 * S * C * XY * ROWS * CZ,
    )

    def trade(*sends):
        x_faces = [lax.ppermute(x, "gx", pairs) for x, pairs in zip(sends[2:], pairs_of("gx"))]
        return [lax.ppermute(x, "gy", pairs) for x, pairs in zip(sends, pairs_of("gy"))] + x_faces

    def untouched(*sends):
        return list(sends)

    stride = 8 if two_x else 4
    (shares,) = call(
        functools.partial(factor_body, two_x),
        [kept(n * stride, 128)],
        (got, locz, coarse_factor),
        4 * S * K * K * n,
    )
    coarse = exchange(shares, n).reshape(n * stride, 128)
    faces = lax.cond(always, trade, untouched, *sends)
    pre, image, sent = call(
        functools.partial(image_body, two_x),
        [shape(S * C, XY, CZ), kept(S * C, XY, CZ), kept(n, 128)],
        (
            loc,
            phi,
            block_diag.reshape(C * C, XY, CZ),
            couple.reshape(6 * C, XY, CZ),
            vectors,
            gram,
            coarse,
            got,
            *swapped,
            *faces,
        ),
        2 * S * C * XY * CZ * 40,
    )
    products = exchange(sent, n).reshape(n, 128)
    maps, fixed = tables()
    krylov, hessenberg, flag = call(
        functools.partial(finish_body, unknowns),
        [shape(S * C, XY, CZ), shape(S, M + 1), pltpu.SMEM((1,), jnp.int32)],
        (products, image, vectors, jnp.asarray(maps), jnp.asarray(fixed)),
        2 * S * C * XY * CZ * 8,
        out_specs=[VMEM, VMEM, pl.BlockSpec(memory_space=pltpu.SMEM)],
    )

    def exact(image, vectors, krylov, hessenberg):
        h = hessenberg[:, :M]
        left = image.reshape(S, C, XY, CZ) - jnp.sum(
            h.T[:, :, None, None, None] * vectors.reshape(M, S, C, XY, CZ), axis=0
        )
        squares = jnp.zeros((1, 128), F32).at[0, :S].set(jnp.sum(left * left, axis=(1, 2, 3)))
        squares = jnp.sum(exchange(jnp.broadcast_to(squares, (n, 128)), n), axis=(0, 1))[:S]
        norm = jnp.sqrt(squares / unknowns + epsilon)
        return (
            (left / norm[:, None, None, None]).reshape(S * C, XY, CZ),
            jnp.concatenate([h, norm[:, None]], axis=1),
        )

    def as_is(image, vectors, krylov, hessenberg):
        return krylov, hessenberg

    krylov, hessenberg = lax.cond(
        flag[0] > 0, exact, as_is, image, vectors, krylov, hessenberg
    )
    cells = (S, C, CX, CY, CZ)
    return krylov.reshape(cells), pre.reshape(cells), hessenberg


def solution(mesh):
    return jax.shard_map(
        on_device,
        mesh=mesh,
        in_specs=(
            P(None, None, None, "gx", "gy", "gz"),
            P(None, "gx", "gy", None, "gz"),
            P(None, None, "gx", "gy", "gz"),
            P(None, None, "gx", "gy", "gz"),
            P(None, None, "gx", "gy", "gz"),
            P(AXES, None),
        ),
        out_specs=(P(None, None, "gx", "gy", "gz"), P(None, None, "gx", "gy", "gz"), P()),
        check_vma=False,
    )
```

```python
import functools

import jax
import jax.numpy as jnp
import numpy as np
from jax import lax
from jax.experimental import pallas as pl
from jax.experimental.pallas import tpu as pltpu
from jax.sharding import PartitionSpec as P

C = 4
CX = 4
CY = 2
CZ = 128
S = 4
M = 6
K = 16
XY = CX * CY
GATHERED = 1 + K * C * XY // CZ
EXTENT = (CX + 4) * (CY + 4)
SIDE = EXTENT // 3
ROWS = C * EXTENT
AXES = ("gx", "gy", "gz")
PAIRS = [(m, n) for m in range(M) for n in range(m, M)]
BASE = 88
CANCEL = 1e-2

epsilon = 1e-06

VMEM = pl.BlockSpec(memory_space=pltpu.VMEM)
F32 = jnp.float32


def call(body, outs, operands, flops, in_specs=None, out_specs=None, scratch=()):
    size = sum(int(np.prod(x.shape)) * x.dtype.itemsize for x in list(operands) + list(outs))
    return pl.pallas_call(
        body,
        out_shape=tuple(outs),
        in_specs=in_specs or [VMEM] * len(operands),
        out_specs=tuple(out_specs or [VMEM] * len(outs)),
        scratch_shapes=list(scratch),
        compiler_params=pltpu.CompilerParams(vmem_limit_bytes=24 * 1024 * 1024),
        cost_estimate=pl.CostEstimate(flops=flops, bytes_accessed=size, transcendentals=0),
    )(*operands)


def shape(*dims, dtype=F32):
    return jax.ShapeDtypeStruct(dims, dtype)


def kept(*dims, dtype=F32):
    return pltpu.VMEM(dims, dtype)


def in_hbm(x):
    return pltpu.with_memory_space_constraint(x, pltpu.HBM)


def iota(axis):
    return lax.broadcasted_iota(jnp.int32, (8, 128), axis)


def rolled(x, shift, axis):
    return pltpu.roll(x, shift % x.shape[axis], axis)


def row_sums(blocks):
    sub = iota(0)
    for bit in (4, 2, 1):
        low = (sub & bit) == 0
        half = len(blocks) // 2
        blocks = [
            jnp.where(
                low,
                blocks[i] + rolled(blocks[i], -bit, 0),
                blocks[i + half] + rolled(blocks[i + half], bit, 0),
            )
            for i in range(half)
        ]
    return blocks[0]


def across(left, right):
    return lax.dot_general(
        left,
        right,
        (((1,), (1,)), ((), ())),
        precision=lax.Precision.HIGHEST,
        preferred_element_type=F32,
    )


def all_rows(x, t):
    return jnp.broadcast_to(x[t : t + 1, :], (8, 128))


def splat(x, lane):
    return jnp.broadcast_to(x[:, lane : lane + 1], (8, 128))


def ends():
    sub, lane = iota(0), iota(1)
    pick = ((sub == 0) & (lane == 0)) | ((sub == 1) & (lane == CZ - 1))
    return jnp.where(pick, 1.0, 0.0).astype(F32)


def both_sides(axis):
    at = lax.axis_index(axis)
    return at > 0, at < lax.axis_size(axis) - 1


def place():
    x, y, z = (lax.axis_index(a) for a in AXES)
    ny, nz = lax.axis_size("gy"), lax.axis_size("gz")
    return (x * ny + y) * nz + z, z > 0, z < nz - 1


def y_faces(first, second):
    even = (iota(0) & 1) == 0
    low = jnp.where(even, first, rolled(second, 1, 0))
    high = jnp.where(even, rolled(first, -1, 0), second)
    return low, high


def load_body(basis, phi, vector, rounded, phi_kept, to_first, to_second, sems):
    copies = [
        pltpu.make_async_copy(basis.at[M - 1], vector, sems.at[0]),
        pltpu.make_async_copy(phi, phi_kept, sems.at[1]),
    ]
    for copy in copies:
        copy.start()
    odd = lax.axis_index("gy") % 2 == 1
    copies[0].wait()
    low = vector[...].astype(jnp.bfloat16)
    rounded[...] = low
    to_first[: S * C] = low.astype(F32)
    to_second[: S * C] = low.astype(F32)
    copies[1].wait()
    half = K * C // 2
    for i in range(half):
        low, high = y_faces(phi_kept[i], phi_kept[half + i])
        to_first[S * C + i] = jnp.where(odd, low, high)
        to_second[S * C + i] = jnp.where(odd, high, low)


def rhs_body(vector, phi, out):
    rows = []
    for s in range(S):
        v = [vector[s * C + c] for c in range(C)]
        prods = [sum(phi[k * C + c] * v[c] for c in range(C)) for k in range(K)]
        rows.append(row_sums(prods[:8]))
        rows.append(row_sums(prods[8:]))
    rows.append(jnp.zeros((64, 128), F32))
    rhs = across(jnp.ones((8, 128), F32), jnp.concatenate(rows, 0))
    faces = across(ends(), phi[...].reshape(K * C * XY, CZ))
    n = out.shape[0] // GATHERED
    me, _, _ = place()
    later = lax.broadcasted_iota(jnp.int32, (n, 128), 0) > me
    out[pl.ds(0, n, stride=GATHERED), :] = jnp.broadcast_to(rhs[0:1], (n, 128))
    for r in range(GATHERED - 1):
        row = faces[:, 128 * r : 128 * r + 128]
        out[pl.ds(r + 1, n, stride=GATHERED), :] = jnp.where(later, row[1:2], row[0:1])


def x_faces(blocks, sends, at):
    odd = lax.axis_index("gx") % 2 == 1
    group = iota(0) >> 1
    count = len(blocks) // 4
    for i in range(count):
        low = high = None
        for g in range(4):
            x = blocks[g * count + i]
            to_low, to_high = rolled(x, 2 * g, 0), rolled(x, 2 * g - 6, 0)
            low = to_low if low is None else jnp.where(group == g, to_low, low)
            high = to_high if high is None else jnp.where(group == g, to_high, high)
        sends[0][at + i] = jnp.where(odd, low, high)
        if len(sends) > 1:
            sends[1][at + i] = jnp.where(odd, high, low)


def solve(inv, cols, starts, done):
    def one(c, carry):
        total = [[jnp.zeros((8, 128), F32) for _ in range(XY)] for _ in range(S)]
        for at, j in starts:
            seen = [cols[s, j : j + 16, :].astype(F32) for s in range(S)]
            for i in range(XY):
                w = inv[c, i, at : at + 16, :].astype(F32)
                for s in range(S):
                    part = w * seen[s]
                    total[s][i] = total[s][i] + part[:8] + part[8:]
        for s in range(S):
            done(s * C + c, row_sums(total[s]))
        return carry

    lax.fori_loop(0, C, one, 0)


def early_body(two_x, phi, basis, inv, cols, gram, loc, inv_kept, *refs):
    phi_faces, (sem,) = refs[: 1 + two_x], refs[1 + two_x :]
    copy = pltpu.make_async_copy(inv, inv_kept, sem)
    copy.start()
    rows = []
    for m, n in PAIRS:
        for s in range(S):
            rows.append(sum(basis[m, s * C + c] * basis[n, s * C + c] for c in range(C)))
    rows += [jnp.zeros((8, 128), F32)] * (BASE - len(rows))
    for g in range(0, BASE, 8):
        gram[g : g + 8, :] = row_sums(rows[g : g + 8])

    x_faces([phi[i] for i in range(K * C)], phi_faces, 0)

    def done(i, x):
        loc[i] = x

    copy.wait()
    solve(inv_kept, cols, [(EXTENT * c + SIDE, SIDE * c) for c in range(C)], done)


def local_body(two_x, inv, cols, early, *refs):
    phi_faces, (loc, locz, *sends) = refs[: 1 + two_x], refs[1 + two_x :]

    def done(i, x):
        loc[i] = early[i] + x

    starts = [(EXTENT * c, 2 * SIDE * c) for c in range(C)]
    starts += [(EXTENT * c + 2 * SIDE, 2 * SIDE * c + SIDE) for c in range(C)]
    solve(inv, cols, starts, done)
    locz[...] = across(ends(), loc[...].reshape(S * C * XY, CZ))
    odd_y = lax.axis_index("gy") % 2 == 1
    for i in range(S * C // 2):
        low, high = y_faces(loc[i], loc[S * C // 2 + i])
        sends[0][i] = jnp.where(odd_y, low, high)
        sends[1][i] = jnp.where(odd_y, high, low)
    x_faces([loc[i] for i in range(S * C)], sends[2:], 0)
    for x, known in zip(sends[2:], phi_faces):
        x[C:] = known[...]


def periodic(x):
    for shift in (16, 32, 64):
        x = x + rolled(x, shift, 1)
    return x


def slots(two_x):
    return ["own", "ylo", "yhi"] + (["xlo", "xhi"] if two_x else ["x"]) + ["zlo", "zhi"]


def factor_body(two_x, got, locz, factor, out):
    n = factor.shape[1] // K
    stride = out.shape[0] // n
    sub, lane = iota(0), iota(1)
    diag = (lane >> 4) == sub
    image = [jnp.zeros((K, 128), F32) for _ in range(S)]
    for b in range(n // 8):
        rhs = got[pl.ds(8 * GATHERED * b, 8, stride=GATHERED), :]
        rows = factor[:, 128 * b : 128 * b + 128]
        for s in range(S):
            mine = jnp.where(diag, periodic(jnp.where((lane >> 4) == s, rhs, 0.0)), 0.0)
            image[s] = image[s] + rows * jnp.sum(mine, axis=0, keepdims=True)
    image = [jnp.sum(x, axis=1, keepdims=True) for x in image]
    shares = []
    for b in range(n // 8):
        rows = factor[:, 128 * b : 128 * b + 128]
        block = jnp.zeros((8, 128), F32)
        for s in range(S):
            part = jnp.sum(rows * image[s], axis=0, keepdims=True)
            mine = periodic(jnp.where(diag, part, 0.0))
            block = jnp.where((lane >> 4) == s, mine, block)
        shares.append(block)
    shares = jnp.concatenate(shares, 0)
    nz = lax.axis_size("gz")
    plane = lax.axis_size("gy") * nz
    shift = {"own": 0, "ylo": nz, "yhi": -nz, "x": plane, "xlo": plane, "xhi": -plane, "zlo": 1, "zhi": -1}
    names = slots(two_x)
    for t in range(0, len(names), 2):
        pair = [rolled(shares, shift[x], 0) if shift[x] else shares for x in names[t : t + 2]]
        row = pair[0] if len(pair) == 1 else pair[0] + rolled(pair[1], 64, 1)
        out[pl.ds(t // 2, n, stride=stride), :] = row
    face = (len(names) + 1) // 2
    for t in range(face, stride):
        out[pl.ds(t, n, stride=stride), :] = jnp.zeros((n, 128), F32)
    me, below, above = place()

    @pl.when(below)
    def _():
        out[pl.ds((me - 1) * stride + face, 1), :] = locz[0:1, :]

    @pl.when(above)
    def _():
        out[pl.ds((me + 1) * stride + face, 1), :] = locz[1:2, :]


def image_body(two_x, loc, phi, diagonal, couple, basis, gram, coarse, got, *rest):
    slabs, faces, (pre, image, sent) = rest[:2], rest[2:-3], rest[-3:]
    n = sent.shape[0]
    stride = coarse.shape[0] // n
    sub, lane = iota(0), iota(1)
    even = (sub & 1) == 0
    if stride == 4:
        total = coarse[0:8, :]
        for b in range(1, coarse.shape[0] // 8):
            total = total + coarse[8 * b : 8 * b + 8, :]
        total = total + rolled(total, 4, 0)
        totals = [all_rows(total, t) for t in range(stride - 1)]
    else:
        totals = [
            jnp.broadcast_to(
                jnp.sum(coarse[pl.ds(t, n, stride=stride), :], axis=0, keepdims=True), (8, 128)
            )
            for t in range(stride - 1)
        ]
    names = slots(two_x)

    def coefs(name):
        at = names.index(name)
        return totals[at // 2] if at % 2 == 0 else rolled(totals[at // 2], 64, 1)

    me, below, above = place()

    def z_side(there, neighbour, coef):
        at = jnp.where(there, neighbour, me)
        parts = [
            jnp.broadcast_to(got[pl.ds(at * GATHERED + 1 + r, 1), :], (8, 128))
            for r in range(GATHERED - 1)
        ]
        row = jnp.broadcast_to(coarse[pl.ds(at * stride + stride - 1, 1), :], (8, 128))
        for s in range(S):
            part = None
            for r in range(GATHERED - 1):
                w = splat(coef, s * K + 4 * r)
                for k in range(1, 4):
                    w = jnp.where((lane >> 5) == k, splat(coef, s * K + 4 * r + k), w)
                part = parts[r] * w if part is None else part + parts[r] * w
            for shift in (32, 64):
                part = part + rolled(part, shift, 1)
            row = row + jnp.where((lane >> 5) == s, part, 0.0)
        return jnp.where(there, row, 0.0)

    zlo = z_side(below, me - 1, coefs("zlo"))
    zhi = z_side(above, me + 1, coefs("zhi"))
    columns = jnp.transpose(jnp.where(sub == 0, zlo, zhi))

    own = coefs("own")
    p = [loc[i] for i in range(S * C)]
    for s in range(S):
        for k in range(K):
            w = splat(own, s * K + k)
            for c in range(C):
                p[s * C + c] = p[s * C + c] + w * phi[k * C + c]

    odd_y = lax.axis_index("gy") % 2 == 1
    odd_x = lax.axis_index("gx") % 2 == 1

    has_y, has_x = both_sides("gy"), both_sides("gx")

    def y_side(slab, face, coef):
        sums = []
        for s in range(S):
            mine = even if s < 2 else ~even
            part = [jnp.where(mine, face[(s % 2) * C + c], 0.0) for c in range(C)]
            for k in range(K // 2):
                w = jnp.where(even, splat(coef, s * K + k), splat(coef, s * K + k + K // 2))
                for c in range(C):
                    part[c] = part[c] + w * slab[S * C + k * C + c]
            sums += part
        return sums

    def x_side(face, coef):
        sums = []
        for s in range(S):
            part = [jnp.where((sub >> 1) == s, face[c], 0.0) for c in range(C)]
            for k in range(K // 4):
                w = splat(coef, s * K + k)
                for g in range(1, 4):
                    w = jnp.where((sub >> 1) == g, splat(coef, s * K + k + 4 * g), w)
                for c in range(C):
                    part[c] = part[c] + w * face[C + k * C + c]
            for x in part:
                x = x + rolled(x, 2, 0)
                sums.append(x + rolled(x, 4, 0))
        return sums

    ylo, yhi = coefs("ylo"), coefs("yhi")
    y_first = y_side(slabs[0], faces[0], jnp.where(odd_y, ylo, yhi))
    y_second = y_side(slabs[1], faces[1], jnp.where(odd_y, yhi, ylo))
    if two_x:
        xlo, xhi = coefs("xlo"), coefs("xhi")
        x_first = x_side(faces[2], jnp.where(odd_x, xlo, xhi))
        x_second = x_side(faces[3], jnp.where(odd_x, xhi, xlo))
    else:
        x_first = x_side(faces[2], coefs("x"))
        x_second = x_first

    for s in range(S):
        sides = []
        for c in range(C):
            i = s * C + c
            x = p[i]
            pre[i] = x
            zl = jnp.broadcast_to(columns[i * XY : (i + 1) * XY, 0:1], (8, 128))
            zh = jnp.broadcast_to(columns[i * XY : (i + 1) * XY, 1:2], (8, 128))
            y_low = jnp.where(odd_y, y_first[i], y_second[i])
            y_high = jnp.where(odd_y, y_second[i], y_first[i])
            x_low = jnp.where(odd_x, x_first[i], x_second[i])
            x_high = jnp.where(odd_x, x_second[i], x_first[i])
            y_low = jnp.where(has_y[0], y_low + rolled(y_low, -1, 0), 0.0)
            y_high = jnp.where(has_y[1], y_high + rolled(y_high, 1, 0), 0.0)
            x_low, x_high = jnp.where(has_x[0], x_low, 0.0), jnp.where(has_x[1], x_high, 0.0)
            sides = [
                jnp.where(sub < CY, x_low, rolled(x, CY, 0)),
                jnp.where(sub >= XY - CY, x_high, rolled(x, -CY, 0)),
                jnp.where(even, y_low, rolled(x, 1, 0)),
                jnp.where(even, rolled(x, -1, 0), y_high),
                jnp.where(lane == 0, zl, rolled(x, 1, 1)),
                jnp.where(lane == CZ - 1, zh, rolled(x, -1, 1)),
            ]
            a = sum(diagonal[c * C + d] * p[s * C + d] for d in range(C))
            for d, side in enumerate(sides):
                a = a - couple[d * C + c] * side
            image[i] = a

    rows = []
    for m in range(M):
        for s in range(S):
            rows.append(sum(basis[m, s * C + c] * image[s * C + c] for c in range(C)))
    for s in range(S):
        rows.append(sum(image[s * C + c] * image[s * C + c] for c in range(C)))
    rows += [jnp.zeros((8, 128), F32)] * 4
    sums = [row_sums(rows[g : g + 8]) for g in range(0, 32, 8)]
    sums = jnp.concatenate([gram[...]] + sums + [jnp.zeros((8, 128), F32)], 0)
    row = across(jnp.ones((8, 128), F32), sums)
    sent[...] = jnp.broadcast_to(row[None], (n // 8, 8, 128)).reshape(n, 128)


def tables():
    first = np.zeros((128, 128), np.float32)
    second = np.zeros((128, 128), np.float32)
    out = np.zeros((128, 128), np.float32)
    fixed = np.zeros((8, 128), np.float32)
    for s in range(S):
        for at, (m, n) in enumerate(PAIRS):
            first[BASE + 4 * m + s, 4 * at + s] = 1
            second[BASE + 4 * n + s, 4 * at + s] = 1
            fixed[2, 4 * at + s] = 1 if m == n else 2
        for m in range(M):
            lane = BASE + 4 * m + s
            first[lane, lane] = 1
            fixed[1, lane] = 1
            fixed[2, lane] = -2
        lane = BASE + 4 * M + s
        fixed[0, lane] = fixed[1, lane] = fixed[2, lane] = 1
        for i in range(M + 1):
            out[BASE + 4 * i + s, i] = 1
    return np.stack([first, second, out]), fixed


def finish_body(unknowns, got, image, basis, maps, fixed, krylov, hessenberg, flag):
    sub, lane = iota(0), iota(1)
    total = got[0:8, :]
    for b in range(1, got.shape[0] // 8):
        total = total + got[8 * b : 8 * b + 8, :]
    for shift in (4, 2, 1):
        total = total + rolled(total, shift, 0)
    h = total / unknowns

    def times(x, table):
        return jnp.dot(x, table, precision=lax.Precision.HIGHEST, preferred_element_type=F32)

    terms = total * all_rows(fixed, 2)
    terms = terms * (times(h, maps[0]) + all_rows(fixed, 0)) * (times(h, maps[1]) + all_rows(fixed, 1))
    size = jnp.abs(terms)
    for shift in (4, 8, 16, 32, 64):
        terms = terms + rolled(terms, shift, 1)
        size = size + rolled(size, shift, 1)
    norm = jnp.sqrt(jnp.maximum(terms, 0.0) / unknowns + epsilon)
    scale = 1.0 / norm
    flag[0] = jnp.max(jnp.where(terms < CANCEL * size, 1, 0))
    for s in range(S):
        w = [splat(h, BASE + 4 * m + s) for m in range(M)]
        f = splat(scale, s)
        for c in range(C):
            i = s * C + c
            krylov[i] = (image[i] - sum(w[m] * basis[m, i] for m in range(M))) * f
    values = jnp.where(lane >= BASE + 4 * M, norm, h)
    values = jnp.where((lane & 3) == sub, values, 0.0)
    hessenberg[...] = times(values, maps[2])[:S, : M + 1]


def pairs_of(axis):
    count = lax.axis_size(axis)
    rounds = [[(i, i + 1) for i in range(0, count, 2)]]
    if count > 2:
        rounds.append([(i, (i + 1) % count) for i in range(1, count, 2)])
    return [r + [(j, i) for i, j in r] for r in rounds]


def swap(axis, low_side, high_side):
    odd = lax.axis_index(axis) % 2 == 1
    rounds = pairs_of(axis)
    sides = [jnp.where(odd, low_side, high_side), jnp.where(odd, high_side, low_side)]
    return [lax.ppermute(x, axis, pairs) for x, pairs in zip(sides, rounds)]


def by_side(axis, got):
    at = lax.axis_index(axis)
    odd = at % 2 == 1
    first, second = got if len(got) == 2 else (got[0], got[0])
    low, high = jnp.where(odd, first, second), jnp.where(odd, second, first)
    none = jnp.zeros_like(first)
    return jnp.where(at > 0, low, none), jnp.where(at < lax.axis_size(axis) - 1, high, none)


def exchange(rows):
    return lax.all_to_all(rows[:, None], AXES, 0, 0, tiled=True).reshape(rows.shape)


def on_device(basis, inverse_rows, block_diag, couple, coarse_basis, coarse_factor):
    n = lax.axis_size("gx") * lax.axis_size("gy") * lax.axis_size("gz")
    unknowns = float(C * XY * CZ * n)
    two_x = lax.axis_size("gx") > 2
    vectors = basis.reshape(M, S * C, XY, CZ)
    phi = coarse_basis.reshape(K * C, XY, CZ)

    slab = S * C + K * C // 2
    vector, rounded, phi, *slabs = call(
        load_body,
        [
            kept(S * C, XY, CZ),
            kept(S * C, XY, CZ, dtype=jnp.bfloat16),
            kept(K * C, XY, CZ),
            kept(slab, XY, CZ),
            kept(slab, XY, CZ),
        ],
        (in_hbm(vectors), in_hbm(phi)),
        S * C * XY * CZ,
        in_specs=[pl.BlockSpec(memory_space=pltpu.HBM)] * 2,
        scratch=[pltpu.SemaphoreType.DMA((2,))],
    )
    rounded = rounded.reshape(S, C, CX, CY, CZ)
    (rhs,) = call(rhs_body, [kept(n * GATHERED, 128)], (vector, phi), 2 * K * S * C * XY * CZ)
    got = exchange(rhs)
    swapped = [lax.ppermute(x, "gy", pairs) for x, pairs in zip(slabs, pairs_of("gy"))]

    always = lax.axis_index("gx") >= 0

    inverse = inverse_rows.reshape(C, XY, ROWS, CZ)

    def extend(swapped, rounded, phi, vectors, inverse):
        parts = [x[: S * C].reshape(S, C, CX, CY, CZ).astype(rounded.dtype) for x in swapped]
        y_low, y_high = by_side("gy", parts)
        extended = jnp.concatenate([y_low, rounded, y_high], axis=3)
        x_low, x_high = by_side("gx", swap("gx", extended[:, :, :2], extended[:, :, -2:]))
        mine = extended.reshape(S, C, CX * (CY + 4), CZ)
        edge = (EXTENT - CX * (CY + 4)) // 2
        middle = mine[:, :, SIDE - edge : 2 * SIDE - edge].reshape(S, C * SIDE, CZ)
        early = call(
            functools.partial(early_body, two_x),
            [kept(BASE, 128), kept(S * C, XY, CZ), kept(*inverse.shape, dtype=inverse.dtype)]
            + [kept(K * C // 4, 8, 128)] * (1 + two_x),
            (phi, vectors, in_hbm(inverse), middle),
            10**10,
            in_specs=[VMEM, VMEM, pl.BlockSpec(memory_space=pltpu.HBM), VMEM],
            scratch=[pltpu.SemaphoreType.DMA],
        )
        outer = jnp.concatenate(
            [
                x_low.reshape(S, C, edge, CZ),
                mine[:, :, : SIDE - edge],
                mine[:, :, 2 * SIDE - edge :],
                x_high.reshape(S, C, edge, CZ),
            ],
            axis=2,
        )
        return [outer.reshape(S, C * 2 * SIDE, CZ)] + list(early)

    def unused(swapped, rounded, phi, vectors, inverse):
        return [
            jnp.zeros((S, C * 2 * SIDE, CZ), rounded.dtype),
            jnp.zeros((BASE, 128), F32),
            jnp.zeros((S * C, XY, CZ), F32),
            jnp.zeros_like(inverse),
        ] + [jnp.zeros((K * C // 4, 8, 128), F32)] * (1 + two_x)

    columns, gram, part, inverse, *phi_faces = lax.cond(
        always, extend, unused, swapped, rounded, phi, vectors, inverse
    )
    half, quarter = S * C // 2, (K + S) * C // 4
    sends = [shape(half, 8, 128)] * 2 + [shape(quarter, 8, 128)] * (2 if two_x else 1)
    loc, locz, *sends = call(
        functools.partial(local_body, two_x),
        [shape(S * C, XY, CZ), shape(8, 128)] + sends,
        (inverse, columns, part, *phi_faces),
        20000 * S * C * XY * ROWS * CZ,
    )

    def trade(*sends):
        x_faces = [lax.ppermute(x, "gx", pairs) for x, pairs in zip(sends[2:], pairs_of("gx"))]
        return [lax.ppermute(x, "gy", pairs) for x, pairs in zip(sends, pairs_of("gy"))] + x_faces

    def untouched(*sends):
        return list(sends)

    stride = (len(slots(two_x)) + 1) // 2 + 1
    (shares,) = call(
        functools.partial(factor_body, two_x),
        [kept(n * stride, 128)],
        (got, locz, coarse_factor),
        4 * S * K * K * n,
    )
    coarse = exchange(shares)
    faces = lax.cond(always, trade, untouched, *sends)
    pre, image, sent = call(
        functools.partial(image_body, two_x),
        [kept(S * C, XY, CZ), kept(S * C, XY, CZ), kept(n, 128)],
        (
            loc,
            phi,
            block_diag.reshape(C * C, XY, CZ),
            couple.reshape(6 * C, XY, CZ),
            vectors,
            gram,
            coarse,
            got,
            *swapped,
            *faces,
        ),
        2 * S * C * XY * CZ * 40,
    )
    products = exchange(sent)
    maps, fixed = tables()
    krylov, hessenberg, flag = call(
        functools.partial(finish_body, unknowns),
        [shape(S * C, XY, CZ), shape(S, M + 1), pltpu.SMEM((1,), jnp.int32)],
        (products, image, vectors, jnp.asarray(maps), jnp.asarray(fixed)),
        2 * S * C * XY * CZ * 8,
        out_specs=[VMEM, VMEM, pl.BlockSpec(memory_space=pltpu.SMEM)],
    )

    def exact(image, vectors, krylov, hessenberg):
        h = hessenberg[:, :M]
        left = image.reshape(S, C, XY, CZ) - jnp.sum(
            h.T[:, :, None, None, None] * vectors.reshape(M, S, C, XY, CZ), axis=0
        )
        squares = jnp.zeros((1, 128), F32).at[0, :S].set(jnp.sum(left * left, axis=(1, 2, 3)))
        squares = jnp.sum(exchange(jnp.broadcast_to(squares, (n, 128))), axis=0)[:S]
        norm = jnp.sqrt(squares / unknowns + epsilon)
        return (
            (left / norm[:, None, None, None]).reshape(S * C, XY, CZ),
            jnp.concatenate([h, norm[:, None]], axis=1),
        )

    def as_is(image, vectors, krylov, hessenberg):
        return krylov, hessenberg

    krylov, hessenberg = lax.cond(
        flag[0] > 0, exact, as_is, image, vectors, krylov, hessenberg
    )
    krylov, pre = lax.optimization_barrier((krylov, pre))
    cells = (S, C, CX, CY, CZ)
    return krylov.reshape(cells), pre.reshape(cells), hessenberg


def solution(mesh):
    return jax.shard_map(
        on_device,
        mesh=mesh,
        in_specs=(
            P(None, None, None, "gx", "gy", "gz"),
            P(None, "gx", "gy", None, "gz"),
            P(None, None, "gx", "gy", "gz"),
            P(None, None, "gx", "gy", "gz"),
            P(None, None, "gx", "gy", "gz"),
            P(AXES, None),
        ),
        out_specs=(P(None, None, "gx", "gy", "gz"), P(None, None, "gx", "gy", "gz"), P()),
        check_vma=False,
    )
```

```python
import functools

import jax
import jax.numpy as jnp
import numpy as np
from jax import lax
from jax.experimental import pallas as pl
from jax.experimental.pallas import tpu as pltpu
from jax.sharding import PartitionSpec as P

C = 4
CX = 4
CY = 2
CZ = 128
S = 4
M = 6
K = 16
XY = CX * CY
GATHERED = 1 + K * C * XY // CZ
EXTENT = (CX + 4) * (CY + 4)
SIDE = EXTENT // 3
ROWS = C * EXTENT
AXES = ("gx", "gy", "gz")
PAIRS = [(m, n) for m in range(M) for n in range(m, M)]
BASE = 88
CANCEL = 1e-2

epsilon = 1e-06

VMEM = pl.BlockSpec(memory_space=pltpu.VMEM)
F32 = jnp.float32


def call(body, outs, operands, flops, in_specs=None, out_specs=None, scratch=()):
    size = sum(int(np.prod(x.shape)) * x.dtype.itemsize for x in list(operands) + list(outs))
    return pl.pallas_call(
        body,
        out_shape=tuple(outs),
        in_specs=in_specs or [VMEM] * len(operands),
        out_specs=tuple(out_specs or [VMEM] * len(outs)),
        scratch_shapes=list(scratch),
        compiler_params=pltpu.CompilerParams(vmem_limit_bytes=24 * 1024 * 1024),
        cost_estimate=pl.CostEstimate(flops=flops, bytes_accessed=size, transcendentals=0),
    )(*operands)


def shape(*dims, dtype=F32):
    return jax.ShapeDtypeStruct(dims, dtype)


def kept(*dims, dtype=F32):
    return pltpu.VMEM(dims, dtype)


def in_hbm(x):
    return pltpu.with_memory_space_constraint(x, pltpu.HBM)


def iota(axis):
    return lax.broadcasted_iota(jnp.int32, (8, 128), axis)


def rolled(x, shift, axis):
    return pltpu.roll(x, shift % x.shape[axis], axis)


def row_sums(blocks):
    sub = iota(0)
    for bit in (4, 2, 1):
        low = (sub & bit) == 0
        half = len(blocks) // 2
        blocks = [
            jnp.where(
                low,
                blocks[i] + rolled(blocks[i], -bit, 0),
                blocks[i + half] + rolled(blocks[i + half], bit, 0),
            )
            for i in range(half)
        ]
    return blocks[0]


def thirds(x):
    parts = []
    for _ in range(3):
        parts.append(x.astype(jnp.bfloat16))
        x = x - parts[-1].astype(F32)
    return parts


def across(left, right):
    left = left.astype(jnp.bfloat16)
    return sum(
        lax.dot_general(left, part, (((1,), (1,)), ((), ())), preferred_element_type=F32)
        for part in thirds(right)
    )


def times(x, table):
    rows = jnp.concatenate([p.astype(F32) for p in thirds(x)] + [jnp.zeros((8, 128), F32)], 0)
    y = jnp.dot(rows.astype(jnp.bfloat16), table, preferred_element_type=F32)
    return y[:8] + y[8:16] + y[16:24]


def all_rows(x, t):
    return jnp.broadcast_to(x[t : t + 1, :], (8, 128))


def splat(x, lane):
    return jnp.broadcast_to(x[:, lane : lane + 1], (8, 128))


def ends():
    sub, lane = iota(0), iota(1)
    pick = ((sub == 0) & (lane == 0)) | ((sub == 1) & (lane == CZ - 1))
    return jnp.where(pick, 1.0, 0.0).astype(F32)


def both_sides(axis):
    at = lax.axis_index(axis)
    return at > 0, at < lax.axis_size(axis) - 1


def place():
    x, y, z = (lax.axis_index(a) for a in AXES)
    ny, nz = lax.axis_size("gy"), lax.axis_size("gz")
    return (x * ny + y) * nz + z, z > 0, z < nz - 1


def y_faces(first, second):
    even = (iota(0) & 1) == 0
    low = jnp.where(even, first, rolled(second, 1, 0))
    high = jnp.where(even, rolled(first, -1, 0), second)
    return low, high


def load_body(basis, phi, vector, rounded, phi_kept, to_first, to_second, sems):
    copies = [
        pltpu.make_async_copy(basis.at[M - 1], vector, sems.at[0]),
        pltpu.make_async_copy(phi, phi_kept, sems.at[1]),
    ]
    for copy in copies:
        copy.start()
    odd = lax.axis_index("gy") % 2 == 1
    copies[0].wait()
    low = vector[...].astype(jnp.bfloat16)
    rounded[...] = low
    to_first[: S * C] = low.astype(F32)
    to_second[: S * C] = low.astype(F32)
    copies[1].wait()
    half = K * C // 2
    for i in range(half):
        low, high = y_faces(phi_kept[i], phi_kept[half + i])
        to_first[S * C + i] = jnp.where(odd, low, high)
        to_second[S * C + i] = jnp.where(odd, high, low)


def rhs_body(vector, phi, out):
    rows = []
    for s in range(S):
        v = [vector[s * C + c] for c in range(C)]
        prods = [sum(phi[k * C + c] * v[c] for c in range(C)) for k in range(K)]
        rows.append(row_sums(prods[:8]))
        rows.append(row_sums(prods[8:]))
    rows.append(jnp.zeros((64, 128), F32))
    rhs = across(jnp.ones((8, 128), F32), jnp.concatenate(rows, 0))
    faces = across(ends(), phi[...].reshape(K * C * XY, CZ))
    n = out.shape[0] // GATHERED
    me, _, _ = place()
    later = lax.broadcasted_iota(jnp.int32, (n, 128), 0) > me
    out[pl.ds(0, n, stride=GATHERED), :] = jnp.broadcast_to(rhs[0:1], (n, 128))
    for r in range(GATHERED - 1):
        row = faces[:, 128 * r : 128 * r + 128]
        out[pl.ds(r + 1, n, stride=GATHERED), :] = jnp.where(later, row[1:2], row[0:1])


def x_faces(blocks, sends, at):
    odd = lax.axis_index("gx") % 2 == 1
    group = iota(0) >> 1
    count = len(blocks) // 4
    for i in range(count):
        low = high = None
        for g in range(4):
            x = blocks[g * count + i]
            to_low, to_high = rolled(x, 2 * g, 0), rolled(x, 2 * g - 6, 0)
            low = to_low if low is None else jnp.where(group == g, to_low, low)
            high = to_high if high is None else jnp.where(group == g, to_high, high)
        sends[0][at + i] = jnp.where(odd, low, high)
        if len(sends) > 1:
            sends[1][at + i] = jnp.where(odd, high, low)


def solve(inv, cols, starts, done):
    def one(c, carry):
        total = [[jnp.zeros((8, 128), F32) for _ in range(XY)] for _ in range(S)]
        for at, j in starts:
            seen = [cols[s, j : j + 16, :].astype(F32) for s in range(S)]
            for i in range(XY):
                w = inv[c, i, at : at + 16, :].astype(F32)
                for s in range(S):
                    part = w * seen[s]
                    total[s][i] = total[s][i] + part[:8] + part[8:]
        for s in range(S):
            done(s * C + c, row_sums(total[s]))
        return carry

    lax.fori_loop(0, C, one, 0)


def early_body(two_x, phi, basis, inv, cols, gram, loc, inv_kept, *refs):
    phi_faces, (sem,) = refs[: 1 + two_x], refs[1 + two_x :]
    copy = pltpu.make_async_copy(inv, inv_kept, sem)
    copy.start()
    rows = []
    for m, n in PAIRS:
        for s in range(S):
            rows.append(sum(basis[m, s * C + c] * basis[n, s * C + c] for c in range(C)))
    rows += [jnp.zeros((8, 128), F32)] * (BASE - len(rows))
    for g in range(0, BASE, 8):
        gram[g : g + 8, :] = row_sums(rows[g : g + 8])

    x_faces([phi[i] for i in range(K * C)], phi_faces, 0)

    def done(i, x):
        loc[i] = x

    copy.wait()
    solve(inv_kept, cols, [(EXTENT * c + SIDE, SIDE * c) for c in range(C)], done)


def local_body(two_x, inv, cols, early, *refs):
    phi_faces, (loc, locz, *sends) = refs[: 1 + two_x], refs[1 + two_x :]

    def done(i, x):
        loc[i] = early[i] + x

    starts = [(EXTENT * c, 2 * SIDE * c) for c in range(C)]
    starts += [(EXTENT * c + 2 * SIDE, 2 * SIDE * c + SIDE) for c in range(C)]
    solve(inv, cols, starts, done)
    locz[...] = across(ends(), loc[...].reshape(S * C * XY, CZ))
    odd_y = lax.axis_index("gy") % 2 == 1
    for i in range(S * C // 2):
        low, high = y_faces(loc[i], loc[S * C // 2 + i])
        sends[0][i] = jnp.where(odd_y, low, high)
        sends[1][i] = jnp.where(odd_y, high, low)
    x_faces([loc[i] for i in range(S * C)], sends[2:], 0)
    for x, known in zip(sends[2:], phi_faces):
        x[C:] = known[...]


def staggered(coef, group):
    out = coef
    for g in range(1, 4):
        out = jnp.where(group == g, rolled(coef, -4 * g, 1), out)
    return out


def slots(two_x):
    return ["own", "ylo", "yhi"] + (["xlo", "xhi"] if two_x else ["x"]) + ["zlo", "zhi"]


def factor_body(two_x, got, locz, factor, out):
    n = factor.shape[1] // K
    stride = out.shape[0] // n
    sub, lane = iota(0), iota(1)
    diag = (lane >> 4) == sub
    image = [jnp.zeros((K, 128), F32) for _ in range(S)]
    for b in range(n // 8):
        rhs = got[pl.ds(8 * GATHERED * b, 8, stride=GATHERED), :]
        rows = factor[:, 128 * b : 128 * b + 128]
        rhs = pltpu.roll(rhs, 0, 1, stride=K, stride_axis=0)
        for s in range(S):
            mine = jnp.where(diag, rolled(rhs, -K * s, 1) if s else rhs, 0.0)
            image[s] = image[s] + rows * jnp.sum(mine, axis=0, keepdims=True)
    image = [jnp.sum(x, axis=1, keepdims=True) for x in image]
    shares = []
    for b in range(n // 8):
        rows = factor[:, 128 * b : 128 * b + 128]
        block = jnp.zeros((8, 128), F32)
        for s in range(S):
            part = jnp.sum(rows * image[s], axis=0, keepdims=True)
            mine = jnp.where(diag, part, 0.0)
            block = block + (rolled(mine, K * s, 1) if s else mine)
        for bit in (1, 2, 4):
            block = jnp.where((sub & bit) == 0, block, rolled(block, -K * bit, 1))
        shares.append(block)
    shares = jnp.concatenate(shares, 0)
    nz = lax.axis_size("gz")
    plane = lax.axis_size("gy") * nz
    shift = {"own": 0, "ylo": nz, "yhi": -nz, "x": plane, "xlo": plane, "xhi": -plane, "zlo": 1, "zhi": -1}
    names = slots(two_x)
    for t in range(0, len(names), 2):
        pair = [rolled(shares, shift[x], 0) if shift[x] else shares for x in names[t : t + 2]]
        row = pair[0] if len(pair) == 1 else pair[0] + rolled(pair[1], 64, 1)
        out[pl.ds(t // 2, n, stride=stride), :] = row
    face = (len(names) + 1) // 2
    for t in range(face, stride):
        out[pl.ds(t, n, stride=stride), :] = jnp.zeros((n, 128), F32)
    me, below, above = place()

    @pl.when(below)
    def _():
        out[pl.ds((me - 1) * stride + face, 1), :] = locz[0:1, :]

    @pl.when(above)
    def _():
        out[pl.ds((me + 1) * stride + face, 1), :] = locz[1:2, :]


def image_body(two_x, loc, phi, diagonal, couple, basis, gram, coarse, got, *rest):
    slabs, faces, (pre, image, sent) = rest[:2], rest[2:-3], rest[-3:]
    n = sent.shape[0]
    stride = coarse.shape[0] // n
    sub, lane = iota(0), iota(1)
    even = (sub & 1) == 0
    if stride == 4:
        total = coarse[0:8, :]
        for b in range(1, coarse.shape[0] // 8):
            total = total + coarse[8 * b : 8 * b + 8, :]
        total = total + rolled(total, 4, 0)
        totals = [all_rows(total, t) for t in range(stride - 1)]
    else:
        totals = [
            jnp.broadcast_to(
                jnp.sum(coarse[pl.ds(t, n, stride=stride), :], axis=0, keepdims=True), (8, 128)
            )
            for t in range(stride - 1)
        ]
    names = slots(two_x)

    def coefs(name):
        at = names.index(name)
        return totals[at // 2] if at % 2 == 0 else rolled(totals[at // 2], 64, 1)

    me, below, above = place()

    lower = sub < 4
    at = [jnp.where(below, me - 1, me), jnp.where(above, me + 1, me)]
    parts = None
    for r in range(8):
        row = got[pl.ds(at[r // 4] * GATHERED + 1 + r % 4, 1), :]
        row = jnp.broadcast_to(row, (8, 128))
        parts = row if r == 0 else jnp.where(sub == r, row, parts)
    coef = staggered(jnp.where(lower, coefs("zlo"), coefs("zhi")), sub & 3)
    z = None
    for s in range(S):
        w = splat(coef, s * K)
        for k in range(1, 4):
            w = jnp.where((lane >> 5) == k, splat(coef, s * K + k), w)
        part = parts * w
        for shift in (32, 64):
            part = part + rolled(part, shift, 1)
        z = part if z is None else jnp.where((lane >> 5) == s, part, z)
    for shift in (1, 2):
        z = z + rolled(z, -shift, 0)
    rows = [coarse[pl.ds(x * stride + stride - 1, 1), :] for x in at]
    rows = [jnp.broadcast_to(x, (8, 128)) for x in rows]
    z = z + jnp.where(lower, rows[0], rows[1])
    there = jnp.where(lower, below.astype(jnp.int32), above.astype(jnp.int32)) == 1
    columns = jnp.transpose(jnp.where(there, z, 0.0))

    own = coefs("own")
    p = [loc[i] for i in range(S * C)]
    for s in range(S):
        for k in range(K):
            w = splat(own, s * K + k)
            for c in range(C):
                p[s * C + c] = p[s * C + c] + w * phi[k * C + c]

    odd_y = lax.axis_index("gy") % 2 == 1
    odd_x = lax.axis_index("gx") % 2 == 1

    has_y, has_x = both_sides("gy"), both_sides("gx")

    def y_side(slab, face, coef):
        coef = jnp.where(even, coef, rolled(coef, -K // 2, 1))
        sums = []
        for s in range(S):
            mine = even if s < 2 else ~even
            part = [jnp.where(mine, face[(s % 2) * C + c], 0.0) for c in range(C)]
            for k in range(K // 2):
                w = splat(coef, s * K + k)
                for c in range(C):
                    part[c] = part[c] + w * slab[S * C + k * C + c]
            sums += part
        return sums

    def x_side(face, coef):
        coef = staggered(coef, sub >> 1)
        sums = []
        for s in range(S):
            part = [jnp.where((sub >> 1) == s, face[c], 0.0) for c in range(C)]
            for k in range(K // 4):
                w = splat(coef, s * K + k)
                for c in range(C):
                    part[c] = part[c] + w * face[C + k * C + c]
            for x in part:
                x = x + rolled(x, 2, 0)
                sums.append(x + rolled(x, 4, 0))
        return sums

    ylo, yhi = coefs("ylo"), coefs("yhi")
    y_first = y_side(slabs[0], faces[0], jnp.where(odd_y, ylo, yhi))
    y_second = y_side(slabs[1], faces[1], jnp.where(odd_y, yhi, ylo))
    if two_x:
        xlo, xhi = coefs("xlo"), coefs("xhi")
        x_first = x_side(faces[2], jnp.where(odd_x, xlo, xhi))
        x_second = x_side(faces[3], jnp.where(odd_x, xhi, xlo))
    else:
        x_first = x_side(faces[2], coefs("x"))
        x_second = x_first

    for s in range(S):
        sides = []
        for c in range(C):
            i = s * C + c
            x = p[i]
            pre[i] = x
            zl = jnp.broadcast_to(columns[i * XY : (i + 1) * XY, 0:1], (8, 128))
            zh = jnp.broadcast_to(columns[i * XY : (i + 1) * XY, 4:5], (8, 128))
            y_low = jnp.where(odd_y, y_first[i], y_second[i])
            y_high = jnp.where(odd_y, y_second[i], y_first[i])
            x_low = jnp.where(odd_x, x_first[i], x_second[i])
            x_high = jnp.where(odd_x, x_second[i], x_first[i])
            y_low = jnp.where(has_y[0], y_low + rolled(y_low, -1, 0), 0.0)
            y_high = jnp.where(has_y[1], y_high + rolled(y_high, 1, 0), 0.0)
            x_low, x_high = jnp.where(has_x[0], x_low, 0.0), jnp.where(has_x[1], x_high, 0.0)
            sides = [
                jnp.where(sub < CY, x_low, rolled(x, CY, 0)),
                jnp.where(sub >= XY - CY, x_high, rolled(x, -CY, 0)),
                jnp.where(even, y_low, rolled(x, 1, 0)),
                jnp.where(even, rolled(x, -1, 0), y_high),
                jnp.where(lane == 0, zl, rolled(x, 1, 1)),
                jnp.where(lane == CZ - 1, zh, rolled(x, -1, 1)),
            ]
            a = sum(diagonal[c * C + d] * p[s * C + d] for d in range(C))
            for d, side in enumerate(sides):
                a = a - couple[d * C + c] * side
            image[i] = a

    rows = []
    for m in range(M):
        for s in range(S):
            rows.append(sum(basis[m, s * C + c] * image[s * C + c] for c in range(C)))
    for s in range(S):
        rows.append(sum(image[s * C + c] * image[s * C + c] for c in range(C)))
    rows += [jnp.zeros((8, 128), F32)] * 4
    sums = [row_sums(rows[g : g + 8]) for g in range(0, 32, 8)]
    sums = jnp.concatenate([gram[...]] + sums + [jnp.zeros((8, 128), F32)], 0)
    row = across(jnp.ones((8, 128), F32), sums)
    sent[...] = jnp.broadcast_to(row[None], (n // 8, 8, 128)).reshape(n, 128)


def tables():
    first = np.zeros((128, 128), np.float32)
    second = np.zeros((128, 128), np.float32)
    out = np.zeros((128, 128), np.float32)
    fixed = np.zeros((8, 128), np.float32)
    for s in range(S):
        for at, (m, n) in enumerate(PAIRS):
            first[BASE + 4 * m + s, 4 * at + s] = 1
            second[BASE + 4 * n + s, 4 * at + s] = 1
            fixed[2, 4 * at + s] = 1 if m == n else 2
        for m in range(M):
            lane = BASE + 4 * m + s
            first[lane, lane] = 1
            fixed[1, lane] = 1
            fixed[2, lane] = -2
        lane = BASE + 4 * M + s
        fixed[0, lane] = fixed[1, lane] = fixed[2, lane] = 1
        for i in range(M + 1):
            out[BASE + 4 * i + s, i] = 1
    return np.stack([first, second, out]).astype(jnp.bfloat16), fixed


def finish_body(unknowns, got, image, basis, maps, fixed, krylov, hessenberg, flag):
    sub, lane = iota(0), iota(1)
    total = got[0:8, :]
    for b in range(1, got.shape[0] // 8):
        total = total + got[8 * b : 8 * b + 8, :]
    for shift in (4, 2, 1):
        total = total + rolled(total, shift, 0)
    h = total / unknowns

    terms = total * all_rows(fixed, 2)
    terms = terms * (times(h, maps[0]) + all_rows(fixed, 0)) * (times(h, maps[1]) + all_rows(fixed, 1))
    size = jnp.abs(terms)
    for shift in (4, 8, 16, 32, 64):
        terms = terms + rolled(terms, shift, 1)
        size = size + rolled(size, shift, 1)
    norm = jnp.sqrt(jnp.maximum(terms, 0.0) / unknowns + epsilon)
    scale = 1.0 / norm
    flag[0] = jnp.max(jnp.where(terms < CANCEL * size, 1, 0))
    for s in range(S):
        w = [splat(h, BASE + 4 * m + s) for m in range(M)]
        f = splat(scale, s)
        for c in range(C):
            i = s * C + c
            krylov[i] = (image[i] - sum(w[m] * basis[m, i] for m in range(M))) * f
    values = jnp.where(lane >= BASE + 4 * M, norm, h)
    values = jnp.where((lane & 3) == sub, values, 0.0)
    hessenberg[...] = times(values, maps[2])[:S, : M + 1]


def pairs_of(axis):
    count = lax.axis_size(axis)
    rounds = [[(i, i + 1) for i in range(0, count, 2)]]
    if count > 2:
        rounds.append([(i, (i + 1) % count) for i in range(1, count, 2)])
    return [r + [(j, i) for i, j in r] for r in rounds]


def swap(axis, low_side, high_side):
    odd = lax.axis_index(axis) % 2 == 1
    rounds = pairs_of(axis)
    sides = [jnp.where(odd, low_side, high_side), jnp.where(odd, high_side, low_side)]
    return [lax.ppermute(x, axis, pairs) for x, pairs in zip(sides, rounds)]


def by_side(axis, got):
    at = lax.axis_index(axis)
    odd = at % 2 == 1
    first, second = got if len(got) == 2 else (got[0], got[0])
    low, high = jnp.where(odd, first, second), jnp.where(odd, second, first)
    none = jnp.zeros_like(first)
    return jnp.where(at > 0, low, none), jnp.where(at < lax.axis_size(axis) - 1, high, none)


def exchange(rows):
    return lax.all_to_all(rows[:, None], AXES, 0, 0, tiled=True).reshape(rows.shape)


def on_device(basis, inverse_rows, block_diag, couple, coarse_basis, coarse_factor):
    n = lax.axis_size("gx") * lax.axis_size("gy") * lax.axis_size("gz")
    unknowns = float(C * XY * CZ * n)
    two_x = lax.axis_size("gx") > 2
    vectors = basis.reshape(M, S * C, XY, CZ)
    phi = coarse_basis.reshape(K * C, XY, CZ)

    slab = S * C + K * C // 2
    vector, rounded, phi, *slabs = call(
        load_body,
        [
            kept(S * C, XY, CZ),
            kept(S * C, XY, CZ, dtype=jnp.bfloat16),
            kept(K * C, XY, CZ),
            kept(slab, XY, CZ),
            kept(slab, XY, CZ),
        ],
        (in_hbm(vectors), in_hbm(phi)),
        S * C * XY * CZ,
        in_specs=[pl.BlockSpec(memory_space=pltpu.HBM)] * 2,
        scratch=[pltpu.SemaphoreType.DMA((2,))],
    )
    rounded = rounded.reshape(S, C, CX, CY, CZ)
    (rhs,) = call(rhs_body, [kept(n * GATHERED, 128)], (vector, phi), 2 * K * S * C * XY * CZ)
    got = exchange(rhs)
    swapped = [lax.ppermute(x, "gy", pairs) for x, pairs in zip(slabs, pairs_of("gy"))]

    always = lax.axis_index("gx") >= 0

    inverse = inverse_rows.reshape(C, XY, ROWS, CZ)

    def extend(swapped, rounded, phi, vectors, inverse):
        parts = [x[: S * C].reshape(S, C, CX, CY, CZ).astype(rounded.dtype) for x in swapped]
        y_low, y_high = by_side("gy", parts)
        extended = jnp.concatenate([y_low, rounded, y_high], axis=3)
        x_low, x_high = by_side("gx", swap("gx", extended[:, :, :2], extended[:, :, -2:]))
        mine = extended.reshape(S, C, CX * (CY + 4), CZ)
        edge = (EXTENT - CX * (CY + 4)) // 2
        middle = mine[:, :, SIDE - edge : 2 * SIDE - edge].reshape(S, C * SIDE, CZ)
        early = call(
            functools.partial(early_body, two_x),
            [kept(BASE, 128), kept(S * C, XY, CZ), kept(*inverse.shape, dtype=inverse.dtype)]
            + [kept(K * C // 4, 8, 128)] * (1 + two_x),
            (phi, vectors, in_hbm(inverse), middle),
            10**10,
            in_specs=[VMEM, VMEM, pl.BlockSpec(memory_space=pltpu.HBM), VMEM],
            scratch=[pltpu.SemaphoreType.DMA],
        )
        outer = jnp.concatenate(
            [
                x_low.reshape(S, C, edge, CZ),
                mine[:, :, : SIDE - edge],
                mine[:, :, 2 * SIDE - edge :],
                x_high.reshape(S, C, edge, CZ),
            ],
            axis=2,
        )
        return [outer.reshape(S, C * 2 * SIDE, CZ)] + list(early)

    def unused(swapped, rounded, phi, vectors, inverse):
        return [
            jnp.zeros((S, C * 2 * SIDE, CZ), rounded.dtype),
            jnp.zeros((BASE, 128), F32),
            jnp.zeros((S * C, XY, CZ), F32),
            jnp.zeros_like(inverse),
        ] + [jnp.zeros((K * C // 4, 8, 128), F32)] * (1 + two_x)

    columns, gram, part, inverse, *phi_faces = lax.cond(
        always, extend, unused, swapped, rounded, phi, vectors, inverse
    )
    half, quarter = S * C // 2, (K + S) * C // 4
    sends = [shape(half, 8, 128)] * 2 + [shape(quarter, 8, 128)] * (2 if two_x else 1)
    loc, locz, *sends = call(
        functools.partial(local_body, two_x),
        [shape(S * C, XY, CZ), shape(8, 128)] + sends,
        (inverse, columns, part, *phi_faces),
        20000 * S * C * XY * ROWS * CZ,
    )

    def trade(*sends):
        x_faces = [lax.ppermute(x, "gx", pairs) for x, pairs in zip(sends[2:], pairs_of("gx"))]
        return [lax.ppermute(x, "gy", pairs) for x, pairs in zip(sends, pairs_of("gy"))] + x_faces

    def untouched(*sends):
        return list(sends)

    stride = (len(slots(two_x)) + 1) // 2 + 1
    (shares,) = call(
        functools.partial(factor_body, two_x),
        [kept(n * stride, 128)],
        (got, locz, coarse_factor),
        4 * S * K * K * n,
    )
    coarse = exchange(shares)
    faces = lax.cond(always, trade, untouched, *sends)
    pre, image, sent = call(
        functools.partial(image_body, two_x),
        [kept(S * C, XY, CZ), kept(S * C, XY, CZ), kept(n, 128)],
        (
            loc,
            phi,
            block_diag.reshape(C * C, XY, CZ),
            couple.reshape(6 * C, XY, CZ),
            vectors,
            gram,
            coarse,
            got,
            *swapped,
            *faces,
        ),
        2 * S * C * XY * CZ * 40,
    )
    products = exchange(sent)
    maps, fixed = tables()
    krylov, hessenberg, flag = call(
        functools.partial(finish_body, unknowns),
        [shape(S * C, XY, CZ), shape(S, M + 1), pltpu.SMEM((1,), jnp.int32)],
        (products, image, vectors, jnp.asarray(maps), jnp.asarray(fixed)),
        2 * S * C * XY * CZ * 8,
        out_specs=[VMEM, VMEM, pl.BlockSpec(memory_space=pltpu.SMEM)],
    )

    def exact(image, vectors, krylov, hessenberg):
        h = hessenberg[:, :M]
        left = image.reshape(S, C, XY, CZ) - jnp.sum(
            h.T[:, :, None, None, None] * vectors.reshape(M, S, C, XY, CZ), axis=0
        )
        squares = jnp.zeros((1, 128), F32).at[0, :S].set(jnp.sum(left * left, axis=(1, 2, 3)))
        squares = jnp.sum(exchange(jnp.broadcast_to(squares, (n, 128))), axis=0)[:S]
        norm = jnp.sqrt(squares / unknowns + epsilon)
        return (
            (left / norm[:, None, None, None]).reshape(S * C, XY, CZ),
            jnp.concatenate([h, norm[:, None]], axis=1),
        )

    def as_is(image, vectors, krylov, hessenberg):
        return krylov, hessenberg

    krylov, hessenberg = lax.cond(
        flag[0] > 0, exact, as_is, image, vectors, krylov, hessenberg
    )
    krylov, pre = lax.optimization_barrier((krylov, pre))
    cells = (S, C, CX, CY, CZ)
    return krylov.reshape(cells), pre.reshape(cells), hessenberg


def solution(mesh):
    return jax.shard_map(
        on_device,
        mesh=mesh,
        in_specs=(
            P(None, None, None, "gx", "gy", "gz"),
            P(None, "gx", "gy", None, "gz"),
            P(None, None, "gx", "gy", "gz"),
            P(None, None, "gx", "gy", "gz"),
            P(None, None, "gx", "gy", "gz"),
            P(AXES, None),
        ),
        out_specs=(P(None, None, "gx", "gy", "gz"), P(None, None, "gx", "gy", "gz"), P()),
        check_vma=False,
    )
```

```python
import functools

import jax
import jax.numpy as jnp
import numpy as np
from jax import lax
from jax.experimental import pallas as pl
from jax.experimental.pallas import tpu as pltpu
from jax.sharding import PartitionSpec as P

C = 4
CX = 4
CY = 2
CZ = 128
S = 4
M = 6
K = 16
XY = CX * CY
GATHERED = 1 + K * C * XY // CZ
EXTENT = (CX + 4) * (CY + 4)
SIDE = EXTENT // 3
ROWS = C * EXTENT
AXES = ("gx", "gy", "gz")
PAIRS = [(m, n) for m in range(M) for n in range(m, M)]
BASE = 88
CANCEL = 1e-2

epsilon = 1e-06

VMEM = pl.BlockSpec(memory_space=pltpu.VMEM)
F32 = jnp.float32


def call(body, outs, operands, flops, in_specs=None, out_specs=None, scratch=()):
    size = sum(int(np.prod(x.shape)) * x.dtype.itemsize for x in list(operands) + list(outs))
    return pl.pallas_call(
        body,
        out_shape=tuple(outs),
        in_specs=in_specs or [VMEM] * len(operands),
        out_specs=tuple(out_specs or [VMEM] * len(outs)),
        scratch_shapes=list(scratch),
        compiler_params=pltpu.CompilerParams(vmem_limit_bytes=24 * 1024 * 1024),
        cost_estimate=pl.CostEstimate(flops=flops, bytes_accessed=size, transcendentals=0),
    )(*operands)


def shape(*dims, dtype=F32):
    return jax.ShapeDtypeStruct(dims, dtype)


def kept(*dims, dtype=F32):
    return pltpu.VMEM(dims, dtype)


def in_hbm(x):
    return pltpu.with_memory_space_constraint(x, pltpu.HBM)


def iota(axis):
    return lax.broadcasted_iota(jnp.int32, (8, 128), axis)


def rolled(x, shift, axis):
    return pltpu.roll(x, shift % x.shape[axis], axis)


def row_sums(blocks):
    sub = iota(0)
    for bit in (4, 2, 1):
        low = (sub & bit) == 0
        half = len(blocks) // 2
        blocks = [
            jnp.where(
                low,
                blocks[i] + rolled(blocks[i], -bit, 0),
                blocks[i + half] + rolled(blocks[i + half], bit, 0),
            )
            for i in range(half)
        ]
    return blocks[0]


def thirds(x):
    parts = []
    for _ in range(3):
        parts.append(x.astype(jnp.bfloat16))
        x = x - parts[-1].astype(F32)
    return parts


def across(left, right):
    left = left.astype(jnp.bfloat16)
    return sum(
        lax.dot_general(left, part, (((1,), (1,)), ((), ())), preferred_element_type=F32)
        for part in thirds(right)
    )


def times(x, table):
    rows = jnp.concatenate([p.astype(F32) for p in thirds(x)] + [jnp.zeros((8, 128), F32)], 0)
    y = jnp.dot(rows.astype(jnp.bfloat16), table, preferred_element_type=F32)
    return y[:8] + y[8:16] + y[16:24]


def all_rows(x, t):
    return jnp.broadcast_to(x[t : t + 1, :], (8, 128))


def splat(x, lane):
    return jnp.broadcast_to(x[:, lane : lane + 1], (8, 128))


def ends():
    sub, lane = iota(0), iota(1)
    pick = ((sub == 0) & (lane == 0)) | ((sub == 1) & (lane == CZ - 1))
    return jnp.where(pick, 1.0, 0.0).astype(F32)


def both_sides(axis):
    at = lax.axis_index(axis)
    return at > 0, at < lax.axis_size(axis) - 1


def place():
    x, y, z = (lax.axis_index(a) for a in AXES)
    ny, nz = lax.axis_size("gy"), lax.axis_size("gz")
    return (x * ny + y) * nz + z, z > 0, z < nz - 1


def y_faces(first, second):
    even = (iota(0) & 1) == 0
    low = jnp.where(even, first, rolled(second, 1, 0))
    high = jnp.where(even, rolled(first, -1, 0), second)
    return low, high


def load_body(basis, phi, vector, rounded, phi_kept, to_first, to_second, sems):
    copies = [
        pltpu.make_async_copy(basis.at[M - 1], vector, sems.at[0]),
        pltpu.make_async_copy(phi, phi_kept, sems.at[1]),
    ]
    for copy in copies:
        copy.start()
    odd = lax.axis_index("gy") % 2 == 1
    copies[0].wait()
    low = vector[...].astype(jnp.bfloat16)
    rounded[...] = low
    to_first[: S * C] = low.astype(F32)
    to_second[: S * C] = low.astype(F32)
    copies[1].wait()
    half = K * C // 2
    for i in range(half):
        low, high = y_faces(phi_kept[i], phi_kept[half + i])
        to_first[S * C + i] = jnp.where(odd, low, high)
        to_second[S * C + i] = jnp.where(odd, high, low)


def rhs_body(vector, phi, out):
    rows = []
    for s in range(S):
        v = [vector[s * C + c] for c in range(C)]
        prods = [sum(phi[k * C + c] * v[c] for c in range(C)) for k in range(K)]
        rows.append(row_sums(prods[:8]))
        rows.append(row_sums(prods[8:]))
    rows.append(jnp.zeros((64, 128), F32))
    rhs = across(jnp.ones((8, 128), F32), jnp.concatenate(rows, 0))
    faces = across(ends(), phi[...].reshape(K * C * XY, CZ))
    n = out.shape[0] // GATHERED
    me, _, _ = place()
    later = lax.broadcasted_iota(jnp.int32, (n, 128), 0) > me
    out[pl.ds(0, n, stride=GATHERED), :] = jnp.broadcast_to(rhs[0:1], (n, 128))
    for r in range(GATHERED - 1):
        row = faces[:, 128 * r : 128 * r + 128]
        out[pl.ds(r + 1, n, stride=GATHERED), :] = jnp.where(later, row[1:2], row[0:1])


def x_faces(blocks, sends, at):
    odd = lax.axis_index("gx") % 2 == 1
    group = iota(0) >> 1
    count = len(blocks) // 4
    for i in range(count):
        low = high = None
        for g in range(4):
            x = blocks[g * count + i]
            to_low, to_high = rolled(x, 2 * g, 0), rolled(x, 2 * g - 6, 0)
            low = to_low if low is None else jnp.where(group == g, to_low, low)
            high = to_high if high is None else jnp.where(group == g, to_high, high)
        sends[0][at + i] = jnp.where(odd, low, high)
        if len(sends) > 1:
            sends[1][at + i] = jnp.where(odd, high, low)


def solve(inv, cols, starts, done, ready=None):
    def one(c, carry):
        if ready is not None:
            ready(c)
        total = [[jnp.zeros((8, 128), F32) for _ in range(XY)] for _ in range(S)]
        for at, j in starts:
            seen = [cols[s, j : j + SIDE, :].astype(F32) for s in range(S)]
            for i in range(XY):
                w = inv[c, i, pl.ds(at, SIDE), :].astype(F32)
                for s in range(S):
                    part = w * seen[s]
                    total[s][i] = total[s][i] + part[:8] + part[8:]
        for s in range(S):
            done(s * C + c, row_sums(total[s]))
        return carry

    lax.fori_loop(0, C, one, 0)


def edge(first):
    return pl.multiple_of(jnp.where(first, 0, 2 * SIDE), SIDE)


def early_body(two_x, phi, basis, inv, cols, gram, loc, inv_kept, *refs):
    phi_faces, (sems,) = refs[: 1 + two_x], refs[1 + two_x :]

    def copy(c):
        return pltpu.make_async_copy(inv.at[c], inv_kept.at[c], sems.at[c])

    for c in range(C):
        copy(c).start()
    rows = []
    for m, n in PAIRS:
        for s in range(S):
            rows.append(sum(basis[m, s * C + c] * basis[n, s * C + c] for c in range(C)))
    rows += [jnp.zeros((8, 128), F32)] * (BASE - len(rows))
    for g in range(0, BASE, 8):
        gram[g : g + 8, :] = row_sums(rows[g : g + 8])

    x_faces([phi[i] for i in range(K * C)], phi_faces, 0)

    def done(i, x):
        loc[i] = x

    if two_x:
        starts = [(EXTENT * c + SIDE, SIDE * c) for c in range(C)]
    else:
        at = edge(lax.axis_index("gx") == 0)
        starts = [(EXTENT * c + SIDE, 2 * SIDE * c) for c in range(C)]
        starts += [(EXTENT * c + at, 2 * SIDE * c + SIDE) for c in range(C)]
    solve(inv_kept, cols, starts, done, lambda c: copy(c).wait())


def local_body(two_x, inv, cols, early, *refs):
    phi_faces, (loc, locz, *sends) = refs[: 1 + two_x], refs[1 + two_x :]

    def done(i, x):
        loc[i] = early[i] + x

    if two_x:
        starts = [(EXTENT * c, 2 * SIDE * c) for c in range(C)]
        starts += [(EXTENT * c + 2 * SIDE, 2 * SIDE * c + SIDE) for c in range(C)]
    else:
        at = edge(lax.axis_index("gx") == 1)
        starts = [(EXTENT * c + at, SIDE * c) for c in range(C)]
    solve(inv, cols, starts, done)
    locz[...] = across(ends(), loc[...].reshape(S * C * XY, CZ))
    odd_y = lax.axis_index("gy") % 2 == 1
    for i in range(S * C // 2):
        low, high = y_faces(loc[i], loc[S * C // 2 + i])
        sends[0][i] = jnp.where(odd_y, low, high)
        sends[1][i] = jnp.where(odd_y, high, low)
    x_faces([loc[i] for i in range(S * C)], sends[2:], 0)
    for x, known in zip(sends[2:], phi_faces):
        x[C:] = known[...]


def staggered(coef, group):
    out = coef
    for g in range(1, 4):
        out = jnp.where(group == g, rolled(coef, -4 * g, 1), out)
    return out


def slots(two_x):
    return ["own", "ylo", "yhi"] + (["xlo", "xhi"] if two_x else ["x"]) + ["zlo", "zhi"]


def factor_body(two_x, got, locz, factor, out):
    n = factor.shape[1] // K
    stride = out.shape[0] // n
    sub, lane = iota(0), iota(1)
    diag = (lane >> 4) == sub
    image = [jnp.zeros((K, 128), F32) for _ in range(S)]
    for b in range(n // 8):
        rhs = got[pl.ds(8 * GATHERED * b, 8, stride=GATHERED), :]
        rows = factor[:, 128 * b : 128 * b + 128]
        rhs = pltpu.roll(rhs, 0, 1, stride=K, stride_axis=0)
        for s in range(S):
            mine = jnp.where(diag, rolled(rhs, -K * s, 1) if s else rhs, 0.0)
            image[s] = image[s] + rows * jnp.sum(mine, axis=0, keepdims=True)
    image = [jnp.sum(x, axis=1, keepdims=True) for x in image]
    shares = []
    for b in range(n // 8):
        rows = factor[:, 128 * b : 128 * b + 128]
        block = jnp.zeros((8, 128), F32)
        for s in range(S):
            part = jnp.sum(rows * image[s], axis=0, keepdims=True)
            mine = jnp.where(diag, part, 0.0)
            block = block + (rolled(mine, K * s, 1) if s else mine)
        for bit in (1, 2, 4):
            block = jnp.where((sub & bit) == 0, block, rolled(block, -K * bit, 1))
        shares.append(block)
    shares = jnp.concatenate(shares, 0)
    nz = lax.axis_size("gz")
    plane = lax.axis_size("gy") * nz
    shift = {"own": 0, "ylo": nz, "yhi": -nz, "x": plane, "xlo": plane, "xhi": -plane, "zlo": 1, "zhi": -1}
    names = slots(two_x)
    for t in range(0, len(names), 2):
        pair = [rolled(shares, shift[x], 0) if shift[x] else shares for x in names[t : t + 2]]
        row = pair[0] if len(pair) == 1 else pair[0] + rolled(pair[1], 64, 1)
        out[pl.ds(t // 2, n, stride=stride), :] = row
    face = (len(names) + 1) // 2
    for t in range(face, stride):
        out[pl.ds(t, n, stride=stride), :] = jnp.zeros((n, 128), F32)
    me, below, above = place()

    @pl.when(below)
    def _():
        out[pl.ds((me - 1) * stride + face, 1), :] = locz[0:1, :]

    @pl.when(above)
    def _():
        out[pl.ds((me + 1) * stride + face, 1), :] = locz[1:2, :]


def image_body(two_x, loc, phi, diagonal, couple, basis, gram, coarse, got, *rest):
    slabs, faces, (pre, image, sent) = rest[:2], rest[2:-3], rest[-3:]
    n = sent.shape[0]
    stride = coarse.shape[0] // n
    sub, lane = iota(0), iota(1)
    even = (sub & 1) == 0
    if stride == 4:
        total = coarse[0:8, :]
        for b in range(1, coarse.shape[0] // 8):
            total = total + coarse[8 * b : 8 * b + 8, :]
        total = total + rolled(total, 4, 0)
        totals = [all_rows(total, t) for t in range(stride - 1)]
    else:
        totals = [
            jnp.broadcast_to(
                jnp.sum(coarse[pl.ds(t, n, stride=stride), :], axis=0, keepdims=True), (8, 128)
            )
            for t in range(stride - 1)
        ]
    names = slots(two_x)

    def coefs(name):
        at = names.index(name)
        return totals[at // 2] if at % 2 == 0 else rolled(totals[at // 2], 64, 1)

    me, below, above = place()

    lower = sub < 4
    at = [jnp.where(below, me - 1, me), jnp.where(above, me + 1, me)]
    parts = None
    for r in range(8):
        row = got[pl.ds(at[r // 4] * GATHERED + 1 + r % 4, 1), :]
        row = jnp.broadcast_to(row, (8, 128))
        parts = row if r == 0 else jnp.where(sub == r, row, parts)
    coef = staggered(jnp.where(lower, coefs("zlo"), coefs("zhi")), sub & 3)
    z = None
    for s in range(S):
        w = splat(coef, s * K)
        for k in range(1, 4):
            w = jnp.where((lane >> 5) == k, splat(coef, s * K + k), w)
        part = parts * w
        for shift in (32, 64):
            part = part + rolled(part, shift, 1)
        z = part if z is None else jnp.where((lane >> 5) == s, part, z)
    for shift in (1, 2):
        z = z + rolled(z, -shift, 0)
    rows = [coarse[pl.ds(x * stride + stride - 1, 1), :] for x in at]
    rows = [jnp.broadcast_to(x, (8, 128)) for x in rows]
    z = z + jnp.where(lower, rows[0], rows[1])
    there = jnp.where(lower, below.astype(jnp.int32), above.astype(jnp.int32)) == 1
    columns = jnp.transpose(jnp.where(there, z, 0.0))

    own = coefs("own")
    p = [loc[i] for i in range(S * C)]
    for s in range(S):
        for k in range(K):
            w = splat(own, s * K + k)
            for c in range(C):
                p[s * C + c] = p[s * C + c] + w * phi[k * C + c]

    odd_y = lax.axis_index("gy") % 2 == 1
    odd_x = lax.axis_index("gx") % 2 == 1

    has_y, has_x = both_sides("gy"), both_sides("gx")

    def y_side(slab, face, coef):
        coef = jnp.where(even, coef, rolled(coef, -K // 2, 1))
        sums = []
        for s in range(S):
            mine = even if s < 2 else ~even
            part = [jnp.where(mine, face[(s % 2) * C + c], 0.0) for c in range(C)]
            for k in range(K // 2):
                w = splat(coef, s * K + k)
                for c in range(C):
                    part[c] = part[c] + w * slab[S * C + k * C + c]
            sums += part
        return sums

    def x_side(face, coef):
        coef = staggered(coef, sub >> 1)
        sums = []
        for s in range(S):
            part = [jnp.where((sub >> 1) == s, face[c], 0.0) for c in range(C)]
            for k in range(K // 4):
                w = splat(coef, s * K + k)
                for c in range(C):
                    part[c] = part[c] + w * face[C + k * C + c]
            for x in part:
                x = x + rolled(x, 2, 0)
                sums.append(x + rolled(x, 4, 0))
        return sums

    ylo, yhi = coefs("ylo"), coefs("yhi")
    y_first = y_side(slabs[0], faces[0], jnp.where(odd_y, ylo, yhi))
    y_second = y_side(slabs[1], faces[1], jnp.where(odd_y, yhi, ylo))
    if two_x:
        xlo, xhi = coefs("xlo"), coefs("xhi")
        x_first = x_side(faces[2], jnp.where(odd_x, xlo, xhi))
        x_second = x_side(faces[3], jnp.where(odd_x, xhi, xlo))
    else:
        x_first = x_side(faces[2], coefs("x"))
        x_second = x_first

    for s in range(S):
        sides = []
        for c in range(C):
            i = s * C + c
            x = p[i]
            pre[i] = x
            zl = jnp.broadcast_to(columns[i * XY : (i + 1) * XY, 0:1], (8, 128))
            zh = jnp.broadcast_to(columns[i * XY : (i + 1) * XY, 4:5], (8, 128))
            y_low = jnp.where(odd_y, y_first[i], y_second[i])
            y_high = jnp.where(odd_y, y_second[i], y_first[i])
            x_low = jnp.where(odd_x, x_first[i], x_second[i])
            x_high = jnp.where(odd_x, x_second[i], x_first[i])
            y_low = jnp.where(has_y[0], y_low + rolled(y_low, -1, 0), 0.0)
            y_high = jnp.where(has_y[1], y_high + rolled(y_high, 1, 0), 0.0)
            x_low, x_high = jnp.where(has_x[0], x_low, 0.0), jnp.where(has_x[1], x_high, 0.0)
            sides = [
                jnp.where(sub < CY, x_low, rolled(x, CY, 0)),
                jnp.where(sub >= XY - CY, x_high, rolled(x, -CY, 0)),
                jnp.where(even, y_low, rolled(x, 1, 0)),
                jnp.where(even, rolled(x, -1, 0), y_high),
                jnp.where(lane == 0, zl, rolled(x, 1, 1)),
                jnp.where(lane == CZ - 1, zh, rolled(x, -1, 1)),
            ]
            a = sum(diagonal[c * C + d] * p[s * C + d] for d in range(C))
            for d, side in enumerate(sides):
                a = a - couple[d * C + c] * side
            image[i] = a

    rows = []
    for m in range(M):
        for s in range(S):
            rows.append(sum(basis[m, s * C + c] * image[s * C + c] for c in range(C)))
    for s in range(S):
        rows.append(sum(image[s * C + c] * image[s * C + c] for c in range(C)))
    rows += [jnp.zeros((8, 128), F32)] * 4
    sums = [row_sums(rows[g : g + 8]) for g in range(0, 32, 8)]
    sums = jnp.concatenate([gram[...]] + sums + [jnp.zeros((8, 128), F32)], 0)
    row = across(jnp.ones((8, 128), F32), sums)
    sent[...] = jnp.broadcast_to(row[None], (n // 8, 8, 128)).reshape(n, 128)


def tables():
    first = np.zeros((128, 128), np.float32)
    second = np.zeros((128, 128), np.float32)
    out = np.zeros((128, 128), np.float32)
    fixed = np.zeros((8, 128), np.float32)
    for s in range(S):
        for at, (m, n) in enumerate(PAIRS):
            first[BASE + 4 * m + s, 4 * at + s] = 1
            second[BASE + 4 * n + s, 4 * at + s] = 1
            fixed[2, 4 * at + s] = 1 if m == n else 2
        for m in range(M):
            lane = BASE + 4 * m + s
            first[lane, lane] = 1
            fixed[1, lane] = 1
            fixed[2, lane] = -2
        lane = BASE + 4 * M + s
        fixed[0, lane] = fixed[1, lane] = fixed[2, lane] = 1
        for i in range(M + 1):
            out[BASE + 4 * i + s, i] = 1
    return np.stack([first, second, out]).astype(jnp.bfloat16), fixed


def finish_body(unknowns, got, image, basis, maps, fixed, krylov, hessenberg, flag):
    sub, lane = iota(0), iota(1)
    total = got[0:8, :]
    for b in range(1, got.shape[0] // 8):
        total = total + got[8 * b : 8 * b + 8, :]
    for shift in (4, 2, 1):
        total = total + rolled(total, shift, 0)
    h = total / unknowns

    terms = total * all_rows(fixed, 2)
    terms = terms * (times(h, maps[0]) + all_rows(fixed, 0)) * (times(h, maps[1]) + all_rows(fixed, 1))
    size = jnp.abs(terms)
    for shift in (4, 8, 16, 32, 64):
        terms = terms + rolled(terms, shift, 1)
        size = size + rolled(size, shift, 1)
    norm = jnp.sqrt(jnp.maximum(terms, 0.0) / unknowns + epsilon)
    scale = 1.0 / norm
    flag[0] = jnp.max(jnp.where(terms < CANCEL * size, 1, 0))
    for s in range(S):
        w = [splat(h, BASE + 4 * m + s) for m in range(M)]
        f = splat(scale, s)
        for c in range(C):
            i = s * C + c
            krylov[i] = (image[i] - sum(w[m] * basis[m, i] for m in range(M))) * f
    values = jnp.where(lane >= BASE + 4 * M, norm, h)
    values = jnp.where((lane & 3) == sub, values, 0.0)
    hessenberg[...] = times(values, maps[2])[:S, : M + 1]


def pairs_of(axis):
    count = lax.axis_size(axis)
    rounds = [[(i, i + 1) for i in range(0, count, 2)]]
    if count > 2:
        rounds.append([(i, (i + 1) % count) for i in range(1, count, 2)])
    return [r + [(j, i) for i, j in r] for r in rounds]


def swap(axis, low_side, high_side):
    odd = lax.axis_index(axis) % 2 == 1
    rounds = pairs_of(axis)
    sides = [jnp.where(odd, low_side, high_side), jnp.where(odd, high_side, low_side)]
    return [lax.ppermute(x, axis, pairs) for x, pairs in zip(sides, rounds)]


def by_side(axis, got):
    at = lax.axis_index(axis)
    odd = at % 2 == 1
    first, second = got if len(got) == 2 else (got[0], got[0])
    low, high = jnp.where(odd, first, second), jnp.where(odd, second, first)
    none = jnp.zeros_like(first)
    return jnp.where(at > 0, low, none), jnp.where(at < lax.axis_size(axis) - 1, high, none)


def exchange(rows):
    return lax.all_to_all(rows[:, None], AXES, 0, 0, tiled=True).reshape(rows.shape)


def on_device(basis, inverse_rows, block_diag, couple, coarse_basis, coarse_factor):
    n = lax.axis_size("gx") * lax.axis_size("gy") * lax.axis_size("gz")
    unknowns = float(C * XY * CZ * n)
    two_x = lax.axis_size("gx") > 2
    vectors = basis.reshape(M, S * C, XY, CZ)
    phi = coarse_basis.reshape(K * C, XY, CZ)

    slab = S * C + K * C // 2
    vector, rounded, phi, *slabs = call(
        load_body,
        [
            kept(S * C, XY, CZ),
            kept(S * C, XY, CZ, dtype=jnp.bfloat16),
            kept(K * C, XY, CZ),
            kept(slab, XY, CZ),
            kept(slab, XY, CZ),
        ],
        (in_hbm(vectors), in_hbm(phi)),
        S * C * XY * CZ,
        in_specs=[pl.BlockSpec(memory_space=pltpu.HBM)] * 2,
        scratch=[pltpu.SemaphoreType.DMA((2,))],
    )
    rounded = rounded.reshape(S, C, CX, CY, CZ)
    (rhs,) = call(rhs_body, [kept(n * GATHERED, 128)], (vector, phi), 2 * K * S * C * XY * CZ)
    got = exchange(rhs)
    swapped = [lax.ppermute(x, "gy", pairs) for x, pairs in zip(slabs, pairs_of("gy"))]

    always = lax.axis_index("gx") >= 0

    inverse = inverse_rows.reshape(C, XY, ROWS, CZ)

    def extend(swapped, rounded, phi, vectors, inverse):
        parts = [x[: S * C].reshape(S, C, CX, CY, CZ).astype(rounded.dtype) for x in swapped]
        y_low, y_high = by_side("gy", parts)
        extended = jnp.concatenate([y_low, rounded, y_high], axis=3)
        slabs = swap("gx", extended[:, :, :2], extended[:, :, -2:])
        mine = extended.reshape(S, C, CX * (CY + 4), CZ)
        width = (EXTENT - CX * (CY + 4)) // 2
        low, high = mine[:, :, : SIDE - width], mine[:, :, 2 * SIDE - width :]
        middle = mine[:, :, SIDE - width : 2 * SIDE - width]
        first = lax.axis_index("gx") == 0
        none = jnp.zeros((S, C, width, CZ), rounded.dtype)
        if not two_x:
            ending = jnp.where(
                first, jnp.concatenate([none, low], axis=2), jnp.concatenate([high, none], axis=2)
            )
            middle = jnp.concatenate([middle, ending], axis=2)
        middle = middle.reshape(S, -1, CZ)
        early = call(
            functools.partial(early_body, two_x),
            [kept(BASE, 128), kept(S * C, XY, CZ), kept(*inverse.shape, dtype=inverse.dtype)]
            + [kept(K * C // 4, 8, 128)] * (1 + two_x),
            (phi, vectors, in_hbm(inverse), middle),
            10**10,
            in_specs=[VMEM, VMEM, pl.BlockSpec(memory_space=pltpu.HBM), VMEM],
            scratch=[pltpu.SemaphoreType.DMA((C,))],
        )
        slabs, early = lax.optimization_barrier((slabs, early))
        if two_x:
            slabs = [x.reshape(S, C, width, CZ) for x in by_side("gx", slabs)]
            outer = jnp.concatenate([slabs[0], low, high, slabs[1]], axis=2)
        else:
            slab = slabs[0].reshape(S, C, width, CZ)
            outer = jnp.where(
                first, jnp.concatenate([high, slab], axis=2), jnp.concatenate([slab, low], axis=2)
            )
        return [outer.reshape(S, -1, CZ)] + list(early)

    def unused(swapped, rounded, phi, vectors, inverse):
        return [
            jnp.zeros((S, C * SIDE * (1 + two_x), CZ), rounded.dtype),
            jnp.zeros((BASE, 128), F32),
            jnp.zeros((S * C, XY, CZ), F32),
            jnp.zeros_like(inverse),
        ] + [jnp.zeros((K * C // 4, 8, 128), F32)] * (1 + two_x)

    columns, gram, part, inverse, *phi_faces = lax.cond(
        always, extend, unused, swapped, rounded, phi, vectors, inverse
    )
    half, quarter = S * C // 2, (K + S) * C // 4
    sends = [shape(half, 8, 128)] * 2 + [shape(quarter, 8, 128)] * (2 if two_x else 1)
    loc, locz, *sends = call(
        functools.partial(local_body, two_x),
        [shape(S * C, XY, CZ), shape(8, 128)] + sends,
        (inverse, columns, part, *phi_faces),
        20000 * S * C * XY * ROWS * CZ,
    )

    def trade(*sends):
        x_faces = [lax.ppermute(x, "gx", pairs) for x, pairs in zip(sends[2:], pairs_of("gx"))]
        return [lax.ppermute(x, "gy", pairs) for x, pairs in zip(sends, pairs_of("gy"))] + x_faces

    def untouched(*sends):
        return list(sends)

    stride = (len(slots(two_x)) + 1) // 2 + 1
    (shares,) = call(
        functools.partial(factor_body, two_x),
        [kept(n * stride, 128)],
        (got, locz, coarse_factor),
        4 * S * K * K * n,
    )
    coarse = exchange(shares)
    faces = lax.cond(always, trade, untouched, *sends)
    pre, image, sent = call(
        functools.partial(image_body, two_x),
        [kept(S * C, XY, CZ), kept(S * C, XY, CZ), kept(n, 128)],
        (
            loc,
            phi,
            block_diag.reshape(C * C, XY, CZ),
            couple.reshape(6 * C, XY, CZ),
            vectors,
            gram,
            coarse,
            got,
            *swapped,
            *faces,
        ),
        2 * S * C * XY * CZ * 40,
    )
    products = exchange(sent)
    maps, fixed = tables()
    krylov, hessenberg, flag = call(
        functools.partial(finish_body, unknowns),
        [shape(S * C, XY, CZ), shape(S, M + 1), pltpu.SMEM((1,), jnp.int32)],
        (products, image, vectors, jnp.asarray(maps), jnp.asarray(fixed)),
        2 * S * C * XY * CZ * 8,
        out_specs=[VMEM, VMEM, pl.BlockSpec(memory_space=pltpu.SMEM)],
    )

    def exact(image, vectors, krylov, hessenberg):
        h = hessenberg[:, :M]
        left = image.reshape(S, C, XY, CZ) - jnp.sum(
            h.T[:, :, None, None, None] * vectors.reshape(M, S, C, XY, CZ), axis=0
        )
        squares = jnp.zeros((1, 128), F32).at[0, :S].set(jnp.sum(left * left, axis=(1, 2, 3)))
        squares = jnp.sum(exchange(jnp.broadcast_to(squares, (n, 128))), axis=0)[:S]
        norm = jnp.sqrt(squares / unknowns + epsilon)
        return (
            (left / norm[:, None, None, None]).reshape(S * C, XY, CZ),
            jnp.concatenate([h, norm[:, None]], axis=1),
        )

    def as_is(image, vectors, krylov, hessenberg):
        return krylov, hessenberg

    krylov, hessenberg = lax.cond(
        flag[0] > 0, exact, as_is, image, vectors, krylov, hessenberg
    )
    krylov, pre = lax.optimization_barrier((krylov, pre))
    cells = (S, C, CX, CY, CZ)
    return krylov.reshape(cells), pre.reshape(cells), hessenberg


def solution(mesh):
    return jax.shard_map(
        on_device,
        mesh=mesh,
        in_specs=(
            P(None, None, None, "gx", "gy", "gz"),
            P(None, "gx", "gy", None, "gz"),
            P(None, None, "gx", "gy", "gz"),
            P(None, None, "gx", "gy", "gz"),
            P(None, None, "gx", "gy", "gz"),
            P(AXES, None),
        ),
        out_specs=(P(None, None, "gx", "gy", "gz"), P(None, None, "gx", "gy", "gz"), P()),
        check_vma=False,
    )
```

```python
import functools

import jax
import jax.numpy as jnp
import numpy as np
from jax import lax
from jax.experimental import pallas as pl
from jax.experimental.pallas import tpu as pltpu
from jax.sharding import PartitionSpec as P

C = 4
CX = 4
CY = 2
CZ = 128
S = 4
M = 6
K = 16
XY = CX * CY
GATHERED = 1 + K * C * XY // CZ
EXTENT = (CX + 4) * (CY + 4)
SIDE = EXTENT // 3
ROWS = C * EXTENT
AXES = ("gx", "gy", "gz")
PAIRS = [(m, n) for m in range(M) for n in range(m, M)]
BASE = 88
CANCEL = 1e-2

epsilon = 1e-06

VMEM = pl.BlockSpec(memory_space=pltpu.VMEM)
HBM = pl.BlockSpec(memory_space=pltpu.HBM)
F32 = jnp.float32


def call(body, outs, operands, flops, in_specs=None, out_specs=None, scratch=()):
    size = sum(int(np.prod(x.shape)) * x.dtype.itemsize for x in list(operands) + list(outs))
    return pl.pallas_call(
        body,
        out_shape=tuple(outs),
        in_specs=in_specs or [VMEM] * len(operands),
        out_specs=tuple(out_specs or [VMEM] * len(outs)),
        scratch_shapes=list(scratch),
        compiler_params=pltpu.CompilerParams(vmem_limit_bytes=24 * 1024 * 1024),
        cost_estimate=pl.CostEstimate(flops=flops, bytes_accessed=size, transcendentals=0),
    )(*operands)


def shape(*dims, dtype=F32):
    return jax.ShapeDtypeStruct(dims, dtype)


def kept(*dims, dtype=F32):
    return pltpu.VMEM(dims, dtype)


def in_hbm(x):
    return pltpu.with_memory_space_constraint(x, pltpu.HBM)


def iota(axis):
    return lax.broadcasted_iota(jnp.int32, (8, 128), axis)


def rolled(x, shift, axis):
    return pltpu.roll(x, shift % x.shape[axis], axis)


def row_sums(blocks):
    sub = iota(0)
    for bit in (4, 2, 1):
        low = (sub & bit) == 0
        half = len(blocks) // 2
        blocks = [
            jnp.where(
                low,
                blocks[i] + rolled(blocks[i], -bit, 0),
                blocks[i + half] + rolled(blocks[i + half], bit, 0),
            )
            for i in range(half)
        ]
    return blocks[0]


def thirds(x):
    parts = []
    for _ in range(3):
        parts.append(x.astype(jnp.bfloat16))
        x = x - parts[-1].astype(F32)
    return parts


def across(left, right):
    left = left.astype(jnp.bfloat16)
    return sum(
        lax.dot_general(left, part, (((1,), (1,)), ((), ())), preferred_element_type=F32)
        for part in thirds(right)
    )


def times(x, table):
    rows = jnp.concatenate([p.astype(F32) for p in thirds(x)] + [jnp.zeros((8, 128), F32)], 0)
    y = jnp.dot(rows.astype(jnp.bfloat16), table, preferred_element_type=F32)
    return y[:8] + y[8:16] + y[16:24]


def all_rows(x, t):
    return jnp.broadcast_to(x[t : t + 1, :], (8, 128))


def splat(x, lane):
    return jnp.broadcast_to(x[:, lane : lane + 1], (8, 128))


def ends():
    sub, lane = iota(0), iota(1)
    pick = ((sub == 0) & (lane == 0)) | ((sub == 1) & (lane == CZ - 1))
    return jnp.where(pick, 1.0, 0.0).astype(F32)


def both_sides(axis):
    at = lax.axis_index(axis)
    return at > 0, at < lax.axis_size(axis) - 1


def place():
    x, y, z = (lax.axis_index(a) for a in AXES)
    ny, nz = lax.axis_size("gy"), lax.axis_size("gz")
    return (x * ny + y) * nz + z, z > 0, z < nz - 1


def y_faces(first, second):
    even = (iota(0) & 1) == 0
    low = jnp.where(even, first, rolled(second, 1, 0))
    high = jnp.where(even, rolled(first, -1, 0), second)
    return low, high


def load_body(basis, phi, vector, rounded, phi_kept, to_first, to_second, sems):
    copies = [
        pltpu.make_async_copy(basis.at[M - 1], vector, sems.at[0]),
        pltpu.make_async_copy(phi, phi_kept, sems.at[1]),
    ]
    for copy in copies:
        copy.start()
    odd = lax.axis_index("gy") % 2 == 1
    copies[0].wait()
    low = vector[...].astype(jnp.bfloat16)
    rounded[...] = low
    to_first[: S * C] = low.astype(F32)
    to_second[: S * C] = low.astype(F32)
    copies[1].wait()
    half = K * C // 2
    for i in range(half):
        low, high = y_faces(phi_kept[i], phi_kept[half + i])
        to_first[S * C + i] = jnp.where(odd, low, high)
        to_second[S * C + i] = jnp.where(odd, high, low)


def rhs_body(vector, phi, out):
    rows = []
    for s in range(S):
        v = [vector[s * C + c] for c in range(C)]
        prods = [sum(phi[k * C + c] * v[c] for c in range(C)) for k in range(K)]
        rows.append(row_sums(prods[:8]))
        rows.append(row_sums(prods[8:]))
    rows.append(jnp.zeros((64, 128), F32))
    rhs = across(jnp.ones((8, 128), F32), jnp.concatenate(rows, 0))
    faces = across(ends(), phi[...].reshape(K * C * XY, CZ))
    n = out.shape[0] // GATHERED
    me, _, _ = place()
    later = lax.broadcasted_iota(jnp.int32, (n, 128), 0) > me
    out[pl.ds(0, n, stride=GATHERED), :] = jnp.broadcast_to(rhs[0:1], (n, 128))
    for r in range(GATHERED - 1):
        row = faces[:, 128 * r : 128 * r + 128]
        out[pl.ds(r + 1, n, stride=GATHERED), :] = jnp.where(later, row[1:2], row[0:1])


def x_faces(blocks, sends, at):
    odd = lax.axis_index("gx") % 2 == 1
    group = iota(0) >> 1
    count = len(blocks) // 4
    for i in range(count):
        low = high = None
        for g in range(4):
            x = blocks[g * count + i]
            to_low, to_high = rolled(x, 2 * g, 0), rolled(x, 2 * g - 6, 0)
            low = to_low if low is None else jnp.where(group == g, to_low, low)
            high = to_high if high is None else jnp.where(group == g, to_high, high)
        sends[0][at + i] = jnp.where(odd, low, high)
        if len(sends) > 1:
            sends[1][at + i] = jnp.where(odd, high, low)


def solve(inv, cols, starts, done, ready=None, unroll=False):
    def one(c, carry):
        if ready is not None:
            ready(c)
        total = [[jnp.zeros((8, 128), F32) for _ in range(XY)] for _ in range(S)]
        for at, j in starts:
            seen = [cols[s, j : j + SIDE, :].astype(F32) for s in range(S)]
            for i in range(XY):
                w = inv[c, i, pl.ds(at, SIDE), :].astype(F32)
                for s in range(S):
                    part = w * seen[s]
                    total[s][i] = total[s][i] + part[:8] + part[8:]
        for s in range(S):
            done(s * C + c, row_sums(total[s]))
        return carry

    if unroll:
        for c in range(C):
            one(c, 0)
    else:
        lax.fori_loop(0, C, one, 0)


def edge(first):
    return pl.multiple_of(jnp.where(first, 0, 2 * SIDE), SIDE)


def early_body(two_x, phi, basis, inv, cols, gram, loc, inv_kept, *refs):
    phi_faces, (vectors, sems) = refs[: 1 + two_x], refs[1 + two_x :]
    fetch = pltpu.make_async_copy(basis, vectors, sems.at[C])
    fetch.start()

    def copy(c):
        return pltpu.make_async_copy(inv.at[c], inv_kept.at[c], sems.at[c])

    for c in range(C):
        copy(c).start()
    x_faces([phi[i] for i in range(K * C)], phi_faces, 0)

    def done(i, x):
        loc[i] = x

    if two_x:
        starts = [(EXTENT * c + SIDE, SIDE * c) for c in range(C)]
    else:
        at = edge(lax.axis_index("gx") == 0)
        starts = [(EXTENT * c + SIDE, 2 * SIDE * c) for c in range(C)]
        starts += [(EXTENT * c + at, 2 * SIDE * c + SIDE) for c in range(C)]
    solve(inv_kept, cols, starts, done, lambda c: copy(c).wait())
    fetch.wait()
    rows = []
    for m, n in PAIRS:
        for s in range(S):
            rows.append(sum(vectors[m, s * C + c] * vectors[n, s * C + c] for c in range(C)))
    rows += [jnp.zeros((8, 128), F32)] * (BASE - len(rows))
    for g in range(0, BASE, 8):
        gram[g : g + 8, :] = row_sums(rows[g : g + 8])


def slots(two_x):
    return ["own", "ylo", "yhi"] + (["xlo", "xhi"] if two_x else ["x"]) + ["zlo", "zhi"]


def factor_body(two_x, got, factor, out):
    n = factor.shape[1] // K
    stride = out.shape[0] // n
    sub, lane = iota(0), iota(1)
    diag = (lane >> 4) == sub
    image = [jnp.zeros((K, 128), F32) for _ in range(S)]
    for b in range(n // 8):
        rhs = got[pl.ds(8 * GATHERED * b, 8, stride=GATHERED), :]
        rows = factor[:, 128 * b : 128 * b + 128]
        rhs = pltpu.roll(rhs, 0, 1, stride=K, stride_axis=0)
        for s in range(S):
            mine = jnp.where(diag, rolled(rhs, -K * s, 1) if s else rhs, 0.0)
            image[s] = image[s] + rows * jnp.sum(mine, axis=0, keepdims=True)
    image = [jnp.sum(x, axis=1, keepdims=True) for x in image]
    shares = []
    for b in range(n // 8):
        rows = factor[:, 128 * b : 128 * b + 128]
        block = jnp.zeros((8, 128), F32)
        for s in range(S):
            part = jnp.sum(rows * image[s], axis=0, keepdims=True)
            mine = jnp.where(diag, part, 0.0)
            block = block + (rolled(mine, K * s, 1) if s else mine)
        for bit in (1, 2, 4):
            block = jnp.where((sub & bit) == 0, block, rolled(block, -K * bit, 1))
        shares.append(block)
    shares = jnp.concatenate(shares, 0)
    nz = lax.axis_size("gz")
    plane = lax.axis_size("gy") * nz
    shift = {"own": 0, "ylo": nz, "yhi": -nz, "x": plane, "xlo": plane, "xhi": -plane, "zlo": 1, "zhi": -1}
    names = slots(two_x)
    for t in range(0, len(names), 2):
        pair = [rolled(shares, shift[x], 0) if shift[x] else shares for x in names[t : t + 2]]
        row = pair[0] if len(pair) == 1 else pair[0] + rolled(pair[1], 64, 1)
        out[pl.ds(t // 2, n, stride=stride), :] = row
    face = (len(names) + 1) // 2
    for t in range(face, stride):
        out[pl.ds(t, n, stride=stride), :] = jnp.zeros((n, 128), F32)


def send_ends(two_x, locz, out):
    face = (len(slots(two_x)) + 1) // 2
    stride = face + 1
    me, below, above = place()

    @pl.when(below)
    def _():
        out[pl.ds((me - 1) * stride + face, 1), :] = locz[0:1]

    @pl.when(above)
    def _():
        out[pl.ds((me + 1) * stride + face, 1), :] = locz[1:2]


def local_body(two_x, inv, cols, early, got, factor, *refs):
    phi_faces, (out, loc, *sends) = refs[: 1 + two_x], refs[1 + two_x :]
    factor_body(two_x, got, factor, out)

    def done(i, x):
        loc[i] = early[i] + x

    if two_x:
        starts = [(EXTENT * c, 2 * SIDE * c) for c in range(C)]
        starts += [(EXTENT * c + 2 * SIDE, 2 * SIDE * c + SIDE) for c in range(C)]
    else:
        at = edge(lax.axis_index("gx") == 1)
        starts = [(EXTENT * c + at, SIDE * c) for c in range(C)]
    solve(inv, cols, starts, done, unroll=True)
    send_ends(two_x, across(ends(), loc[...].reshape(S * C * XY, CZ)), out)
    odd_y = lax.axis_index("gy") % 2 == 1
    for i in range(S * C // 2):
        low, high = y_faces(loc[i], loc[S * C // 2 + i])
        sends[0][i] = jnp.where(odd_y, low, high)
        sends[1][i] = jnp.where(odd_y, high, low)
    x_faces([loc[i] for i in range(S * C)], sends[2:], 0)
    for x, known in zip(sends[2:], phi_faces):
        x[C:] = known[...]


def staggered(coef, group):
    out = coef
    for g in range(1, 4):
        out = jnp.where(group == g, rolled(coef, -4 * g, 1), out)
    return out


def image_body(two_x, loc, phi, diagonal, couple, basis, gram, coarse, got, *rest):
    slabs, faces, (pre, image, sent) = rest[:2], rest[2:-3], rest[-3:]
    n = sent.shape[0]
    stride = coarse.shape[0] // n
    sub, lane = iota(0), iota(1)
    even = (sub & 1) == 0
    if stride == 4:
        total = coarse[0:8, :]
        for b in range(1, coarse.shape[0] // 8):
            total = total + coarse[8 * b : 8 * b + 8, :]
        total = total + rolled(total, 4, 0)
        totals = [all_rows(total, t) for t in range(stride - 1)]
    else:
        totals = [
            jnp.broadcast_to(
                jnp.sum(coarse[pl.ds(t, n, stride=stride), :], axis=0, keepdims=True), (8, 128)
            )
            for t in range(stride - 1)
        ]
    names = slots(two_x)

    def coefs(name):
        at = names.index(name)
        return totals[at // 2] if at % 2 == 0 else rolled(totals[at // 2], 64, 1)

    me, below, above = place()

    lower = sub < 4
    at = [jnp.where(below, me - 1, me), jnp.where(above, me + 1, me)]
    parts = None
    for r in range(8):
        row = got[pl.ds(at[r // 4] * GATHERED + 1 + r % 4, 1), :]
        row = jnp.broadcast_to(row, (8, 128))
        parts = row if r == 0 else jnp.where(sub == r, row, parts)
    coef = staggered(jnp.where(lower, coefs("zlo"), coefs("zhi")), sub & 3)
    z = None
    for s in range(S):
        w = splat(coef, s * K)
        for k in range(1, 4):
            w = jnp.where((lane >> 5) == k, splat(coef, s * K + k), w)
        part = parts * w
        for shift in (32, 64):
            part = part + rolled(part, shift, 1)
        z = part if z is None else jnp.where((lane >> 5) == s, part, z)
    for shift in (1, 2):
        z = z + rolled(z, -shift, 0)
    rows = [coarse[pl.ds(x * stride + stride - 1, 1), :] for x in at]
    rows = [jnp.broadcast_to(x, (8, 128)) for x in rows]
    z = z + jnp.where(lower, rows[0], rows[1])
    there = jnp.where(lower, below.astype(jnp.int32), above.astype(jnp.int32)) == 1
    columns = jnp.transpose(jnp.where(there, z, 0.0))

    own = coefs("own")
    p = [loc[i] for i in range(S * C)]
    for s in range(S):
        for k in range(K):
            w = splat(own, s * K + k)
            for c in range(C):
                p[s * C + c] = p[s * C + c] + w * phi[k * C + c]

    odd_y = lax.axis_index("gy") % 2 == 1
    odd_x = lax.axis_index("gx") % 2 == 1

    has_y, has_x = both_sides("gy"), both_sides("gx")

    def y_side(slab, face, coef):
        coef = jnp.where(even, coef, rolled(coef, -K // 2, 1))
        sums = []
        for s in range(S):
            mine = even if s < 2 else ~even
            part = [jnp.where(mine, face[(s % 2) * C + c], 0.0) for c in range(C)]
            for k in range(K // 2):
                w = splat(coef, s * K + k)
                for c in range(C):
                    part[c] = part[c] + w * slab[S * C + k * C + c]
            sums += part
        return sums

    def x_side(face, coef):
        coef = staggered(coef, sub >> 1)
        sums = []
        for s in range(S):
            part = [jnp.where((sub >> 1) == s, face[c], 0.0) for c in range(C)]
            for k in range(K // 4):
                w = splat(coef, s * K + k)
                for c in range(C):
                    part[c] = part[c] + w * face[C + k * C + c]
            for x in part:
                x = x + rolled(x, 2, 0)
                sums.append(x + rolled(x, 4, 0))
        return sums

    ylo, yhi = coefs("ylo"), coefs("yhi")
    y_first = y_side(slabs[0], faces[0], jnp.where(odd_y, ylo, yhi))
    y_second = y_side(slabs[1], faces[1], jnp.where(odd_y, yhi, ylo))
    if two_x:
        xlo, xhi = coefs("xlo"), coefs("xhi")
        x_first = x_side(faces[2], jnp.where(odd_x, xlo, xhi))
        x_second = x_side(faces[3], jnp.where(odd_x, xhi, xlo))
    else:
        x_first = x_side(faces[2], coefs("x"))
        x_second = x_first

    for s in range(S):
        sides = []
        for c in range(C):
            i = s * C + c
            x = p[i]
            pre[i] = x
            zl = jnp.broadcast_to(columns[i * XY : (i + 1) * XY, 0:1], (8, 128))
            zh = jnp.broadcast_to(columns[i * XY : (i + 1) * XY, 4:5], (8, 128))
            y_low = jnp.where(odd_y, y_first[i], y_second[i])
            y_high = jnp.where(odd_y, y_second[i], y_first[i])
            x_low = jnp.where(odd_x, x_first[i], x_second[i])
            x_high = jnp.where(odd_x, x_second[i], x_first[i])
            y_low = jnp.where(has_y[0], y_low + rolled(y_low, -1, 0), 0.0)
            y_high = jnp.where(has_y[1], y_high + rolled(y_high, 1, 0), 0.0)
            x_low, x_high = jnp.where(has_x[0], x_low, 0.0), jnp.where(has_x[1], x_high, 0.0)
            sides = [
                jnp.where(sub < CY, x_low, rolled(x, CY, 0)),
                jnp.where(sub >= XY - CY, x_high, rolled(x, -CY, 0)),
                jnp.where(even, y_low, rolled(x, 1, 0)),
                jnp.where(even, rolled(x, -1, 0), y_high),
                jnp.where(lane == 0, zl, rolled(x, 1, 1)),
                jnp.where(lane == CZ - 1, zh, rolled(x, -1, 1)),
            ]
            a = sum(diagonal[c * C + d] * p[s * C + d] for d in range(C))
            for d, side in enumerate(sides):
                a = a - couple[d * C + c] * side
            image[i] = a

    rows = []
    for m in range(M):
        for s in range(S):
            rows.append(sum(basis[m, s * C + c] * image[s * C + c] for c in range(C)))
    for s in range(S):
        rows.append(sum(image[s * C + c] * image[s * C + c] for c in range(C)))
    rows += [jnp.zeros((8, 128), F32)] * 4
    sums = [row_sums(rows[g : g + 8]) for g in range(0, 32, 8)]
    sums = jnp.concatenate([gram[...]] + sums + [jnp.zeros((8, 128), F32)], 0)
    row = across(jnp.ones((8, 128), F32), sums)
    sent[...] = jnp.broadcast_to(row[None], (n // 8, 8, 128)).reshape(n, 128)


def tables():
    first = np.zeros((128, 128), np.float32)
    second = np.zeros((128, 128), np.float32)
    out = np.zeros((128, 128), np.float32)
    fixed = np.zeros((8, 128), np.float32)
    for s in range(S):
        for at, (m, n) in enumerate(PAIRS):
            first[BASE + 4 * m + s, 4 * at + s] = 1
            second[BASE + 4 * n + s, 4 * at + s] = 1
            fixed[2, 4 * at + s] = 1 if m == n else 2
        for m in range(M):
            lane = BASE + 4 * m + s
            first[lane, lane] = 1
            fixed[1, lane] = 1
            fixed[2, lane] = -2
        lane = BASE + 4 * M + s
        fixed[0, lane] = fixed[1, lane] = fixed[2, lane] = 1
        for i in range(M + 1):
            out[BASE + 4 * i + s, i] = 1
    return np.stack([first, second, out]).astype(jnp.bfloat16), fixed


def finish_body(unknowns, got, image, basis, maps, fixed, krylov, hessenberg, flag):
    sub, lane = iota(0), iota(1)
    total = got[0:8, :]
    for b in range(1, got.shape[0] // 8):
        total = total + got[8 * b : 8 * b + 8, :]
    for shift in (4, 2, 1):
        total = total + rolled(total, shift, 0)
    h = total / unknowns

    terms = total * all_rows(fixed, 2)
    terms = terms * (times(h, maps[0]) + all_rows(fixed, 0)) * (times(h, maps[1]) + all_rows(fixed, 1))
    size = jnp.abs(terms)
    for shift in (4, 8, 16, 32, 64):
        terms = terms + rolled(terms, shift, 1)
        size = size + rolled(size, shift, 1)
    norm = jnp.sqrt(jnp.maximum(terms, 0.0) / unknowns + epsilon)
    scale = 1.0 / norm
    flag[0] = jnp.max(jnp.where(terms < CANCEL * size, 1, 0))
    for s in range(S):
        w = [splat(h, BASE + 4 * m + s) for m in range(M)]
        f = splat(scale, s)
        for c in range(C):
            i = s * C + c
            krylov[i] = (image[i] - sum(w[m] * basis[m, i] for m in range(M))) * f
    values = jnp.where(lane >= BASE + 4 * M, norm, h)
    values = jnp.where((lane & 3) == sub, values, 0.0)
    hessenberg[...] = times(values, maps[2])[:S, : M + 1]


def pairs_of(axis):
    count = lax.axis_size(axis)
    rounds = [[(i, i + 1) for i in range(0, count, 2)]]
    if count > 2:
        rounds.append([(i, (i + 1) % count) for i in range(1, count, 2)])
    return [r + [(j, i) for i, j in r] for r in rounds]


def swap(axis, low_side, high_side):
    odd = lax.axis_index(axis) % 2 == 1
    rounds = pairs_of(axis)
    sides = [jnp.where(odd, low_side, high_side), jnp.where(odd, high_side, low_side)]
    return [lax.ppermute(x, axis, pairs) for x, pairs in zip(sides, rounds)]


def by_side(axis, got):
    at = lax.axis_index(axis)
    odd = at % 2 == 1
    first, second = got if len(got) == 2 else (got[0], got[0])
    low, high = jnp.where(odd, first, second), jnp.where(odd, second, first)
    none = jnp.zeros_like(first)
    return jnp.where(at > 0, low, none), jnp.where(at < lax.axis_size(axis) - 1, high, none)


def exchange(rows):
    return lax.all_to_all(rows[:, None], AXES, 0, 0, tiled=True).reshape(rows.shape)


def on_device(basis, inverse_rows, block_diag, couple, coarse_basis, coarse_factor):
    n = lax.axis_size("gx") * lax.axis_size("gy") * lax.axis_size("gz")
    unknowns = float(C * XY * CZ * n)
    two_x = lax.axis_size("gx") > 2
    vectors = basis.reshape(M, S * C, XY, CZ)
    phi = coarse_basis.reshape(K * C, XY, CZ)

    slab = S * C + K * C // 2
    vector, rounded, phi, *slabs = call(
        load_body,
        [
            kept(S * C, XY, CZ),
            kept(S * C, XY, CZ, dtype=jnp.bfloat16),
            kept(K * C, XY, CZ),
            kept(slab, XY, CZ),
            kept(slab, XY, CZ),
        ],
        (in_hbm(vectors), in_hbm(phi)),
        S * C * XY * CZ,
        in_specs=[HBM] * 2,
        scratch=[pltpu.SemaphoreType.DMA((2,))],
    )
    rounded = rounded.reshape(S, C, CX, CY, CZ)
    (rhs,) = call(rhs_body, [kept(n * GATHERED, 128)], (vector, phi), 2 * K * S * C * XY * CZ)
    got = exchange(rhs)
    swapped = [lax.ppermute(x, "gy", pairs) for x, pairs in zip(slabs, pairs_of("gy"))]

    always = lax.axis_index("gx") >= 0

    inverse = inverse_rows.reshape(C, XY, ROWS, CZ)

    def extend(swapped, rounded, phi, vectors, inverse):
        parts = [x[: S * C].reshape(S, C, CX, CY, CZ).astype(rounded.dtype) for x in swapped]
        y_low, y_high = by_side("gy", parts)
        extended = jnp.concatenate([y_low, rounded, y_high], axis=3)
        slabs = swap("gx", extended[:, :, :2], extended[:, :, -2:])
        mine = extended.reshape(S, C, CX * (CY + 4), CZ)
        width = (EXTENT - CX * (CY + 4)) // 2
        low, high = mine[:, :, : SIDE - width], mine[:, :, 2 * SIDE - width :]
        middle = mine[:, :, SIDE - width : 2 * SIDE - width]
        first = lax.axis_index("gx") == 0
        none = jnp.zeros((S, C, width, CZ), rounded.dtype)
        if not two_x:
            ending = jnp.where(
                first, jnp.concatenate([none, low], axis=2), jnp.concatenate([high, none], axis=2)
            )
            middle = jnp.concatenate([middle, ending], axis=2)
        middle = middle.reshape(S, -1, CZ)
        early = call(
            functools.partial(early_body, two_x),
            [kept(BASE, 128), kept(S * C, XY, CZ), kept(*inverse.shape, dtype=inverse.dtype)]
            + [kept(K * C // 4, 8, 128)] * (1 + two_x),
            (phi, in_hbm(vectors), in_hbm(inverse), middle),
            10**10,
            in_specs=[VMEM, HBM, HBM, VMEM],
            scratch=[pltpu.VMEM(vectors.shape, F32), pltpu.SemaphoreType.DMA((C + 1,))],
        )
        slabs, early = lax.optimization_barrier((slabs, early))
        if two_x:
            slabs = [x.reshape(S, C, width, CZ) for x in by_side("gx", slabs)]
            outer = jnp.concatenate([slabs[0], low, high, slabs[1]], axis=2)
        else:
            slab = slabs[0].reshape(S, C, width, CZ)
            outer = jnp.where(
                first, jnp.concatenate([high, slab], axis=2), jnp.concatenate([slab, low], axis=2)
            )
        return [outer.reshape(S, -1, CZ)] + list(early)

    def unused(swapped, rounded, phi, vectors, inverse):
        return [
            jnp.zeros((S, C * SIDE * (1 + two_x), CZ), rounded.dtype),
            jnp.zeros((BASE, 128), F32),
            jnp.zeros((S * C, XY, CZ), F32),
            jnp.zeros_like(inverse),
        ] + [jnp.zeros((K * C // 4, 8, 128), F32)] * (1 + two_x)

    columns, gram, part, inverse, *phi_faces = lax.cond(
        always, extend, unused, swapped, rounded, phi, vectors, inverse
    )
    half, quarter = S * C // 2, (K + S) * C // 4
    sends = [shape(half, 8, 128)] * 2 + [shape(quarter, 8, 128)] * (2 if two_x else 1)
    stride = (len(slots(two_x)) + 1) // 2 + 1
    shares, loc, *sends = call(
        functools.partial(local_body, two_x),
        [kept(n * stride, 128), shape(S * C, XY, CZ)] + sends,
        (inverse, columns, part, got, coarse_factor, *phi_faces),
        2 * S * C * XY * C * SIDE * CZ,
    )

    def trade(*sends):
        x_faces = [lax.ppermute(x, "gx", pairs) for x, pairs in zip(sends[2:], pairs_of("gx"))]
        return [lax.ppermute(x, "gy", pairs) for x, pairs in zip(sends, pairs_of("gy"))] + x_faces

    def untouched(*sends):
        return list(sends)

    coarse = exchange(shares)
    faces = lax.cond(always, trade, untouched, *sends)
    pre, image, sent = call(
        functools.partial(image_body, two_x),
        [kept(S * C, XY, CZ), kept(S * C, XY, CZ), kept(n, 128)],
        (
            loc,
            phi,
            block_diag.reshape(C * C, XY, CZ),
            couple.reshape(6 * C, XY, CZ),
            vectors,
            gram,
            coarse,
            got,
            *swapped,
            *faces,
        ),
        2 * S * C * XY * CZ * 40,
    )
    products = exchange(sent)
    maps, fixed = tables()
    krylov, hessenberg, flag = call(
        functools.partial(finish_body, unknowns),
        [shape(S * C, XY, CZ), shape(S, M + 1), pltpu.SMEM((1,), jnp.int32)],
        (products, image, vectors, jnp.asarray(maps), jnp.asarray(fixed)),
        2 * S * C * XY * CZ * 8,
        out_specs=[VMEM, VMEM, pl.BlockSpec(memory_space=pltpu.SMEM)],
    )

    def exact(image, vectors, krylov, hessenberg):
        h = hessenberg[:, :M]
        left = image.reshape(S, C, XY, CZ) - jnp.sum(
            h.T[:, :, None, None, None] * vectors.reshape(M, S, C, XY, CZ), axis=0
        )
        squares = jnp.zeros((1, 128), F32).at[0, :S].set(jnp.sum(left * left, axis=(1, 2, 3)))
        squares = jnp.sum(exchange(jnp.broadcast_to(squares, (n, 128))), axis=0)[:S]
        norm = jnp.sqrt(squares / unknowns + epsilon)
        return (
            (left / norm[:, None, None, None]).reshape(S * C, XY, CZ),
            jnp.concatenate([h, norm[:, None]], axis=1),
        )

    def as_is(image, vectors, krylov, hessenberg):
        return krylov, hessenberg

    krylov, hessenberg = lax.cond(
        flag[0] > 0, exact, as_is, image, vectors, krylov, hessenberg
    )
    krylov, pre = lax.optimization_barrier((krylov, pre))
    cells = (S, C, CX, CY, CZ)
    return krylov.reshape(cells), pre.reshape(cells), hessenberg


def solution(mesh):
    return jax.shard_map(
        on_device,
        mesh=mesh,
        in_specs=(
            P(None, None, None, "gx", "gy", "gz"),
            P(None, "gx", "gy", None, "gz"),
            P(None, None, "gx", "gy", "gz"),
            P(None, None, "gx", "gy", "gz"),
            P(None, None, "gx", "gy", "gz"),
            P(AXES, None),
        ),
        out_specs=(P(None, None, "gx", "gy", "gz"), P(None, None, "gx", "gy", "gz"), P()),
        check_vma=False,
    )
```

```python
import functools

import jax
import jax.numpy as jnp
import numpy as np
from jax import lax
from jax.experimental import pallas as pl
from jax.experimental.pallas import tpu as pltpu
from jax.sharding import PartitionSpec as P

C = 4
CX = 4
CY = 2
CZ = 128
S = 4
M = 6
K = 16
XY = CX * CY
GATHERED = 1 + K * C * XY // CZ
EXTENT = (CX + 4) * (CY + 4)
SIDE = EXTENT // 3
ROWS = C * EXTENT
AXES = ("gx", "gy", "gz")
PAIRS = [(m, n) for m in range(M) for n in range(m, M)]
BASE = 88
CANCEL = 1e-2

epsilon = 1e-06

VMEM = pl.BlockSpec(memory_space=pltpu.VMEM)
HBM = pl.BlockSpec(memory_space=pltpu.HBM)
F32 = jnp.float32


def call(body, outs, operands, flops, in_specs=None, out_specs=None, scratch=()):
    size = sum(int(np.prod(x.shape)) * x.dtype.itemsize for x in list(operands) + list(outs))
    return pl.pallas_call(
        body,
        out_shape=tuple(outs),
        in_specs=in_specs or [VMEM] * len(operands),
        out_specs=tuple(out_specs or [VMEM] * len(outs)),
        scratch_shapes=list(scratch),
        compiler_params=pltpu.CompilerParams(vmem_limit_bytes=24 * 1024 * 1024),
        cost_estimate=pl.CostEstimate(flops=flops, bytes_accessed=size, transcendentals=0),
    )(*operands)


def shape(*dims, dtype=F32):
    return jax.ShapeDtypeStruct(dims, dtype)


def kept(*dims, dtype=F32):
    return pltpu.VMEM(dims, dtype)


def in_hbm(x):
    return pltpu.with_memory_space_constraint(x, pltpu.HBM)


def iota(axis):
    return lax.broadcasted_iota(jnp.int32, (8, 128), axis)


def rolled(x, shift, axis):
    return pltpu.roll(x, shift % x.shape[axis], axis)


def row_sums(blocks):
    sub = iota(0)
    for bit in (4, 2, 1):
        low = (sub & bit) == 0
        half = len(blocks) // 2
        blocks = [
            jnp.where(
                low,
                blocks[i] + rolled(blocks[i], -bit, 0),
                blocks[i + half] + rolled(blocks[i + half], bit, 0),
            )
            for i in range(half)
        ]
    return blocks[0]


def thirds(x):
    parts = []
    for _ in range(3):
        parts.append(x.astype(jnp.bfloat16))
        x = x - parts[-1].astype(F32)
    return parts


def across(left, right):
    left = left.astype(jnp.bfloat16)
    return sum(
        lax.dot_general(left, part, (((1,), (1,)), ((), ())), preferred_element_type=F32)
        for part in thirds(right)
    )


def times(x, table):
    rows = jnp.concatenate([p.astype(F32) for p in thirds(x)] + [jnp.zeros((8, 128), F32)], 0)
    y = jnp.dot(rows.astype(jnp.bfloat16), table, preferred_element_type=F32)
    return y[:8] + y[8:16] + y[16:24]


def all_rows(x, t):
    return jnp.broadcast_to(x[t : t + 1, :], (8, 128))


def splat(x, lane):
    return jnp.broadcast_to(x[:, lane : lane + 1], (8, 128))


def ends():
    sub, lane = iota(0), iota(1)
    pick = ((sub == 0) & (lane == 0)) | ((sub == 1) & (lane == CZ - 1))
    return jnp.where(pick, 1.0, 0.0).astype(F32)


def both_sides(axis):
    at = lax.axis_index(axis)
    return at > 0, at < lax.axis_size(axis) - 1


def place():
    x, y, z = (lax.axis_index(a) for a in AXES)
    ny, nz = lax.axis_size("gy"), lax.axis_size("gz")
    return (x * ny + y) * nz + z, z > 0, z < nz - 1


def y_faces(first, second):
    even = (iota(0) & 1) == 0
    low = jnp.where(even, first, rolled(second, 1, 0))
    high = jnp.where(even, rolled(first, -1, 0), second)
    return low, high


def load_body(basis, phi, vector, rounded, phi_kept, to_first, to_second, sems):
    copies = [
        pltpu.make_async_copy(basis.at[M - 1], vector, sems.at[0]),
        pltpu.make_async_copy(phi, phi_kept, sems.at[1]),
    ]
    for copy in copies:
        copy.start()
    odd = lax.axis_index("gy") % 2 == 1
    copies[0].wait()
    low = vector[...].astype(jnp.bfloat16)
    rounded[...] = low
    to_first[: S * C] = low.astype(F32)
    to_second[: S * C] = low.astype(F32)
    copies[1].wait()
    half = K * C // 2
    for i in range(half):
        low, high = y_faces(phi_kept[i], phi_kept[half + i])
        to_first[S * C + i] = jnp.where(odd, low, high)
        to_second[S * C + i] = jnp.where(odd, high, low)


def rhs_body(vector, phi, out):
    rows = []
    for s in range(S):
        v = [vector[s * C + c] for c in range(C)]
        prods = [sum(phi[k * C + c] * v[c] for c in range(C)) for k in range(K)]
        rows.append(row_sums(prods[:8]))
        rows.append(row_sums(prods[8:]))
    rows.append(jnp.zeros((64, 128), F32))
    rhs = across(jnp.ones((8, 128), F32), jnp.concatenate(rows, 0))
    faces = across(ends(), phi[...].reshape(K * C * XY, CZ))
    n = out.shape[0] // GATHERED
    me, _, _ = place()
    later = lax.broadcasted_iota(jnp.int32, (n, 128), 0) > me
    out[pl.ds(0, n, stride=GATHERED), :] = jnp.broadcast_to(rhs[0:1], (n, 128))
    for r in range(GATHERED - 1):
        row = faces[:, 128 * r : 128 * r + 128]
        out[pl.ds(r + 1, n, stride=GATHERED), :] = jnp.where(later, row[1:2], row[0:1])


def x_faces(blocks, sends, at):
    odd = lax.axis_index("gx") % 2 == 1
    group = iota(0) >> 1
    count = len(blocks) // 4
    for i in range(count):
        low = high = None
        for g in range(4):
            x = blocks[g * count + i]
            to_low, to_high = rolled(x, 2 * g, 0), rolled(x, 2 * g - 6, 0)
            low = to_low if low is None else jnp.where(group == g, to_low, low)
            high = to_high if high is None else jnp.where(group == g, to_high, high)
        sends[0][at + i] = jnp.where(odd, low, high)
        if len(sends) > 1:
            sends[1][at + i] = jnp.where(odd, high, low)


def solve(inv, cols, starts, done, ready=None, unroll=False):
    def one(c, carry):
        if ready is not None:
            ready(c)
        total = [[jnp.zeros((8, 128), F32) for _ in range(XY)] for _ in range(S)]
        for at, j in starts:
            seen = [cols[s, j : j + SIDE, :].astype(F32) for s in range(S)]
            for i in range(XY):
                w = inv[c, i, pl.ds(at, SIDE), :].astype(F32)
                for s in range(S):
                    part = w * seen[s]
                    total[s][i] = total[s][i] + part[:8] + part[8:]
        for s in range(S):
            done(s * C + c, row_sums(total[s]))
        return carry

    if unroll:
        for c in range(C):
            one(c, 0)
    else:
        lax.fori_loop(0, C, one, 0)


def edge(first):
    return pl.multiple_of(jnp.where(first, 0, 2 * SIDE), SIDE)


def early_body(two_x, phi, basis, inv, cols, gram, loc, inv_kept, *refs):
    phi_faces, (vectors, sems) = refs[: 1 + two_x], refs[1 + two_x :]
    fetch = pltpu.make_async_copy(basis, vectors, sems.at[C])
    fetch.start()

    def copy(c):
        return pltpu.make_async_copy(inv.at[c], inv_kept.at[c], sems.at[c])

    for c in range(C):
        copy(c).start()
    x_faces([phi[i] for i in range(K * C)], phi_faces, 0)

    def done(i, x):
        loc[i] = x

    if two_x:
        starts = [(EXTENT * c + SIDE, SIDE * c) for c in range(C)]
    else:
        at = edge(lax.axis_index("gx") == 0)
        starts = [(EXTENT * c + SIDE, 2 * SIDE * c) for c in range(C)]
        starts += [(EXTENT * c + at, 2 * SIDE * c + SIDE) for c in range(C)]
    solve(inv_kept, cols, starts, done, lambda c: copy(c).wait())
    fetch.wait()
    rows = []
    for m, n in PAIRS:
        for s in range(S):
            rows.append(sum(vectors[m, s * C + c] * vectors[n, s * C + c] for c in range(C)))
    rows += [jnp.zeros((8, 128), F32)] * (BASE - len(rows))
    for g in range(0, BASE, 8):
        gram[g : g + 8, :] = row_sums(rows[g : g + 8])


def slots(two_x):
    return ["own", "ylo", "yhi"] + (["xlo", "xhi"] if two_x else ["x"]) + ["zlo", "zhi"]


def factor_body(two_x, got, factor, out):
    n = factor.shape[1] // K
    stride = out.shape[0] // n
    sub, lane = iota(0), iota(1)
    diag = (lane >> 4) == sub
    image = [jnp.zeros((K, 128), F32) for _ in range(S)]
    for b in range(n // 8):
        rhs = got[pl.ds(8 * GATHERED * b, 8, stride=GATHERED), :]
        rows = factor[:, 128 * b : 128 * b + 128]
        rhs = pltpu.roll(rhs, 0, 1, stride=K, stride_axis=0)
        for s in range(S):
            mine = jnp.where(diag, rolled(rhs, -K * s, 1) if s else rhs, 0.0)
            image[s] = image[s] + rows * jnp.sum(mine, axis=0, keepdims=True)
    image = [jnp.sum(x, axis=1, keepdims=True) for x in image]
    shares = []
    for b in range(n // 8):
        rows = factor[:, 128 * b : 128 * b + 128]
        block = jnp.zeros((8, 128), F32)
        for s in range(S):
            part = jnp.sum(rows * image[s], axis=0, keepdims=True)
            mine = jnp.where(diag, part, 0.0)
            block = block + (rolled(mine, K * s, 1) if s else mine)
        for bit in (1, 2, 4):
            block = jnp.where((sub & bit) == 0, block, rolled(block, -K * bit, 1))
        shares.append(block)
    shares = jnp.concatenate(shares, 0)
    nz = lax.axis_size("gz")
    plane = lax.axis_size("gy") * nz
    shift = {"own": 0, "ylo": nz, "yhi": -nz, "x": plane, "xlo": plane, "xhi": -plane, "zlo": 1, "zhi": -1}
    names = slots(two_x)
    for t in range(0, len(names), 2):
        pair = [rolled(shares, shift[x], 0) if shift[x] else shares for x in names[t : t + 2]]
        row = pair[0] if len(pair) == 1 else pair[0] + rolled(pair[1], 64, 1)
        out[pl.ds(t // 2, n, stride=stride), :] = row
    face = (len(names) + 1) // 2
    for t in range(face, stride):
        out[pl.ds(t, n, stride=stride), :] = jnp.zeros((n, 128), F32)


def send_ends(two_x, locz, out):
    face = (len(slots(two_x)) + 1) // 2
    stride = face + 1
    me, below, above = place()

    @pl.when(below)
    def _():
        out[pl.ds((me - 1) * stride + face, 1), :] = locz[0:1]

    @pl.when(above)
    def _():
        out[pl.ds((me + 1) * stride + face, 1), :] = locz[1:2]


def local_body(two_x, inv, cols, early, got, factor, *refs):
    phi_faces, (out, loc, *sends) = refs[: 1 + two_x], refs[1 + two_x :]

    def done(i, x):
        loc[i] = early[i] + x

    if two_x:
        starts = [(EXTENT * c, 2 * SIDE * c) for c in range(C)]
        starts += [(EXTENT * c + 2 * SIDE, 2 * SIDE * c + SIDE) for c in range(C)]
    else:
        at = edge(lax.axis_index("gx") == 1)
        starts = [(EXTENT * c + at, SIDE * c) for c in range(C)]
    solve(inv, cols, starts, done, unroll=True)
    factor_body(two_x, got, factor, out)
    send_ends(two_x, across(ends(), loc[...].reshape(S * C * XY, CZ)), out)
    odd_y = lax.axis_index("gy") % 2 == 1
    for i in range(S * C // 2):
        low, high = y_faces(loc[i], loc[S * C // 2 + i])
        sends[0][i] = jnp.where(odd_y, low, high)
        sends[1][i] = jnp.where(odd_y, high, low)
    x_faces([loc[i] for i in range(S * C)], sends[2:], 0)
    for x, known in zip(sends[2:], phi_faces):
        x[C:] = known[...]


def staggered(coef, group):
    out = coef
    for g in range(1, 4):
        out = jnp.where(group == g, rolled(coef, -4 * g, 1), out)
    return out


def image_body(two_x, loc, phi, diagonal, couple, basis, gram, coarse, got, *rest):
    slabs, faces, (pre, image, sent) = rest[:2], rest[2:-3], rest[-3:]
    n = sent.shape[0]
    stride = coarse.shape[0] // n
    sub, lane = iota(0), iota(1)
    even = (sub & 1) == 0
    if stride == 4:
        total = coarse[0:8, :]
        for b in range(1, coarse.shape[0] // 8):
            total = total + coarse[8 * b : 8 * b + 8, :]
        total = total + rolled(total, 4, 0)
        totals = [all_rows(total, t) for t in range(stride - 1)]
    else:
        totals = [
            jnp.broadcast_to(
                jnp.sum(coarse[pl.ds(t, n, stride=stride), :], axis=0, keepdims=True), (8, 128)
            )
            for t in range(stride - 1)
        ]
    names = slots(two_x)

    def coefs(name):
        at = names.index(name)
        return totals[at // 2] if at % 2 == 0 else rolled(totals[at // 2], 64, 1)

    me, below, above = place()

    lower = sub < 4
    at = [jnp.where(below, me - 1, me), jnp.where(above, me + 1, me)]
    parts = None
    for r in range(8):
        row = got[pl.ds(at[r // 4] * GATHERED + 1 + r % 4, 1), :]
        row = jnp.broadcast_to(row, (8, 128))
        parts = row if r == 0 else jnp.where(sub == r, row, parts)
    coef = staggered(jnp.where(lower, coefs("zlo"), coefs("zhi")), sub & 3)
    z = None
    for s in range(S):
        w = splat(coef, s * K)
        for k in range(1, 4):
            w = jnp.where((lane >> 5) == k, splat(coef, s * K + k), w)
        part = parts * w
        for shift in (32, 64):
            part = part + rolled(part, shift, 1)
        z = part if z is None else jnp.where((lane >> 5) == s, part, z)
    for shift in (1, 2):
        z = z + rolled(z, -shift, 0)
    rows = [coarse[pl.ds(x * stride + stride - 1, 1), :] for x in at]
    rows = [jnp.broadcast_to(x, (8, 128)) for x in rows]
    z = z + jnp.where(lower, rows[0], rows[1])
    there = jnp.where(lower, below.astype(jnp.int32), above.astype(jnp.int32)) == 1
    columns = jnp.transpose(jnp.where(there, z, 0.0))

    own = coefs("own")
    p = [loc[i] for i in range(S * C)]
    for s in range(S):
        for k in range(K):
            w = splat(own, s * K + k)
            for c in range(C):
                p[s * C + c] = p[s * C + c] + w * phi[k * C + c]

    odd_y = lax.axis_index("gy") % 2 == 1
    odd_x = lax.axis_index("gx") % 2 == 1

    has_y, has_x = both_sides("gy"), both_sides("gx")

    def y_side(slab, face, coef):
        coef = jnp.where(even, coef, rolled(coef, -K // 2, 1))
        sums = []
        for s in range(S):
            mine = even if s < 2 else ~even
            part = [jnp.where(mine, face[(s % 2) * C + c], 0.0) for c in range(C)]
            for k in range(K // 2):
                w = splat(coef, s * K + k)
                for c in range(C):
                    part[c] = part[c] + w * slab[S * C + k * C + c]
            sums += part
        return sums

    def x_side(face, coef):
        coef = staggered(coef, sub >> 1)
        sums = []
        for s in range(S):
            part = [jnp.where((sub >> 1) == s, face[c], 0.0) for c in range(C)]
            for k in range(K // 4):
                w = splat(coef, s * K + k)
                for c in range(C):
                    part[c] = part[c] + w * face[C + k * C + c]
            for x in part:
                x = x + rolled(x, 2, 0)
                sums.append(x + rolled(x, 4, 0))
        return sums

    ylo, yhi = coefs("ylo"), coefs("yhi")
    y_first = y_side(slabs[0], faces[0], jnp.where(odd_y, ylo, yhi))
    y_second = y_side(slabs[1], faces[1], jnp.where(odd_y, yhi, ylo))
    if two_x:
        xlo, xhi = coefs("xlo"), coefs("xhi")
        x_first = x_side(faces[2], jnp.where(odd_x, xlo, xhi))
        x_second = x_side(faces[3], jnp.where(odd_x, xhi, xlo))
    else:
        x_first = x_side(faces[2], coefs("x"))
        x_second = x_first

    for s in range(S):
        sides = []
        for c in range(C):
            i = s * C + c
            x = p[i]
            pre[i] = x
            zl = jnp.broadcast_to(columns[i * XY : (i + 1) * XY, 0:1], (8, 128))
            zh = jnp.broadcast_to(columns[i * XY : (i + 1) * XY, 4:5], (8, 128))
            y_low = jnp.where(odd_y, y_first[i], y_second[i])
            y_high = jnp.where(odd_y, y_second[i], y_first[i])
            x_low = jnp.where(odd_x, x_first[i], x_second[i])
            x_high = jnp.where(odd_x, x_second[i], x_first[i])
            y_low = jnp.where(has_y[0], y_low + rolled(y_low, -1, 0), 0.0)
            y_high = jnp.where(has_y[1], y_high + rolled(y_high, 1, 0), 0.0)
            x_low, x_high = jnp.where(has_x[0], x_low, 0.0), jnp.where(has_x[1], x_high, 0.0)
            sides = [
                jnp.where(sub < CY, x_low, rolled(x, CY, 0)),
                jnp.where(sub >= XY - CY, x_high, rolled(x, -CY, 0)),
                jnp.where(even, y_low, rolled(x, 1, 0)),
                jnp.where(even, rolled(x, -1, 0), y_high),
                jnp.where(lane == 0, zl, rolled(x, 1, 1)),
                jnp.where(lane == CZ - 1, zh, rolled(x, -1, 1)),
            ]
            a = sum(diagonal[c * C + d] * p[s * C + d] for d in range(C))
            for d, side in enumerate(sides):
                a = a - couple[d * C + c] * side
            image[i] = a

    rows = []
    for m in range(M):
        for s in range(S):
            rows.append(sum(basis[m, s * C + c] * image[s * C + c] for c in range(C)))
    for s in range(S):
        rows.append(sum(image[s * C + c] * image[s * C + c] for c in range(C)))
    rows += [jnp.zeros((8, 128), F32)] * 4
    sums = [row_sums(rows[g : g + 8]) for g in range(0, 32, 8)]
    sums = jnp.concatenate([gram[...]] + sums + [jnp.zeros((8, 128), F32)], 0)
    row = across(jnp.ones((8, 128), F32), sums)
    sent[...] = jnp.broadcast_to(row[None], (n // 8, 8, 128)).reshape(n, 128)


def tables():
    first = np.zeros((128, 128), np.float32)
    second = np.zeros((128, 128), np.float32)
    out = np.zeros((128, 128), np.float32)
    fixed = np.zeros((8, 128), np.float32)
    for s in range(S):
        for at, (m, n) in enumerate(PAIRS):
            first[BASE + 4 * m + s, 4 * at + s] = 1
            second[BASE + 4 * n + s, 4 * at + s] = 1
            fixed[2, 4 * at + s] = 1 if m == n else 2
        for m in range(M):
            lane = BASE + 4 * m + s
            first[lane, lane] = 1
            fixed[1, lane] = 1
            fixed[2, lane] = -2
        lane = BASE + 4 * M + s
        fixed[0, lane] = fixed[1, lane] = fixed[2, lane] = 1
        for i in range(M + 1):
            out[BASE + 4 * i + s, i] = 1
    lanes = np.arange(128)
    fold = (lanes[:, None] % 4 == lanes[None, :] % 4).astype(np.float32)
    return np.stack([first, second, out, fold]).astype(jnp.bfloat16), fixed


def finish_body(unknowns, got, image, basis, maps, fixed, krylov, hessenberg, flag):
    sub, lane = iota(0), iota(1)
    total = got[0:8, :]
    for b in range(1, got.shape[0] // 8):
        total = total + got[8 * b : 8 * b + 8, :]
    for shift in (4, 2, 1):
        total = total + rolled(total, shift, 0)
    h = total / unknowns

    terms = total * all_rows(fixed, 2)
    terms = terms * (times(h, maps[0]) + all_rows(fixed, 0)) * (times(h, maps[1]) + all_rows(fixed, 1))
    sums = times(jnp.where(sub < 4, terms, jnp.abs(terms)), maps[3])
    terms, size = all_rows(sums, 0), all_rows(sums, 4)
    square = jnp.maximum(terms, 0.0) / unknowns + epsilon
    scale, norm = lax.rsqrt(square), jnp.sqrt(square)
    flag[0] = jnp.max(jnp.where(terms < CANCEL * size, 1, 0))
    for s in range(S):
        w = [splat(h, BASE + 4 * m + s) for m in range(M)]
        f = splat(scale, s)
        for c in range(C):
            i = s * C + c
            krylov[i] = (image[i] - sum(w[m] * basis[m, i] for m in range(M))) * f
    values = jnp.where(lane >= BASE + 4 * M, norm, h)
    values = jnp.where((lane & 3) == sub, values, 0.0)
    hessenberg[...] = times(values, maps[2])[:S, : M + 1]


def pairs_of(axis):
    count = lax.axis_size(axis)
    rounds = [[(i, i + 1) for i in range(0, count, 2)]]
    if count > 2:
        rounds.append([(i, (i + 1) % count) for i in range(1, count, 2)])
    return [r + [(j, i) for i, j in r] for r in rounds]


def swap(axis, low_side, high_side):
    odd = lax.axis_index(axis) % 2 == 1
    rounds = pairs_of(axis)
    sides = [jnp.where(odd, low_side, high_side), jnp.where(odd, high_side, low_side)]
    return [lax.ppermute(x, axis, pairs) for x, pairs in zip(sides, rounds)]


def by_side(axis, got):
    at = lax.axis_index(axis)
    odd = at % 2 == 1
    first, second = got if len(got) == 2 else (got[0], got[0])
    low, high = jnp.where(odd, first, second), jnp.where(odd, second, first)
    none = jnp.zeros_like(first)
    return jnp.where(at > 0, low, none), jnp.where(at < lax.axis_size(axis) - 1, high, none)


def exchange(rows):
    return lax.all_to_all(rows[:, None], AXES, 0, 0, tiled=True).reshape(rows.shape)


def on_device(basis, inverse_rows, block_diag, couple, coarse_basis, coarse_factor):
    n = lax.axis_size("gx") * lax.axis_size("gy") * lax.axis_size("gz")
    unknowns = float(C * XY * CZ * n)
    two_x = lax.axis_size("gx") > 2
    vectors = basis.reshape(M, S * C, XY, CZ)
    phi = coarse_basis.reshape(K * C, XY, CZ)

    slab = S * C + K * C // 2
    vector, rounded, phi, *slabs = call(
        load_body,
        [
            kept(S * C, XY, CZ),
            kept(S * C, XY, CZ, dtype=jnp.bfloat16),
            kept(K * C, XY, CZ),
            kept(slab, XY, CZ),
            kept(slab, XY, CZ),
        ],
        (in_hbm(vectors), in_hbm(phi)),
        S * C * XY * CZ,
        in_specs=[HBM] * 2,
        scratch=[pltpu.SemaphoreType.DMA((2,))],
    )
    rounded = rounded.reshape(S, C, CX, CY, CZ)
    (rhs,) = call(rhs_body, [kept(n * GATHERED, 128)], (vector, phi), 2 * K * S * C * XY * CZ)
    got = exchange(rhs)
    swapped = [lax.ppermute(x, "gy", pairs) for x, pairs in zip(slabs, pairs_of("gy"))]

    always = lax.axis_index("gx") >= 0

    inverse = inverse_rows.reshape(C, XY, ROWS, CZ)

    def extend(swapped, rounded, phi, vectors, inverse):
        parts = [x[: S * C].reshape(S, C, CX, CY, CZ).astype(rounded.dtype) for x in swapped]
        y_low, y_high = by_side("gy", parts)
        extended = jnp.concatenate([y_low, rounded, y_high], axis=3)
        slabs = swap("gx", extended[:, :, :2], extended[:, :, -2:])
        mine = extended.reshape(S, C, CX * (CY + 4), CZ)
        width = (EXTENT - CX * (CY + 4)) // 2
        low, high = mine[:, :, : SIDE - width], mine[:, :, 2 * SIDE - width :]
        middle = mine[:, :, SIDE - width : 2 * SIDE - width]
        first = lax.axis_index("gx") == 0
        none = jnp.zeros((S, C, width, CZ), rounded.dtype)
        if not two_x:
            ending = jnp.where(
                first, jnp.concatenate([none, low], axis=2), jnp.concatenate([high, none], axis=2)
            )
            middle = jnp.concatenate([middle, ending], axis=2)
        middle = middle.reshape(S, -1, CZ)
        early = call(
            functools.partial(early_body, two_x),
            [kept(BASE, 128), kept(S * C, XY, CZ), kept(*inverse.shape, dtype=inverse.dtype)]
            + [kept(K * C // 4, 8, 128)] * (1 + two_x),
            (phi, in_hbm(vectors), in_hbm(inverse), middle),
            10**10,
            in_specs=[VMEM, HBM, HBM, VMEM],
            scratch=[pltpu.VMEM(vectors.shape, F32), pltpu.SemaphoreType.DMA((C + 1,))],
        )
        slabs, early = lax.optimization_barrier((slabs, early))
        if two_x:
            slabs = [x.reshape(S, C, width, CZ) for x in by_side("gx", slabs)]
            outer = jnp.concatenate([slabs[0], low, high, slabs[1]], axis=2)
        else:
            slab = slabs[0].reshape(S, C, width, CZ)
            outer = jnp.where(
                first, jnp.concatenate([high, slab], axis=2), jnp.concatenate([slab, low], axis=2)
            )
        return [outer.reshape(S, -1, CZ)] + list(early)

    def unused(swapped, rounded, phi, vectors, inverse):
        return [
            jnp.zeros((S, C * SIDE * (1 + two_x), CZ), rounded.dtype),
            jnp.zeros((BASE, 128), F32),
            jnp.zeros((S * C, XY, CZ), F32),
            jnp.zeros_like(inverse),
        ] + [jnp.zeros((K * C // 4, 8, 128), F32)] * (1 + two_x)

    columns, gram, part, inverse, *phi_faces = lax.cond(
        always, extend, unused, swapped, rounded, phi, vectors, inverse
    )
    half, quarter = S * C // 2, (K + S) * C // 4
    sends = [shape(half, 8, 128)] * 2 + [shape(quarter, 8, 128)] * (2 if two_x else 1)
    stride = (len(slots(two_x)) + 1) // 2 + 1
    shares, loc, *sends = call(
        functools.partial(local_body, two_x),
        [kept(n * stride, 128), shape(S * C, XY, CZ)] + sends,
        (inverse, columns, part, got, coarse_factor, *phi_faces),
        2 * S * C * XY * C * SIDE * CZ,
    )

    def trade(*sends):
        x_faces = [lax.ppermute(x, "gx", pairs) for x, pairs in zip(sends[2:], pairs_of("gx"))]
        return [lax.ppermute(x, "gy", pairs) for x, pairs in zip(sends, pairs_of("gy"))] + x_faces

    def untouched(*sends):
        return list(sends)

    coarse = exchange(shares)
    faces = lax.cond(always, trade, untouched, *sends)
    pre, image, sent = call(
        functools.partial(image_body, two_x),
        [kept(S * C, XY, CZ), kept(S * C, XY, CZ), kept(n, 128)],
        (
            loc,
            phi,
            block_diag.reshape(C * C, XY, CZ),
            couple.reshape(6 * C, XY, CZ),
            vectors,
            gram,
            coarse,
            got,
            *swapped,
            *faces,
        ),
        2 * S * C * XY * CZ * 40,
    )
    products = exchange(sent)
    maps, fixed = tables()
    krylov, hessenberg, flag = call(
        functools.partial(finish_body, unknowns),
        [shape(S * C, XY, CZ), shape(S, M + 1), pltpu.SMEM((1,), jnp.int32)],
        (products, image, vectors, jnp.asarray(maps), jnp.asarray(fixed)),
        2 * S * C * XY * CZ * 8,
        out_specs=[VMEM, VMEM, pl.BlockSpec(memory_space=pltpu.SMEM)],
    )

    def exact(image, vectors, krylov, hessenberg):
        h = hessenberg[:, :M]
        left = image.reshape(S, C, XY, CZ) - jnp.sum(
            h.T[:, :, None, None, None] * vectors.reshape(M, S, C, XY, CZ), axis=0
        )
        squares = jnp.zeros((1, 128), F32).at[0, :S].set(jnp.sum(left * left, axis=(1, 2, 3)))
        squares = jnp.sum(exchange(jnp.broadcast_to(squares, (n, 128))), axis=0)[:S]
        norm = jnp.sqrt(squares / unknowns + epsilon)
        return (
            (left / norm[:, None, None, None]).reshape(S * C, XY, CZ),
            jnp.concatenate([h, norm[:, None]], axis=1),
        )

    def as_is(image, vectors, krylov, hessenberg):
        return krylov, hessenberg

    krylov, hessenberg = lax.cond(
        flag[0] > 0, exact, as_is, image, vectors, krylov, hessenberg
    )
    krylov, pre = lax.optimization_barrier((krylov, pre))
    cells = (S, C, CX, CY, CZ)
    return krylov.reshape(cells), pre.reshape(cells), hessenberg


def solution(mesh):
    return jax.shard_map(
        on_device,
        mesh=mesh,
        in_specs=(
            P(None, None, None, "gx", "gy", "gz"),
            P(None, "gx", "gy", None, "gz"),
            P(None, None, "gx", "gy", "gz"),
            P(None, None, "gx", "gy", "gz"),
            P(None, None, "gx", "gy", "gz"),
            P(AXES, None),
        ),
        out_specs=(P(None, None, "gx", "gy", "gz"), P(None, None, "gx", "gy", "gz"), P()),
        check_vma=False,
    )
```

```python
import functools

import jax
import jax.numpy as jnp
import numpy as np
from jax import lax
from jax.experimental import pallas as pl
from jax.experimental.pallas import tpu as pltpu
from jax.sharding import PartitionSpec as P

C = 4
CX = 4
CY = 2
CZ = 128
S = 4
M = 6
K = 16
XY = CX * CY
GATHERED = 1 + K * C * XY // CZ
EXTENT = (CX + 4) * (CY + 4)
SIDE = EXTENT // 3
ROWS = C * EXTENT
AXES = ("gx", "gy", "gz")
PAIRS = [(m, n) for m in range(M) for n in range(m, M)]
BASE = 88
CANCEL = 1e-2

epsilon = 1e-06

VMEM = pl.BlockSpec(memory_space=pltpu.VMEM)
HBM = pl.BlockSpec(memory_space=pltpu.HBM)
F32 = jnp.float32


def call(body, outs, operands, flops, in_specs=None, out_specs=None, scratch=()):
    size = sum(int(np.prod(x.shape)) * x.dtype.itemsize for x in list(operands) + list(outs))
    return pl.pallas_call(
        body,
        out_shape=tuple(outs),
        in_specs=in_specs or [VMEM] * len(operands),
        out_specs=tuple(out_specs or [VMEM] * len(outs)),
        scratch_shapes=list(scratch),
        compiler_params=pltpu.CompilerParams(vmem_limit_bytes=24 * 1024 * 1024),
        cost_estimate=pl.CostEstimate(flops=flops, bytes_accessed=size, transcendentals=0),
    )(*operands)


def shape(*dims, dtype=F32):
    return jax.ShapeDtypeStruct(dims, dtype)


def kept(*dims, dtype=F32):
    return pltpu.VMEM(dims, dtype)


def in_hbm(x):
    return pltpu.with_memory_space_constraint(x, pltpu.HBM)


def iota(axis):
    return lax.broadcasted_iota(jnp.int32, (8, 128), axis)


def rolled(x, shift, axis):
    return pltpu.roll(x, shift % x.shape[axis], axis)


def row_sums(blocks):
    sub = iota(0)
    for bit in (4, 2, 1):
        low = (sub & bit) == 0
        half = len(blocks) // 2
        blocks = [
            jnp.where(
                low,
                blocks[i] + rolled(blocks[i], -bit, 0),
                blocks[i + half] + rolled(blocks[i + half], bit, 0),
            )
            for i in range(half)
        ]
    return blocks[0]


def thirds(x):
    parts = []
    for _ in range(3):
        parts.append(x.astype(jnp.bfloat16))
        x = x - parts[-1].astype(F32)
    return parts


def across(left, right):
    left = left.astype(jnp.bfloat16)
    return sum(
        lax.dot_general(left, part, (((1,), (1,)), ((), ())), preferred_element_type=F32)
        for part in thirds(right)
    )


def times(x, table):
    rows = jnp.concatenate([p.astype(F32) for p in thirds(x)] + [jnp.zeros((8, 128), F32)], 0)
    y = jnp.dot(rows.astype(jnp.bfloat16), table, preferred_element_type=F32)
    return y[:8] + y[8:16] + y[16:24]


def all_rows(x, t):
    return jnp.broadcast_to(x[t : t + 1, :], (8, 128))


def splat(x, lane):
    return jnp.broadcast_to(x[:, lane : lane + 1], (8, 128))


def ends():
    sub, lane = iota(0), iota(1)
    pick = ((sub == 0) & (lane == 0)) | ((sub == 1) & (lane == CZ - 1))
    return jnp.where(pick, 1.0, 0.0).astype(F32)


def both_sides(axis):
    at = lax.axis_index(axis)
    return at > 0, at < lax.axis_size(axis) - 1


def place():
    x, y, z = (lax.axis_index(a) for a in AXES)
    ny, nz = lax.axis_size("gy"), lax.axis_size("gz")
    return (x * ny + y) * nz + z, z > 0, z < nz - 1


def y_faces(first, second):
    even = (iota(0) & 1) == 0
    low = jnp.where(even, first, rolled(second, 1, 0))
    high = jnp.where(even, rolled(first, -1, 0), second)
    return low, high


def load_body(basis, phi, vector, rounded, phi_kept, to_first, to_second, sems):
    copies = [
        pltpu.make_async_copy(basis.at[M - 1], vector, sems.at[0]),
        pltpu.make_async_copy(phi, phi_kept, sems.at[1]),
    ]
    for copy in copies:
        copy.start()
    odd = lax.axis_index("gy") % 2 == 1
    copies[0].wait()
    low = vector[...].astype(jnp.bfloat16)
    rounded[...] = low
    to_first[: S * C] = low.astype(F32)
    to_second[: S * C] = low.astype(F32)
    copies[1].wait()
    half = K * C // 2
    for i in range(half):
        low, high = y_faces(phi_kept[i], phi_kept[half + i])
        to_first[S * C + i] = jnp.where(odd, low, high)
        to_second[S * C + i] = jnp.where(odd, high, low)


def rhs_body(vector, phi, out):
    rows = []
    for s in range(S):
        v = [vector[s * C + c] for c in range(C)]
        prods = [sum(phi[k * C + c] * v[c] for c in range(C)) for k in range(K)]
        rows.append(row_sums(prods[:8]))
        rows.append(row_sums(prods[8:]))
    rows.append(jnp.zeros((64, 128), F32))
    rhs = across(jnp.ones((8, 128), F32), jnp.concatenate(rows, 0))
    faces = across(ends(), phi[...].reshape(K * C * XY, CZ))
    n = out.shape[0] // GATHERED
    me, _, _ = place()
    later = lax.broadcasted_iota(jnp.int32, (n, 128), 0) > me
    out[pl.ds(0, n, stride=GATHERED), :] = jnp.broadcast_to(rhs[0:1], (n, 128))
    for r in range(GATHERED - 1):
        row = faces[:, 128 * r : 128 * r + 128]
        out[pl.ds(r + 1, n, stride=GATHERED), :] = jnp.where(later, row[1:2], row[0:1])


def x_faces(blocks, sends, at):
    odd = lax.axis_index("gx") % 2 == 1
    group = iota(0) >> 1
    count = len(blocks) // 4
    for i in range(count):
        low = high = None
        for g in range(4):
            x = blocks[g * count + i]
            to_low, to_high = rolled(x, 2 * g, 0), rolled(x, 2 * g - 6, 0)
            low = to_low if low is None else jnp.where(group == g, to_low, low)
            high = to_high if high is None else jnp.where(group == g, to_high, high)
        sends[0][at + i] = jnp.where(odd, low, high)
        if len(sends) > 1:
            sends[1][at + i] = jnp.where(odd, high, low)


def solve(inv, cols, starts, done, ready=None, unroll=False):
    def one(c, carry):
        if ready is not None:
            ready(c)
        total = [[jnp.zeros((8, 128), F32) for _ in range(XY)] for _ in range(S)]
        for at, j in starts:
            seen = [cols[s, j : j + SIDE, :].astype(F32) for s in range(S)]
            for i in range(XY):
                w = inv[c, i, pl.ds(at, SIDE), :].astype(F32)
                for s in range(S):
                    part = w * seen[s]
                    total[s][i] = total[s][i] + part[:8] + part[8:]
        for s in range(S):
            done(s * C + c, row_sums(total[s]))
        return carry

    if unroll:
        for c in range(C):
            one(c, 0)
    else:
        lax.fori_loop(0, C, one, 0)


def edge(first):
    return pl.multiple_of(jnp.where(first, 0, 2 * SIDE), SIDE)


def early_body(two_x, phi, basis, inv, cols, gram, loc, inv_kept, *refs):
    phi_faces, (vectors, sems) = refs[: 1 + two_x], refs[1 + two_x :]
    fetch = pltpu.make_async_copy(basis, vectors, sems.at[C])
    fetch.start()

    def copy(c):
        return pltpu.make_async_copy(inv.at[c], inv_kept.at[c], sems.at[c])

    for c in range(C):
        copy(c).start()
    x_faces([phi[i] for i in range(K * C)], phi_faces, 0)

    def done(i, x):
        loc[i] = x

    if two_x:
        starts = [(EXTENT * c + SIDE, SIDE * c) for c in range(C)]
    else:
        at = edge(lax.axis_index("gx") == 0)
        starts = [(EXTENT * c + SIDE, 2 * SIDE * c) for c in range(C)]
        starts += [(EXTENT * c + at, 2 * SIDE * c + SIDE) for c in range(C)]
    solve(inv_kept, cols, starts, done, lambda c: copy(c).wait())
    fetch.wait()
    rows = []
    for m, n in PAIRS:
        for s in range(S):
            rows.append(sum(vectors[m, s * C + c] * vectors[n, s * C + c] for c in range(C)))
    rows += [jnp.zeros((8, 128), F32)] * (BASE - len(rows))
    for g in range(0, BASE, 8):
        gram[g : g + 8, :] = row_sums(rows[g : g + 8])


def slots(two_x):
    return ["own", "ylo", "yhi"] + (["xlo", "xhi"] if two_x else ["x"]) + ["zlo", "zhi"]


def factor_body(two_x, got, factor, out):
    n = factor.shape[1] // K
    stride = out.shape[0] // n
    sub, lane = iota(0), iota(1)
    mine = [(lane >> 4) == ((sub + s) & 7) for s in range(S)]
    columns = []
    for b in range(n // 8):
        rows = factor[:, 128 * b : 128 * b + 128]
        columns.append([rows] + [rolled(rows, K * s, 1) for s in range(1, S)])
    image = [jnp.zeros((K, 128), F32) for _ in range(S)]
    for b in range(n // 8):
        rhs = got[pl.ds(8 * GATHERED * b, 8, stride=GATHERED), :]
        rhs = pltpu.roll(rhs, 0, 1, stride=K, stride_axis=0)
        for s in range(S):
            row = jnp.sum(jnp.where(mine[s], rhs, 0.0), axis=0, keepdims=True)
            image[s] = image[s] + columns[b][s] * row
    image = [jnp.sum(x, axis=1, keepdims=True) for x in image]
    shares = []
    for b in range(n // 8):
        block = jnp.zeros((8, 128), F32)
        for s in range(S):
            row = jnp.sum(columns[b][s] * image[s], axis=0, keepdims=True)
            block = jnp.where(mine[s], row, block)
        for bit in (1, 2, 4):
            block = jnp.where((sub & bit) == 0, block, rolled(block, -K * bit, 1))
        shares.append(jnp.where(lane < S * K, block, 0.0))
    shares = jnp.concatenate(shares, 0)
    nz = lax.axis_size("gz")
    plane = lax.axis_size("gy") * nz
    shift = {"own": 0, "ylo": nz, "yhi": -nz, "x": plane, "xlo": plane, "xhi": -plane, "zlo": 1, "zhi": -1}
    names = slots(two_x)
    for t in range(0, len(names), 2):
        pair = [rolled(shares, shift[x], 0) if shift[x] else shares for x in names[t : t + 2]]
        row = pair[0] if len(pair) == 1 else pair[0] + rolled(pair[1], 64, 1)
        out[pl.ds(t // 2, n, stride=stride), :] = row
    face = (len(names) + 1) // 2
    for t in range(face, stride):
        out[pl.ds(t, n, stride=stride), :] = jnp.zeros((n, 128), F32)


def send_ends(two_x, locz, out):
    face = (len(slots(two_x)) + 1) // 2
    stride = face + 1
    me, below, above = place()

    @pl.when(below)
    def _():
        out[pl.ds((me - 1) * stride + face, 1), :] = locz[0:1]

    @pl.when(above)
    def _():
        out[pl.ds((me + 1) * stride + face, 1), :] = locz[1:2]


def local_body(two_x, inv, cols, early, got, factor, *refs):
    phi_faces, (out, loc, *sends) = refs[: 1 + two_x], refs[1 + two_x :]

    def done(i, x):
        loc[i] = early[i] + x

    if two_x:
        starts = [(EXTENT * c, 2 * SIDE * c) for c in range(C)]
        starts += [(EXTENT * c + 2 * SIDE, 2 * SIDE * c + SIDE) for c in range(C)]
    else:
        at = edge(lax.axis_index("gx") == 1)
        starts = [(EXTENT * c + at, SIDE * c) for c in range(C)]
    solve(inv, cols, starts, done, unroll=True)
    factor_body(two_x, got, factor, out)
    send_ends(two_x, across(ends(), loc[...].reshape(S * C * XY, CZ)), out)
    odd_y = lax.axis_index("gy") % 2 == 1
    for i in range(S * C // 2):
        low, high = y_faces(loc[i], loc[S * C // 2 + i])
        sends[0][i] = jnp.where(odd_y, low, high)
        sends[1][i] = jnp.where(odd_y, high, low)
    x_faces([loc[i] for i in range(S * C)], sends[2:], 0)
    for x, known in zip(sends[2:], phi_faces):
        x[C:] = known[...]


def staggered(coef, group):
    out = coef
    for g in range(1, 4):
        out = jnp.where(group == g, rolled(coef, -4 * g, 1), out)
    return out


def image_body(two_x, loc, phi, diagonal, couple, basis, gram, coarse, got, *rest):
    slabs, faces, (pre, image, sent) = rest[:2], rest[2:-3], rest[-3:]
    n = sent.shape[0]
    stride = coarse.shape[0] // n
    sub, lane = iota(0), iota(1)
    even = (sub & 1) == 0
    if stride == 4:
        total = coarse[0:8, :]
        for b in range(1, coarse.shape[0] // 8):
            total = total + coarse[8 * b : 8 * b + 8, :]
        total = total + rolled(total, 4, 0)
        totals = [all_rows(total, t) for t in range(stride - 1)]
    else:
        totals = [
            jnp.broadcast_to(
                jnp.sum(coarse[pl.ds(t, n, stride=stride), :], axis=0, keepdims=True), (8, 128)
            )
            for t in range(stride - 1)
        ]
    names = slots(two_x)

    def coefs(name):
        at = names.index(name)
        return totals[at // 2] if at % 2 == 0 else rolled(totals[at // 2], 64, 1)

    me, below, above = place()

    lower = sub < 4
    at = [jnp.where(below, me - 1, me), jnp.where(above, me + 1, me)]
    parts = None
    for r in range(8):
        row = got[pl.ds(at[r // 4] * GATHERED + 1 + r % 4, 1), :]
        row = jnp.broadcast_to(row, (8, 128))
        parts = row if r == 0 else jnp.where(sub == r, row, parts)
    coef = staggered(jnp.where(lower, coefs("zlo"), coefs("zhi")), sub & 3)
    z = None
    for s in range(S):
        w = splat(coef, s * K)
        for k in range(1, 4):
            w = jnp.where((lane >> 5) == k, splat(coef, s * K + k), w)
        part = parts * w
        for shift in (32, 64):
            part = part + rolled(part, shift, 1)
        z = part if z is None else jnp.where((lane >> 5) == s, part, z)
    for shift in (1, 2):
        z = z + rolled(z, -shift, 0)
    rows = [coarse[pl.ds(x * stride + stride - 1, 1), :] for x in at]
    rows = [jnp.broadcast_to(x, (8, 128)) for x in rows]
    z = z + jnp.where(lower, rows[0], rows[1])
    there = jnp.where(lower, below.astype(jnp.int32), above.astype(jnp.int32)) == 1
    columns = jnp.transpose(jnp.where(there, z, 0.0))

    odd_y = lax.axis_index("gy") % 2 == 1
    odd_x = lax.axis_index("gx") % 2 == 1

    has_y, has_x = both_sides("gy"), both_sides("gx")

    def y_side(slab, face, coef):
        coef = jnp.where(even, coef, rolled(coef, -K // 2, 1))
        sums = []
        for s in range(S):
            mine = even if s < 2 else ~even
            part = [jnp.where(mine, face[(s % 2) * C + c], 0.0) for c in range(C)]
            for k in range(K // 2):
                w = splat(coef, s * K + k)
                for c in range(C):
                    part[c] = part[c] + w * slab[S * C + k * C + c]
            sums += part
        return sums

    def x_side(face, coef):
        coef = staggered(coef, sub >> 1)
        sums = []
        for s in range(S):
            part = [jnp.where((sub >> 1) == s, face[c], 0.0) for c in range(C)]
            for k in range(K // 4):
                w = splat(coef, s * K + k)
                for c in range(C):
                    part[c] = part[c] + w * face[C + k * C + c]
            for x in part:
                x = x + rolled(x, 2, 0)
                sums.append(x + rolled(x, 4, 0))
        return sums

    ylo, yhi = coefs("ylo"), coefs("yhi")
    y_first = y_side(slabs[0], faces[0], jnp.where(odd_y, ylo, yhi))
    y_second = y_side(slabs[1], faces[1], jnp.where(odd_y, yhi, ylo))
    if two_x:
        xlo, xhi = coefs("xlo"), coefs("xhi")
        x_first = x_side(faces[2], jnp.where(odd_x, xlo, xhi))
        x_second = x_side(faces[3], jnp.where(odd_x, xhi, xlo))
    else:
        x_first = x_side(faces[2], coefs("x"))
        x_second = x_first

    own = coefs("own")
    p = [loc[i] for i in range(S * C)]
    for s in range(S):
        for k in range(K):
            w = splat(own, s * K + k)
            for c in range(C):
                p[s * C + c] = p[s * C + c] + w * phi[k * C + c]

    for s in range(S):
        sides = []
        for c in range(C):
            i = s * C + c
            x = p[i]
            pre[i] = x
            zl = jnp.broadcast_to(columns[i * XY : (i + 1) * XY, 0:1], (8, 128))
            zh = jnp.broadcast_to(columns[i * XY : (i + 1) * XY, 4:5], (8, 128))
            y_low = jnp.where(odd_y, y_first[i], y_second[i])
            y_high = jnp.where(odd_y, y_second[i], y_first[i])
            x_low = jnp.where(odd_x, x_first[i], x_second[i])
            x_high = jnp.where(odd_x, x_second[i], x_first[i])
            y_low = jnp.where(has_y[0], y_low + rolled(y_low, -1, 0), 0.0)
            y_high = jnp.where(has_y[1], y_high + rolled(y_high, 1, 0), 0.0)
            x_low, x_high = jnp.where(has_x[0], x_low, 0.0), jnp.where(has_x[1], x_high, 0.0)
            sides = [
                jnp.where(sub < CY, x_low, rolled(x, CY, 0)),
                jnp.where(sub >= XY - CY, x_high, rolled(x, -CY, 0)),
                jnp.where(even, y_low, rolled(x, 1, 0)),
                jnp.where(even, rolled(x, -1, 0), y_high),
                jnp.where(lane == 0, zl, rolled(x, 1, 1)),
                jnp.where(lane == CZ - 1, zh, rolled(x, -1, 1)),
            ]
            a = sum(diagonal[c * C + d] * p[s * C + d] for d in range(C))
            for d, side in enumerate(sides):
                a = a - couple[d * C + c] * side
            image[i] = a

    rows = []
    for m in range(M):
        for s in range(S):
            rows.append(sum(basis[m, s * C + c] * image[s * C + c] for c in range(C)))
    for s in range(S):
        rows.append(sum(image[s * C + c] * image[s * C + c] for c in range(C)))
    rows += [jnp.zeros((8, 128), F32)] * 4
    sums = [row_sums(rows[g : g + 8]) for g in range(0, 32, 8)]
    sums = jnp.concatenate([gram[...]] + sums + [jnp.zeros((8, 128), F32)], 0)
    row = across(jnp.ones((8, 128), F32), sums)
    sent[...] = jnp.broadcast_to(row[None], (n // 8, 8, 128)).reshape(n, 128)


def tables():
    first = np.zeros((128, 128), np.float32)
    second = np.zeros((128, 128), np.float32)
    out = np.zeros((128, 128), np.float32)
    fixed = np.zeros((8, 128), np.float32)
    for s in range(S):
        for at, (m, n) in enumerate(PAIRS):
            first[BASE + 4 * m + s, 4 * at + s] = 1
            second[BASE + 4 * n + s, 4 * at + s] = 1
            fixed[2, 4 * at + s] = 1 if m == n else 2
        for m in range(M):
            lane = BASE + 4 * m + s
            first[lane, lane] = 1
            fixed[1, lane] = 1
            fixed[2, lane] = -2
        lane = BASE + 4 * M + s
        fixed[0, lane] = fixed[1, lane] = fixed[2, lane] = 1
        for i in range(M + 1):
            out[BASE + 4 * i + s, i] = 1
    lanes = np.arange(128)
    fold = (lanes[:, None] % 4 == lanes[None, :] % 4).astype(np.float32)
    return np.stack([first, second, out, fold]).astype(jnp.bfloat16), fixed


def finish_body(unknowns, got, image, basis, maps, fixed, krylov, hessenberg, flag):
    sub, lane = iota(0), iota(1)
    total = got[0:8, :]
    for b in range(1, got.shape[0] // 8):
        total = total + got[8 * b : 8 * b + 8, :]
    for shift in (4, 2, 1):
        total = total + rolled(total, shift, 0)
    h = total / unknowns

    terms = total * all_rows(fixed, 2)
    terms = terms * (times(h, maps[0]) + all_rows(fixed, 0)) * (times(h, maps[1]) + all_rows(fixed, 1))
    sums = times(jnp.where(sub < 4, terms, jnp.abs(terms)), maps[3])
    terms, size = all_rows(sums, 0), all_rows(sums, 4)
    square = jnp.maximum(terms, 0.0) / unknowns + epsilon
    scale, norm = lax.rsqrt(square), jnp.sqrt(square)
    flag[0] = jnp.max(jnp.where(terms < CANCEL * size, 1, 0))
    for s in range(S):
        w = [splat(h, BASE + 4 * m + s) for m in range(M)]
        f = splat(scale, s)
        for c in range(C):
            i = s * C + c
            krylov[i] = (image[i] - sum(w[m] * basis[m, i] for m in range(M))) * f
    values = jnp.where(lane >= BASE + 4 * M, norm, h)
    values = jnp.where((lane & 3) == sub, values, 0.0)
    hessenberg[...] = times(values, maps[2])[:S, : M + 1]


def pairs_of(axis):
    count = lax.axis_size(axis)
    rounds = [[(i, i + 1) for i in range(0, count, 2)]]
    if count > 2:
        rounds.append([(i, (i + 1) % count) for i in range(1, count, 2)])
    return [r + [(j, i) for i, j in r] for r in rounds]


def swap(axis, low_side, high_side):
    odd = lax.axis_index(axis) % 2 == 1
    rounds = pairs_of(axis)
    sides = [jnp.where(odd, low_side, high_side), jnp.where(odd, high_side, low_side)]
    return [lax.ppermute(x, axis, pairs) for x, pairs in zip(sides, rounds)]


def by_side(axis, got):
    at = lax.axis_index(axis)
    odd = at % 2 == 1
    first, second = got if len(got) == 2 else (got[0], got[0])
    low, high = jnp.where(odd, first, second), jnp.where(odd, second, first)
    none = jnp.zeros_like(first)
    return jnp.where(at > 0, low, none), jnp.where(at < lax.axis_size(axis) - 1, high, none)


def exchange(rows):
    return lax.all_to_all(rows[:, None], AXES, 0, 0, tiled=True).reshape(rows.shape)


def on_device(basis, inverse_rows, block_diag, couple, coarse_basis, coarse_factor):
    n = lax.axis_size("gx") * lax.axis_size("gy") * lax.axis_size("gz")
    unknowns = float(C * XY * CZ * n)
    two_x = lax.axis_size("gx") > 2
    vectors = basis.reshape(M, S * C, XY, CZ)
    phi = coarse_basis.reshape(K * C, XY, CZ)

    slab = S * C + K * C // 2
    vector, rounded, phi, *slabs = call(
        load_body,
        [
            kept(S * C, XY, CZ),
            kept(S * C, XY, CZ, dtype=jnp.bfloat16),
            kept(K * C, XY, CZ),
            kept(slab, XY, CZ),
            kept(slab, XY, CZ),
        ],
        (in_hbm(vectors), in_hbm(phi)),
        S * C * XY * CZ,
        in_specs=[HBM] * 2,
        scratch=[pltpu.SemaphoreType.DMA((2,))],
    )
    rounded = rounded.reshape(S, C, CX, CY, CZ)
    (rhs,) = call(rhs_body, [kept(n * GATHERED, 128)], (vector, phi), 2 * K * S * C * XY * CZ)
    got = exchange(rhs)
    swapped = [lax.ppermute(x, "gy", pairs) for x, pairs in zip(slabs, pairs_of("gy"))]

    always = lax.axis_index("gx") >= 0

    inverse = inverse_rows.reshape(C, XY, ROWS, CZ)

    def extend(swapped, rounded, phi, vectors, inverse):
        parts = [x[: S * C].reshape(S, C, CX, CY, CZ).astype(rounded.dtype) for x in swapped]
        y_low, y_high = by_side("gy", parts)
        extended = jnp.concatenate([y_low, rounded, y_high], axis=3)
        slabs = swap("gx", extended[:, :, :2], extended[:, :, -2:])
        mine = extended.reshape(S, C, CX * (CY + 4), CZ)
        width = (EXTENT - CX * (CY + 4)) // 2
        low, high = mine[:, :, : SIDE - width], mine[:, :, 2 * SIDE - width :]
        middle = mine[:, :, SIDE - width : 2 * SIDE - width]
        first = lax.axis_index("gx") == 0
        none = jnp.zeros((S, C, width, CZ), rounded.dtype)
        if not two_x:
            ending = jnp.where(
                first, jnp.concatenate([none, low], axis=2), jnp.concatenate([high, none], axis=2)
            )
            middle = jnp.concatenate([middle, ending], axis=2)
        middle = middle.reshape(S, -1, CZ)
        early = call(
            functools.partial(early_body, two_x),
            [kept(BASE, 128), kept(S * C, XY, CZ), kept(*inverse.shape, dtype=inverse.dtype)]
            + [kept(K * C // 4, 8, 128)] * (1 + two_x),
            (phi, in_hbm(vectors), in_hbm(inverse), middle),
            10**10,
            in_specs=[VMEM, HBM, HBM, VMEM],
            scratch=[pltpu.VMEM(vectors.shape, F32), pltpu.SemaphoreType.DMA((C + 1,))],
        )
        slabs, early = lax.optimization_barrier((slabs, early))
        if two_x:
            slabs = [x.reshape(S, C, width, CZ) for x in by_side("gx", slabs)]
            outer = jnp.concatenate([slabs[0], low, high, slabs[1]], axis=2)
        else:
            slab = slabs[0].reshape(S, C, width, CZ)
            outer = jnp.where(
                first, jnp.concatenate([high, slab], axis=2), jnp.concatenate([slab, low], axis=2)
            )
        return [outer.reshape(S, -1, CZ)] + list(early)

    def unused(swapped, rounded, phi, vectors, inverse):
        return [
            jnp.zeros((S, C * SIDE * (1 + two_x), CZ), rounded.dtype),
            jnp.zeros((BASE, 128), F32),
            jnp.zeros((S * C, XY, CZ), F32),
            jnp.zeros_like(inverse),
        ] + [jnp.zeros((K * C // 4, 8, 128), F32)] * (1 + two_x)

    columns, gram, part, inverse, *phi_faces = lax.cond(
        always, extend, unused, swapped, rounded, phi, vectors, inverse
    )
    half, quarter = S * C // 2, (K + S) * C // 4
    sends = [shape(half, 8, 128)] * 2 + [shape(quarter, 8, 128)] * (2 if two_x else 1)
    stride = (len(slots(two_x)) + 1) // 2 + 1
    shares, loc, *sends = call(
        functools.partial(local_body, two_x),
        [kept(n * stride, 128), shape(S * C, XY, CZ)] + sends,
        (inverse, columns, part, got, coarse_factor, *phi_faces),
        2 * S * C * XY * C * SIDE * CZ,
    )

    def trade(*sends):
        x_faces = [lax.ppermute(x, "gx", pairs) for x, pairs in zip(sends[2:], pairs_of("gx"))]
        return [lax.ppermute(x, "gy", pairs) for x, pairs in zip(sends, pairs_of("gy"))] + x_faces

    def untouched(*sends):
        return list(sends)

    coarse = exchange(shares)
    faces = lax.cond(always, trade, untouched, *sends)
    pre, image, sent = call(
        functools.partial(image_body, two_x),
        [kept(S * C, XY, CZ), kept(S * C, XY, CZ), kept(n, 128)],
        (
            loc,
            phi,
            block_diag.reshape(C * C, XY, CZ),
            couple.reshape(6 * C, XY, CZ),
            vectors,
            gram,
            coarse,
            got,
            *swapped,
            *faces,
        ),
        2 * S * C * XY * CZ * 40,
    )
    products = exchange(sent)
    maps, fixed = tables()
    krylov, hessenberg, flag = call(
        functools.partial(finish_body, unknowns),
        [shape(S * C, XY, CZ), shape(S, M + 1), pltpu.SMEM((1,), jnp.int32)],
        (products, image, vectors, jnp.asarray(maps), jnp.asarray(fixed)),
        2 * S * C * XY * CZ * 8,
        out_specs=[VMEM, VMEM, pl.BlockSpec(memory_space=pltpu.SMEM)],
    )

    def exact(image, vectors, krylov, hessenberg):
        h = hessenberg[:, :M]
        left = image.reshape(S, C, XY, CZ) - jnp.sum(
            h.T[:, :, None, None, None] * vectors.reshape(M, S, C, XY, CZ), axis=0
        )
        squares = jnp.zeros((1, 128), F32).at[0, :S].set(jnp.sum(left * left, axis=(1, 2, 3)))
        squares = jnp.sum(exchange(jnp.broadcast_to(squares, (n, 128))), axis=0)[:S]
        norm = jnp.sqrt(squares / unknowns + epsilon)
        return (
            (left / norm[:, None, None, None]).reshape(S * C, XY, CZ),
            jnp.concatenate([h, norm[:, None]], axis=1),
        )

    def as_is(image, vectors, krylov, hessenberg):
        return krylov, hessenberg

    krylov, hessenberg = lax.cond(
        flag[0] > 0, exact, as_is, image, vectors, krylov, hessenberg
    )
    krylov, pre = lax.optimization_barrier((krylov, pre))
    cells = (S, C, CX, CY, CZ)
    return krylov.reshape(cells), pre.reshape(cells), hessenberg


def solution(mesh):
    return jax.shard_map(
        on_device,
        mesh=mesh,
        in_specs=(
            P(None, None, None, "gx", "gy", "gz"),
            P(None, "gx", "gy", None, "gz"),
            P(None, None, "gx", "gy", "gz"),
            P(None, None, "gx", "gy", "gz"),
            P(None, None, "gx", "gy", "gz"),
            P(AXES, None),
        ),
        out_specs=(P(None, None, "gx", "gy", "gz"), P(None, None, "gx", "gy", "gz"), P()),
        check_vma=False,
    )
```

```python
import functools

import jax
import jax.numpy as jnp
import numpy as np
from jax import lax
from jax.experimental import pallas as pl
from jax.experimental.pallas import tpu as pltpu
from jax.sharding import PartitionSpec as P

C = 4
CX = 4
CY = 2
CZ = 128
S = 4
M = 6
K = 16
XY = CX * CY
GATHERED = 1 + K * C * XY // CZ
EXTENT = (CX + 4) * (CY + 4)
SIDE = EXTENT // 3
ROWS = C * EXTENT
AXES = ("gx", "gy", "gz")
PAIRS = [(m, n) for m in range(M) for n in range(m, M)]
BASE = 88
CANCEL = 1e-2

epsilon = 1e-06

VMEM = pl.BlockSpec(memory_space=pltpu.VMEM)
HBM = pl.BlockSpec(memory_space=pltpu.HBM)
F32 = jnp.float32


def call(body, outs, operands, flops, in_specs=None, out_specs=None, scratch=()):
    size = sum(int(np.prod(x.shape)) * x.dtype.itemsize for x in list(operands) + list(outs))
    return pl.pallas_call(
        body,
        out_shape=tuple(outs),
        in_specs=in_specs or [VMEM] * len(operands),
        out_specs=tuple(out_specs or [VMEM] * len(outs)),
        scratch_shapes=list(scratch),
        compiler_params=pltpu.CompilerParams(vmem_limit_bytes=24 * 1024 * 1024),
        cost_estimate=pl.CostEstimate(flops=flops, bytes_accessed=size, transcendentals=0),
    )(*operands)


def shape(*dims, dtype=F32):
    return jax.ShapeDtypeStruct(dims, dtype)


def kept(*dims, dtype=F32):
    return pltpu.VMEM(dims, dtype)


def in_hbm(x):
    return pltpu.with_memory_space_constraint(x, pltpu.HBM)


def iota(axis):
    return lax.broadcasted_iota(jnp.int32, (8, 128), axis)


def rolled(x, shift, axis):
    return pltpu.roll(x, shift % x.shape[axis], axis)


def row_sums(blocks):
    sub = iota(0)
    for bit in (4, 2, 1):
        low = (sub & bit) == 0
        half = len(blocks) // 2
        blocks = [
            jnp.where(
                low,
                blocks[i] + rolled(blocks[i], -bit, 0),
                blocks[i + half] + rolled(blocks[i + half], bit, 0),
            )
            for i in range(half)
        ]
    return blocks[0]


def thirds(x):
    parts = []
    for _ in range(3):
        parts.append(x.astype(jnp.bfloat16))
        x = x - parts[-1].astype(F32)
    return parts


def across(left, right):
    left = left.astype(jnp.bfloat16)
    return sum(
        lax.dot_general(left, part, (((1,), (1,)), ((), ())), preferred_element_type=F32)
        for part in thirds(right)
    )


def times(x, table):
    rows = jnp.concatenate([p.astype(F32) for p in thirds(x)] + [jnp.zeros((8, 128), F32)], 0)
    y = jnp.dot(rows.astype(jnp.bfloat16), table, preferred_element_type=F32)
    return y[:8] + y[8:16] + y[16:24]


def all_rows(x, t):
    return jnp.broadcast_to(x[t : t + 1, :], (8, 128))


def splat(x, lane):
    return jnp.broadcast_to(x[:, lane : lane + 1], (8, 128))


def ends():
    sub, lane = iota(0), iota(1)
    pick = ((sub == 0) & (lane == 0)) | ((sub == 1) & (lane == CZ - 1))
    return jnp.where(pick, 1.0, 0.0).astype(F32)


def both_sides(axis):
    at = lax.axis_index(axis)
    return at > 0, at < lax.axis_size(axis) - 1


def place():
    x, y, z = (lax.axis_index(a) for a in AXES)
    ny, nz = lax.axis_size("gy"), lax.axis_size("gz")
    return (x * ny + y) * nz + z, z > 0, z < nz - 1


def y_faces(first, second):
    even = (iota(0) & 1) == 0
    low = jnp.where(even, first, rolled(second, 1, 0))
    high = jnp.where(even, rolled(first, -1, 0), second)
    return low, high


def load_body(basis, phi, vector, rounded, phi_kept, to_first, to_second, sems):
    copies = [
        pltpu.make_async_copy(basis.at[M - 1], vector, sems.at[0]),
        pltpu.make_async_copy(phi, phi_kept, sems.at[1]),
    ]
    for copy in copies:
        copy.start()
    odd = lax.axis_index("gy") % 2 == 1
    copies[0].wait()
    low = vector[...].astype(jnp.bfloat16)
    rounded[...] = low
    to_first[: S * C] = low.astype(F32)
    to_second[: S * C] = low.astype(F32)
    copies[1].wait()
    half = K * C // 2
    for i in range(half):
        low, high = y_faces(phi_kept[i], phi_kept[half + i])
        to_first[S * C + i] = jnp.where(odd, low, high)
        to_second[S * C + i] = jnp.where(odd, high, low)


def rhs_body(vector, phi, out):
    faces = across(ends(), phi[...].reshape(K * C * XY, CZ))
    rows = []
    for s in range(S):
        v = [vector[s * C + c] for c in range(C)]
        prods = [sum(phi[k * C + c] * v[c] for c in range(C)) for k in range(K)]
        rows.append(row_sums(prods[:8]))
        rows.append(row_sums(prods[8:]))
    rows.append(jnp.zeros((64, 128), F32))
    rhs = across(jnp.ones((8, 128), F32), jnp.concatenate(rows, 0))
    n = out.shape[0] // GATHERED
    me, _, _ = place()
    later = lax.broadcasted_iota(jnp.int32, (n, 128), 0) > me
    out[pl.ds(0, n, stride=GATHERED), :] = jnp.broadcast_to(rhs[0:1], (n, 128))
    for r in range(GATHERED - 1):
        row = faces[:, 128 * r : 128 * r + 128]
        out[pl.ds(r + 1, n, stride=GATHERED), :] = jnp.where(later, row[1:2], row[0:1])


def x_faces(blocks, sends, at):
    odd = lax.axis_index("gx") % 2 == 1
    group = iota(0) >> 1
    count = len(blocks) // 4
    for i in range(count):
        low = high = None
        for g in range(4):
            x = blocks[g * count + i]
            to_low, to_high = rolled(x, 2 * g, 0), rolled(x, 2 * g - 6, 0)
            low = to_low if low is None else jnp.where(group == g, to_low, low)
            high = to_high if high is None else jnp.where(group == g, to_high, high)
        sends[0][at + i] = jnp.where(odd, low, high)
        if len(sends) > 1:
            sends[1][at + i] = jnp.where(odd, high, low)


def solve(inv, cols, starts, done, ready=None, unroll=False):
    def one(c, carry):
        if ready is not None:
            ready(c)
        total = [[jnp.zeros((8, 128), F32) for _ in range(XY)] for _ in range(S)]
        for at, j in starts:
            seen = [cols[s, j : j + SIDE, :].astype(F32) for s in range(S)]
            for i in range(XY):
                w = inv[c, i, pl.ds(at, SIDE), :].astype(F32)
                for s in range(S):
                    part = w * seen[s]
                    total[s][i] = total[s][i] + part[:8] + part[8:]
        for s in range(S):
            done(s * C + c, row_sums(total[s]))
        return carry

    if unroll:
        for c in range(C):
            one(c, 0)
    else:
        lax.fori_loop(0, C, one, 0)


def edge(first):
    return pl.multiple_of(jnp.where(first, 0, 2 * SIDE), SIDE)


def early_body(two_x, phi, basis, inv, cols, gram, loc, inv_kept, *refs):
    phi_faces, (vectors, sems) = refs[: 1 + two_x], refs[1 + two_x :]
    fetch = pltpu.make_async_copy(basis, vectors, sems.at[C])
    fetch.start()

    def copy(c):
        return pltpu.make_async_copy(inv.at[c], inv_kept.at[c], sems.at[c])

    for c in range(C):
        copy(c).start()
    x_faces([phi[i] for i in range(K * C)], phi_faces, 0)

    def done(i, x):
        loc[i] = x

    if two_x:
        starts = [(EXTENT * c + SIDE, SIDE * c) for c in range(C)]
    else:
        at = edge(lax.axis_index("gx") == 0)
        starts = [(EXTENT * c + SIDE, 2 * SIDE * c) for c in range(C)]
        starts += [(EXTENT * c + at, 2 * SIDE * c + SIDE) for c in range(C)]
    solve(inv_kept, cols, starts, done, lambda c: copy(c).wait())
    fetch.wait()
    rows = []
    for m, n in PAIRS:
        for s in range(S):
            rows.append(sum(vectors[m, s * C + c] * vectors[n, s * C + c] for c in range(C)))
    rows += [jnp.zeros((8, 128), F32)] * (BASE - len(rows))
    for g in range(0, BASE, 8):
        gram[g : g + 8, :] = row_sums(rows[g : g + 8])


def slots(two_x):
    return ["own", "ylo", "yhi"] + (["xlo", "xhi"] if two_x else ["x"]) + ["zlo", "zhi"]


def factor_body(two_x, got, factor, out):
    n = factor.shape[1] // K
    stride = out.shape[0] // n
    sub, lane = iota(0), iota(1)
    mine = [(lane >> 4) == ((sub + s) & 7) for s in range(S)]
    columns = []
    for b in range(n // 8):
        rows = factor[:, 128 * b : 128 * b + 128]
        columns.append([rows] + [rolled(rows, K * s, 1) for s in range(1, S)])
    image = [jnp.zeros((K, 128), F32) for _ in range(S)]
    for b in range(n // 8):
        rhs = got[pl.ds(8 * GATHERED * b, 8, stride=GATHERED), :]
        rhs = pltpu.roll(rhs, 0, 1, stride=K, stride_axis=0)
        for s in range(S):
            row = jnp.sum(jnp.where(mine[s], rhs, 0.0), axis=0, keepdims=True)
            image[s] = image[s] + columns[b][s] * row
    image = [jnp.sum(x, axis=1, keepdims=True) for x in image]
    shares = []
    for b in range(n // 8):
        block = jnp.zeros((8, 128), F32)
        for s in range(S):
            row = jnp.sum(columns[b][s] * image[s], axis=0, keepdims=True)
            block = jnp.where(mine[s], row, block)
        for bit in (1, 2, 4):
            block = jnp.where((sub & bit) == 0, block, rolled(block, -K * bit, 1))
        shares.append(jnp.where(lane < S * K, block, 0.0))
    shares = jnp.concatenate(shares, 0)
    nz = lax.axis_size("gz")
    plane = lax.axis_size("gy") * nz
    shift = {"own": 0, "ylo": nz, "yhi": -nz, "x": plane, "xlo": plane, "xhi": -plane, "zlo": 1, "zhi": -1}
    names = slots(two_x)
    for t in range(0, len(names), 2):
        pair = [rolled(shares, shift[x], 0) if shift[x] else shares for x in names[t : t + 2]]
        row = pair[0] if len(pair) == 1 else pair[0] + rolled(pair[1], 64, 1)
        out[pl.ds(t // 2, n, stride=stride), :] = row
    face = (len(names) + 1) // 2
    for t in range(face, stride):
        out[pl.ds(t, n, stride=stride), :] = jnp.zeros((n, 128), F32)


def send_ends(two_x, locz, out):
    face = (len(slots(two_x)) + 1) // 2
    stride = face + 1
    me, below, above = place()

    @pl.when(below)
    def _():
        out[pl.ds((me - 1) * stride + face, 1), :] = locz[0:1]

    @pl.when(above)
    def _():
        out[pl.ds((me + 1) * stride + face, 1), :] = locz[1:2]


def local_body(two_x, inv, cols, early, got, factor, *refs):
    phi_faces, (out, loc, *sends) = refs[: 1 + two_x], refs[1 + two_x :]

    def done(i, x):
        loc[i] = early[i] + x

    if two_x:
        starts = [(EXTENT * c, 2 * SIDE * c) for c in range(C)]
        starts += [(EXTENT * c + 2 * SIDE, 2 * SIDE * c + SIDE) for c in range(C)]
    else:
        at = edge(lax.axis_index("gx") == 1)
        starts = [(EXTENT * c + at, SIDE * c) for c in range(C)]
    solve(inv, cols, starts, done, unroll=True)
    factor_body(two_x, got, factor, out)
    send_ends(two_x, across(ends(), loc[...].reshape(S * C * XY, CZ)), out)
    odd_y = lax.axis_index("gy") % 2 == 1
    for i in range(S * C // 2):
        low, high = y_faces(loc[i], loc[S * C // 2 + i])
        sends[0][i] = jnp.where(odd_y, low, high)
        sends[1][i] = jnp.where(odd_y, high, low)
    x_faces([loc[i] for i in range(S * C)], sends[2:], 0)
    for x, known in zip(sends[2:], phi_faces):
        x[C:] = known[...]


def staggered(coef, group):
    out = coef
    for g in range(1, 4):
        out = jnp.where(group == g, rolled(coef, -4 * g, 1), out)
    return out


def image_body(two_x, loc, phi, diagonal, couple, basis, gram, coarse, got, *rest):
    slabs, faces, (pre, image, sent) = rest[:2], rest[2:-3], rest[-3:]
    n = sent.shape[0]
    stride = coarse.shape[0] // n
    sub, lane = iota(0), iota(1)
    even = (sub & 1) == 0
    if stride == 4:
        total = coarse[0:8, :]
        for b in range(1, coarse.shape[0] // 8):
            total = total + coarse[8 * b : 8 * b + 8, :]
        total = total + rolled(total, 4, 0)
        totals = [all_rows(total, t) for t in range(stride - 1)]
    else:
        totals = [
            jnp.broadcast_to(
                jnp.sum(coarse[pl.ds(t, n, stride=stride), :], axis=0, keepdims=True), (8, 128)
            )
            for t in range(stride - 1)
        ]
    names = slots(two_x)

    def coefs(name):
        at = names.index(name)
        return totals[at // 2] if at % 2 == 0 else rolled(totals[at // 2], 64, 1)

    me, below, above = place()

    lower = sub < 4
    at = [jnp.where(below, me - 1, me), jnp.where(above, me + 1, me)]
    parts = None
    for r in range(8):
        row = got[pl.ds(at[r // 4] * GATHERED + 1 + r % 4, 1), :]
        row = jnp.broadcast_to(row, (8, 128))
        parts = row if r == 0 else jnp.where(sub == r, row, parts)
    coef = staggered(jnp.where(lower, coefs("zlo"), coefs("zhi")), sub & 3)
    z = None
    for s in range(S):
        w = splat(coef, s * K)
        for k in range(1, 4):
            w = jnp.where((lane >> 5) == k, splat(coef, s * K + k), w)
        part = parts * w
        for shift in (32, 64):
            part = part + rolled(part, shift, 1)
        z = part if z is None else jnp.where((lane >> 5) == s, part, z)
    for shift in (1, 2):
        z = z + rolled(z, -shift, 0)
    rows = [coarse[pl.ds(x * stride + stride - 1, 1), :] for x in at]
    rows = [jnp.broadcast_to(x, (8, 128)) for x in rows]
    z = z + jnp.where(lower, rows[0], rows[1])
    there = jnp.where(lower, below.astype(jnp.int32), above.astype(jnp.int32)) == 1
    columns = jnp.transpose(jnp.where(there, z, 0.0))

    odd_y = lax.axis_index("gy") % 2 == 1
    odd_x = lax.axis_index("gx") % 2 == 1

    has_y, has_x = both_sides("gy"), both_sides("gx")

    def y_side(slab, face, coef):
        coef = jnp.where(even, coef, rolled(coef, -K // 2, 1))
        sums = []
        for s in range(S):
            mine = even if s < 2 else ~even
            part = [jnp.where(mine, face[(s % 2) * C + c], 0.0) for c in range(C)]
            for k in range(K // 2):
                w = splat(coef, s * K + k)
                for c in range(C):
                    part[c] = part[c] + w * slab[S * C + k * C + c]
            sums += part
        return sums

    def x_side(face, coef):
        coef = staggered(coef, sub >> 1)
        sums = []
        for s in range(S):
            part = [jnp.where((sub >> 1) == s, face[c], 0.0) for c in range(C)]
            for k in range(K // 4):
                w = splat(coef, s * K + k)
                for c in range(C):
                    part[c] = part[c] + w * face[C + k * C + c]
            for x in part:
                x = x + rolled(x, 2, 0)
                sums.append(x + rolled(x, 4, 0))
        return sums

    ylo, yhi = coefs("ylo"), coefs("yhi")
    y_first = y_side(slabs[0], faces[0], jnp.where(odd_y, ylo, yhi))
    y_second = y_side(slabs[1], faces[1], jnp.where(odd_y, yhi, ylo))
    if two_x:
        xlo, xhi = coefs("xlo"), coefs("xhi")
        x_first = x_side(faces[2], jnp.where(odd_x, xlo, xhi))
        x_second = x_side(faces[3], jnp.where(odd_x, xhi, xlo))
    else:
        x_first = x_side(faces[2], coefs("x"))
        x_second = x_first

    own = coefs("own")
    p = [loc[i] for i in range(S * C)]
    for s in range(S):
        for k in range(K):
            w = splat(own, s * K + k)
            for c in range(C):
                p[s * C + c] = p[s * C + c] + w * phi[k * C + c]

    for s in range(S):
        sides = []
        for c in range(C):
            i = s * C + c
            x = p[i]
            pre[i] = x
            zl = jnp.broadcast_to(columns[i * XY : (i + 1) * XY, 0:1], (8, 128))
            zh = jnp.broadcast_to(columns[i * XY : (i + 1) * XY, 4:5], (8, 128))
            y_low = jnp.where(odd_y, y_first[i], y_second[i])
            y_high = jnp.where(odd_y, y_second[i], y_first[i])
            x_low = jnp.where(odd_x, x_first[i], x_second[i])
            x_high = jnp.where(odd_x, x_second[i], x_first[i])
            y_low = jnp.where(has_y[0], y_low + rolled(y_low, -1, 0), 0.0)
            y_high = jnp.where(has_y[1], y_high + rolled(y_high, 1, 0), 0.0)
            x_low, x_high = jnp.where(has_x[0], x_low, 0.0), jnp.where(has_x[1], x_high, 0.0)
            sides = [
                jnp.where(sub < CY, x_low, rolled(x, CY, 0)),
                jnp.where(sub >= XY - CY, x_high, rolled(x, -CY, 0)),
                jnp.where(even, y_low, rolled(x, 1, 0)),
                jnp.where(even, rolled(x, -1, 0), y_high),
                jnp.where(lane == 0, zl, rolled(x, 1, 1)),
                jnp.where(lane == CZ - 1, zh, rolled(x, -1, 1)),
            ]
            a = sum(diagonal[c * C + d] * p[s * C + d] for d in range(C))
            for d, side in enumerate(sides):
                a = a - couple[d * C + c] * side
            image[i] = a

    rows = []
    for m in range(M):
        for s in range(S):
            rows.append(sum(basis[m, s * C + c] * image[s * C + c] for c in range(C)))
    for s in range(S):
        rows.append(sum(image[s * C + c] * image[s * C + c] for c in range(C)))
    rows += [jnp.zeros((8, 128), F32)] * 4
    sums = [row_sums(rows[g : g + 8]) for g in range(0, 32, 8)]
    sums = jnp.concatenate([gram[...]] + sums + [jnp.zeros((8, 128), F32)], 0)
    row = across(jnp.ones((8, 128), F32), sums)
    sent[...] = jnp.broadcast_to(row[None], (n // 8, 8, 128)).reshape(n, 128)


def tables():
    first = np.zeros((128, 128), np.float32)
    second = np.zeros((128, 128), np.float32)
    out = np.zeros((128, 128), np.float32)
    fixed = np.zeros((8, 128), np.float32)
    for s in range(S):
        for at, (m, n) in enumerate(PAIRS):
            first[BASE + 4 * m + s, 4 * at + s] = 1
            second[BASE + 4 * n + s, 4 * at + s] = 1
            fixed[2, 4 * at + s] = 1 if m == n else 2
        for m in range(M):
            lane = BASE + 4 * m + s
            first[lane, lane] = 1
            fixed[1, lane] = 1
            fixed[2, lane] = -2
        lane = BASE + 4 * M + s
        fixed[0, lane] = fixed[1, lane] = fixed[2, lane] = 1
        for i in range(M + 1):
            out[BASE + 4 * i + s, i] = 1
    lanes = np.arange(128)
    fold = (lanes[:, None] % 4 == lanes[None, :] % 4).astype(np.float32)
    return np.stack([first, second, out, fold]).astype(jnp.bfloat16), fixed


def finish_body(unknowns, got, image, basis, maps, fixed, krylov, hessenberg, flag):
    sub, lane = iota(0), iota(1)
    total = got[0:8, :]
    for b in range(1, got.shape[0] // 8):
        total = total + got[8 * b : 8 * b + 8, :]
    for shift in (4, 2, 1):
        total = total + rolled(total, shift, 0)
    h = total / unknowns

    terms = total * all_rows(fixed, 2)
    terms = terms * (times(h, maps[0]) + all_rows(fixed, 0)) * (times(h, maps[1]) + all_rows(fixed, 1))
    sums = times(jnp.where(sub < 4, terms, jnp.abs(terms)), maps[3])
    terms, size = all_rows(sums, 0), all_rows(sums, 4)
    square = jnp.maximum(terms, 0.0) / unknowns + epsilon
    scale, norm = lax.rsqrt(square), jnp.sqrt(square)
    flag[0] = jnp.max(jnp.where(terms < CANCEL * size, 1, 0))
    for s in range(S):
        w = [splat(h, BASE + 4 * m + s) for m in range(M)]
        f = splat(scale, s)
        for c in range(C):
            i = s * C + c
            krylov[i] = (image[i] - sum(w[m] * basis[m, i] for m in range(M))) * f
    values = jnp.where(lane >= BASE + 4 * M, norm, h)
    values = jnp.where((lane & 3) == sub, values, 0.0)
    hessenberg[...] = times(values, maps[2])[:S, : M + 1]


def pairs_of(axis):
    count = lax.axis_size(axis)
    rounds = [[(i, i + 1) for i in range(0, count, 2)]]
    if count > 2:
        rounds.append([(i, (i + 1) % count) for i in range(1, count, 2)])
    return [r + [(j, i) for i, j in r] for r in rounds]


def swap(axis, low_side, high_side):
    odd = lax.axis_index(axis) % 2 == 1
    rounds = pairs_of(axis)
    sides = [jnp.where(odd, low_side, high_side), jnp.where(odd, high_side, low_side)]
    return [lax.ppermute(x, axis, pairs) for x, pairs in zip(sides, rounds)]


def by_side(axis, got):
    at = lax.axis_index(axis)
    odd = at % 2 == 1
    first, second = got if len(got) == 2 else (got[0], got[0])
    low, high = jnp.where(odd, first, second), jnp.where(odd, second, first)
    none = jnp.zeros_like(first)
    return jnp.where(at > 0, low, none), jnp.where(at < lax.axis_size(axis) - 1, high, none)


def exchange(rows):
    return lax.all_to_all(rows[:, None], AXES, 0, 0, tiled=True).reshape(rows.shape)


def on_device(basis, inverse_rows, block_diag, couple, coarse_basis, coarse_factor):
    n = lax.axis_size("gx") * lax.axis_size("gy") * lax.axis_size("gz")
    unknowns = float(C * XY * CZ * n)
    two_x = lax.axis_size("gx") > 2
    vectors = basis.reshape(M, S * C, XY, CZ)
    phi = coarse_basis.reshape(K * C, XY, CZ)

    slab = S * C + K * C // 2
    vector, rounded, phi, *slabs = call(
        load_body,
        [
            kept(S * C, XY, CZ),
            kept(S * C, XY, CZ, dtype=jnp.bfloat16),
            kept(K * C, XY, CZ),
            kept(slab, XY, CZ),
            kept(slab, XY, CZ),
        ],
        (in_hbm(vectors), in_hbm(phi)),
        S * C * XY * CZ,
        in_specs=[HBM] * 2,
        scratch=[pltpu.SemaphoreType.DMA((2,))],
    )
    rounded = rounded.reshape(S, C, CX, CY, CZ)
    (rhs,) = call(rhs_body, [kept(n * GATHERED, 128)], (vector, phi), 2 * K * S * C * XY * CZ)
    got = exchange(rhs)
    swapped = [lax.ppermute(x, "gy", pairs) for x, pairs in zip(slabs, pairs_of("gy"))]

    always = lax.axis_index("gx") >= 0

    inverse = inverse_rows.reshape(C, XY, ROWS, CZ)

    def extend(swapped, rounded, phi, vectors, inverse):
        parts = [x[: S * C].reshape(S, C, CX, CY, CZ).astype(rounded.dtype) for x in swapped]
        y_low, y_high = by_side("gy", parts)
        extended = jnp.concatenate([y_low, rounded, y_high], axis=3)
        slabs = swap("gx", extended[:, :, :2], extended[:, :, -2:])
        mine = extended.reshape(S, C, CX * (CY + 4), CZ)
        width = (EXTENT - CX * (CY + 4)) // 2
        low, high = mine[:, :, : SIDE - width], mine[:, :, 2 * SIDE - width :]
        middle = mine[:, :, SIDE - width : 2 * SIDE - width]
        first = lax.axis_index("gx") == 0
        none = jnp.zeros((S, C, width, CZ), rounded.dtype)
        if not two_x:
            ending = jnp.where(
                first, jnp.concatenate([none, low], axis=2), jnp.concatenate([high, none], axis=2)
            )
            middle = jnp.concatenate([middle, ending], axis=2)
        middle = middle.reshape(S, -1, CZ)
        early = call(
            functools.partial(early_body, two_x),
            [kept(BASE, 128), kept(S * C, XY, CZ), kept(*inverse.shape, dtype=inverse.dtype)]
            + [kept(K * C // 4, 8, 128)] * (1 + two_x),
            (phi, in_hbm(vectors), in_hbm(inverse), middle),
            10**10,
            in_specs=[VMEM, HBM, HBM, VMEM],
            scratch=[pltpu.VMEM(vectors.shape, F32), pltpu.SemaphoreType.DMA((C + 1,))],
        )
        slabs, early = lax.optimization_barrier((slabs, early))
        if two_x:
            slabs = [x.reshape(S, C, width, CZ) for x in by_side("gx", slabs)]
            outer = jnp.concatenate([slabs[0], low, high, slabs[1]], axis=2)
        else:
            slab = slabs[0].reshape(S, C, width, CZ)
            outer = jnp.where(
                first, jnp.concatenate([high, slab], axis=2), jnp.concatenate([slab, low], axis=2)
            )
        return [outer.reshape(S, -1, CZ)] + list(early)

    def unused(swapped, rounded, phi, vectors, inverse):
        return [
            jnp.zeros((S, C * SIDE * (1 + two_x), CZ), rounded.dtype),
            jnp.zeros((BASE, 128), F32),
            jnp.zeros((S * C, XY, CZ), F32),
            jnp.zeros_like(inverse),
        ] + [jnp.zeros((K * C // 4, 8, 128), F32)] * (1 + two_x)

    columns, gram, part, inverse, *phi_faces = lax.cond(
        always, extend, unused, swapped, rounded, phi, vectors, inverse
    )
    half, quarter = S * C // 2, (K + S) * C // 4
    sends = [shape(half, 8, 128)] * 2 + [shape(quarter, 8, 128)] * (2 if two_x else 1)
    stride = (len(slots(two_x)) + 1) // 2 + 1
    shares, loc, *sends = call(
        functools.partial(local_body, two_x),
        [kept(n * stride, 128), shape(S * C, XY, CZ)] + sends,
        (inverse, columns, part, got, coarse_factor, *phi_faces),
        2 * S * C * XY * C * SIDE * CZ,
    )

    def trade(*sends):
        x_faces = [lax.ppermute(x, "gx", pairs) for x, pairs in zip(sends[2:], pairs_of("gx"))]
        return [lax.ppermute(x, "gy", pairs) for x, pairs in zip(sends, pairs_of("gy"))] + x_faces

    def untouched(*sends):
        return list(sends)

    coarse = exchange(shares)
    faces = lax.cond(always, trade, untouched, *sends)
    pre, image, sent = call(
        functools.partial(image_body, two_x),
        [kept(S * C, XY, CZ), kept(S * C, XY, CZ), kept(n, 128)],
        (
            loc,
            phi,
            block_diag.reshape(C * C, XY, CZ),
            couple.reshape(6 * C, XY, CZ),
            vectors,
            gram,
            coarse,
            got,
            *swapped,
            *faces,
        ),
        2 * S * C * XY * CZ * 40,
    )
    products = exchange(sent)
    maps, fixed = tables()
    krylov, hessenberg, flag = call(
        functools.partial(finish_body, unknowns),
        [shape(S * C, XY, CZ), shape(S, M + 1), pltpu.SMEM((1,), jnp.int32)],
        (products, image, vectors, jnp.asarray(maps), jnp.asarray(fixed)),
        2 * S * C * XY * CZ * 8,
        out_specs=[VMEM, VMEM, pl.BlockSpec(memory_space=pltpu.SMEM)],
    )

    def exact(image, vectors, krylov, hessenberg):
        h = hessenberg[:, :M]
        left = image.reshape(S, C, XY, CZ) - jnp.sum(
            h.T[:, :, None, None, None] * vectors.reshape(M, S, C, XY, CZ), axis=0
        )
        squares = jnp.zeros((1, 128), F32).at[0, :S].set(jnp.sum(left * left, axis=(1, 2, 3)))
        squares = jnp.sum(exchange(jnp.broadcast_to(squares, (n, 128))), axis=0)[:S]
        norm = jnp.sqrt(squares / unknowns + epsilon)
        return (
            (left / norm[:, None, None, None]).reshape(S * C, XY, CZ),
            jnp.concatenate([h, norm[:, None]], axis=1),
        )

    def as_is(image, vectors, krylov, hessenberg):
        return krylov, hessenberg

    krylov, hessenberg = lax.cond(
        flag[0] > 0, exact, as_is, image, vectors, krylov, hessenberg
    )
    krylov, pre = lax.optimization_barrier((krylov, pre))
    cells = (S, C, CX, CY, CZ)
    return krylov.reshape(cells), pre.reshape(cells), hessenberg


def solution(mesh):
    return jax.shard_map(
        on_device,
        mesh=mesh,
        in_specs=(
            P(None, None, None, "gx", "gy", "gz"),
            P(None, "gx", "gy", None, "gz"),
            P(None, None, "gx", "gy", "gz"),
            P(None, None, "gx", "gy", "gz"),
            P(None, None, "gx", "gy", "gz"),
            P(AXES, None),
        ),
        out_specs=(P(None, None, "gx", "gy", "gz"), P(None, None, "gx", "gy", "gz"), P()),
        check_vma=False,
    )
```

```python
import functools

import jax
import jax.numpy as jnp
import numpy as np
from jax import lax
from jax.experimental import pallas as pl
from jax.experimental.pallas import tpu as pltpu
from jax.sharding import PartitionSpec as P

C = 4
CX = 4
CY = 2
CZ = 128
S = 4
M = 6
K = 16
XY = CX * CY
GATHERED = 1 + K * C * XY // CZ
EXTENT = (CX + 4) * (CY + 4)
SIDE = EXTENT // 3
ROWS = C * EXTENT
AXES = ("gx", "gy", "gz")
PAIRS = [(m, n) for m in range(M) for n in range(m, M)]
BASE = 88
CANCEL = 1e-2

epsilon = 1e-06

VMEM = pl.BlockSpec(memory_space=pltpu.VMEM)
HBM = pl.BlockSpec(memory_space=pltpu.HBM)
F32 = jnp.float32


def call(body, outs, operands, flops, in_specs=None, out_specs=None, scratch=()):
    size = sum(int(np.prod(x.shape)) * x.dtype.itemsize for x in list(operands) + list(outs))
    return pl.pallas_call(
        body,
        out_shape=tuple(outs),
        in_specs=in_specs or [VMEM] * len(operands),
        out_specs=tuple(out_specs or [VMEM] * len(outs)),
        scratch_shapes=list(scratch),
        compiler_params=pltpu.CompilerParams(vmem_limit_bytes=24 * 1024 * 1024),
        cost_estimate=pl.CostEstimate(flops=flops, bytes_accessed=size, transcendentals=0),
    )(*operands)


def shape(*dims, dtype=F32):
    return jax.ShapeDtypeStruct(dims, dtype)


def kept(*dims, dtype=F32):
    return pltpu.VMEM(dims, dtype)


def in_hbm(x):
    return pltpu.with_memory_space_constraint(x, pltpu.HBM)


def iota(axis):
    return lax.broadcasted_iota(jnp.int32, (8, 128), axis)


def rolled(x, shift, axis):
    return pltpu.roll(x, shift % x.shape[axis], axis)


def row_sums(blocks):
    sub = iota(0)
    for bit in (4, 2, 1):
        low = (sub & bit) == 0
        half = len(blocks) // 2
        blocks = [
            jnp.where(
                low,
                blocks[i] + rolled(blocks[i], -bit, 0),
                blocks[i + half] + rolled(blocks[i + half], bit, 0),
            )
            for i in range(half)
        ]
    return blocks[0]


def thirds(x):
    parts = []
    for _ in range(3):
        parts.append(x.astype(jnp.bfloat16))
        x = x - parts[-1].astype(F32)
    return parts


def across(left, right):
    left = left.astype(jnp.bfloat16)
    return sum(
        lax.dot_general(left, part, (((1,), (1,)), ((), ())), preferred_element_type=F32)
        for part in thirds(right)
    )


def times(x, table):
    rows = jnp.concatenate([p.astype(F32) for p in thirds(x)] + [jnp.zeros((8, 128), F32)], 0)
    y = jnp.dot(rows.astype(jnp.bfloat16), table, preferred_element_type=F32)
    return y[:8] + y[8:16] + y[16:24]


def all_rows(x, t):
    return jnp.broadcast_to(x[t : t + 1, :], (8, 128))


def splat(x, lane):
    return jnp.broadcast_to(x[:, lane : lane + 1], (8, 128))


def ends():
    sub, lane = iota(0), iota(1)
    pick = ((sub == 0) & (lane == 0)) | ((sub == 1) & (lane == CZ - 1))
    return jnp.where(pick, 1.0, 0.0).astype(F32)


def both_sides(axis):
    at = lax.axis_index(axis)
    return at > 0, at < lax.axis_size(axis) - 1


def place():
    x, y, z = (lax.axis_index(a) for a in AXES)
    ny, nz = lax.axis_size("gy"), lax.axis_size("gz")
    return (x * ny + y) * nz + z, z > 0, z < nz - 1


def y_faces(first, second):
    even = (iota(0) & 1) == 0
    low = jnp.where(even, first, rolled(second, 1, 0))
    high = jnp.where(even, rolled(first, -1, 0), second)
    return low, high


def load_body(basis, phi, vector, rounded, phi_kept, to_first, to_second, sems):
    copies = [
        pltpu.make_async_copy(basis.at[M - 1], vector, sems.at[0]),
        pltpu.make_async_copy(phi, phi_kept, sems.at[1]),
    ]
    for copy in copies:
        copy.start()
    odd = lax.axis_index("gy") % 2 == 1
    copies[0].wait()
    low = vector[...].astype(jnp.bfloat16)
    rounded[...] = low
    to_first[: S * C] = low.astype(F32)
    to_second[: S * C] = low.astype(F32)
    copies[1].wait()
    half = K * C // 2
    for i in range(half):
        low, high = y_faces(phi_kept[i], phi_kept[half + i])
        to_first[S * C + i] = jnp.where(odd, low, high)
        to_second[S * C + i] = jnp.where(odd, high, low)


def rhs_body(vector, phi, out):
    rows = []
    for s in range(S):
        v = [vector[s * C + c] for c in range(C)]
        prods = [sum(phi[k * C + c] * v[c] for c in range(C)) for k in range(K)]
        rows.append(row_sums(prods[:8]))
        rows.append(row_sums(prods[8:]))
    rows.append(jnp.zeros((64, 128), F32))
    rhs = across(jnp.ones((8, 128), F32), jnp.concatenate(rows, 0))
    faces = across(ends(), phi[...].reshape(K * C * XY, CZ))
    n = out.shape[0] // GATHERED
    me, _, _ = place()
    later = lax.broadcasted_iota(jnp.int32, (n, 128), 0) > me
    out[pl.ds(0, n, stride=GATHERED), :] = jnp.broadcast_to(rhs[0:1], (n, 128))
    for r in range(GATHERED - 1):
        row = faces[:, 128 * r : 128 * r + 128]
        out[pl.ds(r + 1, n, stride=GATHERED), :] = jnp.where(later, row[1:2], row[0:1])


def x_faces(blocks, sends, at):
    odd = lax.axis_index("gx") % 2 == 1
    group = iota(0) >> 1
    count = len(blocks) // 4
    for i in range(count):
        low = high = None
        for g in range(4):
            x = blocks[g * count + i]
            to_low, to_high = rolled(x, 2 * g, 0), rolled(x, 2 * g - 6, 0)
            low = to_low if low is None else jnp.where(group == g, to_low, low)
            high = to_high if high is None else jnp.where(group == g, to_high, high)
        sends[0][at + i] = jnp.where(odd, low, high)
        if len(sends) > 1:
            sends[1][at + i] = jnp.where(odd, high, low)


def solve(inv, cols, starts, done, ready=None, unroll=False):
    def one(c, carry):
        if ready is not None:
            ready(c)
        total = [[jnp.zeros((8, 128), F32) for _ in range(XY)] for _ in range(S)]
        for at, j in starts:
            seen = [cols[s, j : j + SIDE, :].astype(F32) for s in range(S)]
            for i in range(XY):
                w = inv[c, i, pl.ds(at, SIDE), :].astype(F32)
                for s in range(S):
                    part = w * seen[s]
                    total[s][i] = total[s][i] + part[:8] + part[8:]
        for s in range(S):
            done(s * C + c, row_sums(total[s]))
        return carry

    if unroll:
        for c in range(C):
            one(c, 0)
    else:
        lax.fori_loop(0, C, one, 0)


def edge(first):
    return pl.multiple_of(jnp.where(first, 0, 2 * SIDE), SIDE)


def early_body(two_x, phi, basis, inv, cols, gram, loc, inv_kept, *refs):
    phi_faces, (vectors, sems) = refs[: 1 + two_x], refs[1 + two_x :]
    fetch = pltpu.make_async_copy(basis, vectors, sems.at[C])
    fetch.start()

    def copy(c):
        return pltpu.make_async_copy(inv.at[c], inv_kept.at[c], sems.at[c])

    for c in range(C):
        copy(c).start()
    x_faces([phi[i] for i in range(K * C)], phi_faces, 0)

    def done(i, x):
        loc[i] = x

    if two_x:
        starts = [(EXTENT * c + SIDE, SIDE * c) for c in range(C)]
    else:
        at = edge(lax.axis_index("gx") == 0)
        starts = [(EXTENT * c + SIDE, 2 * SIDE * c) for c in range(C)]
        starts += [(EXTENT * c + at, 2 * SIDE * c + SIDE) for c in range(C)]
    solve(inv_kept, cols, starts, done, lambda c: copy(c).wait())
    fetch.wait()
    rows = []
    for m, n in PAIRS:
        for s in range(S):
            rows.append(sum(vectors[m, s * C + c] * vectors[n, s * C + c] for c in range(C)))
    rows += [jnp.zeros((8, 128), F32)] * (BASE - len(rows))
    for g in range(0, BASE, 8):
        gram[g : g + 8, :] = row_sums(rows[g : g + 8])


def slots(two_x):
    return ["own", "ylo", "yhi"] + (["xlo", "xhi"] if two_x else ["x"]) + ["zlo", "zhi"]


def factor_body(two_x, got, factor, out):
    n = factor.shape[1] // K
    stride = out.shape[0] // n
    sub, lane = iota(0), iota(1)
    mine = [(lane >> 4) == ((sub + s) & 7) for s in range(S)]
    columns = []
    for b in range(n // 8):
        rows = factor[:, 128 * b : 128 * b + 128]
        columns.append([rows] + [rolled(rows, K * s, 1) for s in range(1, S)])
    image = [jnp.zeros((K, 128), F32) for _ in range(S)]
    for b in range(n // 8):
        rhs = got[pl.ds(8 * GATHERED * b, 8, stride=GATHERED), :]
        rhs = pltpu.roll(rhs, 0, 1, stride=K, stride_axis=0)
        for s in range(S):
            row = jnp.sum(jnp.where(mine[s], rhs, 0.0), axis=0, keepdims=True)
            image[s] = image[s] + columns[b][s] * row
    image = [jnp.sum(x, axis=1, keepdims=True) for x in image]
    shares = []
    for b in range(n // 8):
        block = jnp.zeros((8, 128), F32)
        for s in range(S):
            row = jnp.sum(columns[b][s] * image[s], axis=0, keepdims=True)
            block = jnp.where(mine[s], row, block)
        for bit in (1, 2, 4):
            block = jnp.where((sub & bit) == 0, block, rolled(block, -K * bit, 1))
        shares.append(jnp.where(lane < S * K, block, 0.0))
    shares = jnp.concatenate(shares, 0)
    nz = lax.axis_size("gz")
    plane = lax.axis_size("gy") * nz
    shift = {"own": 0, "ylo": nz, "yhi": -nz, "x": plane, "xlo": plane, "xhi": -plane, "zlo": 1, "zhi": -1}
    names = slots(two_x)
    for t in range(0, len(names), 2):
        pair = [rolled(shares, shift[x], 0) if shift[x] else shares for x in names[t : t + 2]]
        row = pair[0] if len(pair) == 1 else pair[0] + rolled(pair[1], 64, 1)
        out[pl.ds(t // 2, n, stride=stride), :] = row
    face = (len(names) + 1) // 2
    for t in range(face, stride):
        out[pl.ds(t, n, stride=stride), :] = jnp.zeros((n, 128), F32)


def send_ends(two_x, locz, out):
    face = (len(slots(two_x)) + 1) // 2
    stride = face + 1
    me, below, above = place()

    @pl.when(below)
    def _():
        out[pl.ds((me - 1) * stride + face, 1), :] = locz[0:1]

    @pl.when(above)
    def _():
        out[pl.ds((me + 1) * stride + face, 1), :] = locz[1:2]


def local_body(two_x, inv, cols, early, got, factor, *refs):
    phi_faces, (out, loc, *sends) = refs[: 1 + two_x], refs[1 + two_x :]

    def done(i, x):
        loc[i] = early[i] + x

    if two_x:
        starts = [(EXTENT * c, 2 * SIDE * c) for c in range(C)]
        starts += [(EXTENT * c + 2 * SIDE, 2 * SIDE * c + SIDE) for c in range(C)]
    else:
        at = edge(lax.axis_index("gx") == 1)
        starts = [(EXTENT * c + at, SIDE * c) for c in range(C)]
    factor_body(two_x, got, factor, out)
    solve(inv, cols, starts, done, unroll=True)
    send_ends(two_x, across(ends(), loc[...].reshape(S * C * XY, CZ)), out)
    odd_y = lax.axis_index("gy") % 2 == 1
    for i in range(S * C // 2):
        low, high = y_faces(loc[i], loc[S * C // 2 + i])
        sends[0][i] = jnp.where(odd_y, low, high)
        sends[1][i] = jnp.where(odd_y, high, low)
    x_faces([loc[i] for i in range(S * C)], sends[2:], 0)
    for x, known in zip(sends[2:], phi_faces):
        x[C:] = known[...]


def staggered(coef, group):
    out = coef
    for g in range(1, 4):
        out = jnp.where(group == g, rolled(coef, -4 * g, 1), out)
    return out


def image_body(two_x, loc, phi, diagonal, couple, basis, gram, coarse, got, *rest):
    slabs, faces, (pre, image, sent) = rest[:2], rest[2:-3], rest[-3:]
    n = sent.shape[0]
    stride = coarse.shape[0] // n
    sub, lane = iota(0), iota(1)
    even = (sub & 1) == 0
    if stride == 4:
        total = coarse[0:8, :]
        for b in range(1, coarse.shape[0] // 8):
            total = total + coarse[8 * b : 8 * b + 8, :]
        total = total + rolled(total, 4, 0)
        totals = [all_rows(total, t) for t in range(stride - 1)]
    else:
        totals = [
            jnp.broadcast_to(
                jnp.sum(coarse[pl.ds(t, n, stride=stride), :], axis=0, keepdims=True), (8, 128)
            )
            for t in range(stride - 1)
        ]
    names = slots(two_x)

    def coefs(name):
        at = names.index(name)
        return totals[at // 2] if at % 2 == 0 else rolled(totals[at // 2], 64, 1)

    me, below, above = place()

    lower = sub < 4
    at = [jnp.where(below, me - 1, me), jnp.where(above, me + 1, me)]
    parts = None
    for r in range(8):
        row = got[pl.ds(at[r // 4] * GATHERED + 1 + r % 4, 1), :]
        row = jnp.broadcast_to(row, (8, 128))
        parts = row if r == 0 else jnp.where(sub == r, row, parts)
    coef = staggered(jnp.where(lower, coefs("zlo"), coefs("zhi")), sub & 3)
    z = None
    for s in range(S):
        w = splat(coef, s * K)
        for k in range(1, 4):
            w = jnp.where((lane >> 5) == k, splat(coef, s * K + k), w)
        part = parts * w
        for shift in (32, 64):
            part = part + rolled(part, shift, 1)
        z = part if z is None else jnp.where((lane >> 5) == s, part, z)
    for shift in (1, 2):
        z = z + rolled(z, -shift, 0)
    rows = [coarse[pl.ds(x * stride + stride - 1, 1), :] for x in at]
    rows = [jnp.broadcast_to(x, (8, 128)) for x in rows]
    z = z + jnp.where(lower, rows[0], rows[1])
    there = jnp.where(lower, below.astype(jnp.int32), above.astype(jnp.int32)) == 1
    columns = jnp.transpose(jnp.where(there, z, 0.0))

    odd_y = lax.axis_index("gy") % 2 == 1
    odd_x = lax.axis_index("gx") % 2 == 1

    has_y, has_x = both_sides("gy"), both_sides("gx")

    def y_side(slab, face, coef):
        coef = jnp.where(even, coef, rolled(coef, -K // 2, 1))
        sums = []
        for s in range(S):
            mine = even if s < 2 else ~even
            part = [jnp.where(mine, face[(s % 2) * C + c], 0.0) for c in range(C)]
            for k in range(K // 2):
                w = splat(coef, s * K + k)
                for c in range(C):
                    part[c] = part[c] + w * slab[S * C + k * C + c]
            sums += part
        return sums

    def x_side(face, coef):
        coef = staggered(coef, sub >> 1)
        sums = []
        for s in range(S):
            part = [jnp.where((sub >> 1) == s, face[c], 0.0) for c in range(C)]
            for k in range(K // 4):
                w = splat(coef, s * K + k)
                for c in range(C):
                    part[c] = part[c] + w * face[C + k * C + c]
            for x in part:
                x = x + rolled(x, 2, 0)
                sums.append(x + rolled(x, 4, 0))
        return sums

    ylo, yhi = coefs("ylo"), coefs("yhi")
    y_first = y_side(slabs[0], faces[0], jnp.where(odd_y, ylo, yhi))
    y_second = y_side(slabs[1], faces[1], jnp.where(odd_y, yhi, ylo))
    if two_x:
        xlo, xhi = coefs("xlo"), coefs("xhi")
        x_first = x_side(faces[2], jnp.where(odd_x, xlo, xhi))
        x_second = x_side(faces[3], jnp.where(odd_x, xhi, xlo))
    else:
        x_first = x_side(faces[2], coefs("x"))
        x_second = x_first

    own = coefs("own")
    p = [loc[i] for i in range(S * C)]
    for s in range(S):
        for k in range(K):
            w = splat(own, s * K + k)
            for c in range(C):
                p[s * C + c] = p[s * C + c] + w * phi[k * C + c]

    for s in range(S):
        sides = []
        for c in range(C):
            i = s * C + c
            x = p[i]
            pre[i] = x
            zl = jnp.broadcast_to(columns[i * XY : (i + 1) * XY, 0:1], (8, 128))
            zh = jnp.broadcast_to(columns[i * XY : (i + 1) * XY, 4:5], (8, 128))
            y_low = jnp.where(odd_y, y_first[i], y_second[i])
            y_high = jnp.where(odd_y, y_second[i], y_first[i])
            x_low = jnp.where(odd_x, x_first[i], x_second[i])
            x_high = jnp.where(odd_x, x_second[i], x_first[i])
            y_low = jnp.where(has_y[0], y_low + rolled(y_low, -1, 0), 0.0)
            y_high = jnp.where(has_y[1], y_high + rolled(y_high, 1, 0), 0.0)
            x_low, x_high = jnp.where(has_x[0], x_low, 0.0), jnp.where(has_x[1], x_high, 0.0)
            sides = [
                jnp.where(sub < CY, x_low, rolled(x, CY, 0)),
                jnp.where(sub >= XY - CY, x_high, rolled(x, -CY, 0)),
                jnp.where(even, y_low, rolled(x, 1, 0)),
                jnp.where(even, rolled(x, -1, 0), y_high),
                jnp.where(lane == 0, zl, rolled(x, 1, 1)),
                jnp.where(lane == CZ - 1, zh, rolled(x, -1, 1)),
            ]
            a = sum(diagonal[c * C + d] * p[s * C + d] for d in range(C))
            for d, side in enumerate(sides):
                a = a - couple[d * C + c] * side
            image[i] = a

    rows = []
    for m in range(M):
        for s in range(S):
            rows.append(sum(basis[m, s * C + c] * image[s * C + c] for c in range(C)))
    for s in range(S):
        rows.append(sum(image[s * C + c] * image[s * C + c] for c in range(C)))
    rows += [jnp.zeros((8, 128), F32)] * 4
    sums = [row_sums(rows[g : g + 8]) for g in range(0, 32, 8)]
    sums = jnp.concatenate([gram[...]] + sums + [jnp.zeros((8, 128), F32)], 0)
    row = across(jnp.ones((8, 128), F32), sums)
    sent[...] = jnp.broadcast_to(row[None], (n // 8, 8, 128)).reshape(n, 128)


def tables():
    first = np.zeros((128, 128), np.float32)
    second = np.zeros((128, 128), np.float32)
    out = np.zeros((128, 128), np.float32)
    fixed = np.zeros((8, 128), np.float32)
    for s in range(S):
        for at, (m, n) in enumerate(PAIRS):
            first[BASE + 4 * m + s, 4 * at + s] = 1
            second[BASE + 4 * n + s, 4 * at + s] = 1
            fixed[2, 4 * at + s] = 1 if m == n else 2
        for m in range(M):
            lane = BASE + 4 * m + s
            first[lane, lane] = 1
            fixed[1, lane] = 1
            fixed[2, lane] = -2
        lane = BASE + 4 * M + s
        fixed[0, lane] = fixed[1, lane] = fixed[2, lane] = 1
        for i in range(M + 1):
            out[BASE + 4 * i + s, i] = 1
    lanes = np.arange(128)
    fold = (lanes[:, None] % 4 == lanes[None, :] % 4).astype(np.float32)
    return np.stack([first, second, out, fold]).astype(jnp.bfloat16), fixed


def finish_body(unknowns, got, image, basis, maps, fixed, krylov, hessenberg, flag):
    sub, lane = iota(0), iota(1)
    total = got[0:8, :]
    for b in range(1, got.shape[0] // 8):
        total = total + got[8 * b : 8 * b + 8, :]
    for shift in (4, 2, 1):
        total = total + rolled(total, shift, 0)
    h = total / unknowns

    terms = total * all_rows(fixed, 2)
    terms = terms * (times(h, maps[0]) + all_rows(fixed, 0)) * (times(h, maps[1]) + all_rows(fixed, 1))
    sums = times(jnp.where(sub < 4, terms, jnp.abs(terms)), maps[3])
    terms, size = all_rows(sums, 0), all_rows(sums, 4)
    square = jnp.maximum(terms, 0.0) / unknowns + epsilon
    scale, norm = lax.rsqrt(square), jnp.sqrt(square)
    flag[0] = jnp.max(jnp.where(terms < CANCEL * size, 1, 0))
    for s in range(S):
        w = [splat(h, BASE + 4 * m + s) for m in range(M)]
        f = splat(scale, s)
        for c in range(C):
            i = s * C + c
            krylov[i] = (image[i] - sum(w[m] * basis[m, i] for m in range(M))) * f
    values = jnp.where(lane >= BASE + 4 * M, norm, h)
    values = jnp.where((lane & 3) == sub, values, 0.0)
    hessenberg[...] = times(values, maps[2])[:S, : M + 1]


def pairs_of(axis):
    count = lax.axis_size(axis)
    rounds = [[(i, i + 1) for i in range(0, count, 2)]]
    if count > 2:
        rounds.append([(i, (i + 1) % count) for i in range(1, count, 2)])
    return [r + [(j, i) for i, j in r] for r in rounds]


def swap(axis, low_side, high_side):
    odd = lax.axis_index(axis) % 2 == 1
    rounds = pairs_of(axis)
    sides = [jnp.where(odd, low_side, high_side), jnp.where(odd, high_side, low_side)]
    return [lax.ppermute(x, axis, pairs) for x, pairs in zip(sides, rounds)]


def by_side(axis, got):
    at = lax.axis_index(axis)
    odd = at % 2 == 1
    first, second = got if len(got) == 2 else (got[0], got[0])
    low, high = jnp.where(odd, first, second), jnp.where(odd, second, first)
    none = jnp.zeros_like(first)
    return jnp.where(at > 0, low, none), jnp.where(at < lax.axis_size(axis) - 1, high, none)


def exchange(rows):
    return lax.all_to_all(rows[:, None], AXES, 0, 0, tiled=True).reshape(rows.shape)


def on_device(basis, inverse_rows, block_diag, couple, coarse_basis, coarse_factor):
    n = lax.axis_size("gx") * lax.axis_size("gy") * lax.axis_size("gz")
    unknowns = float(C * XY * CZ * n)
    two_x = lax.axis_size("gx") > 2
    vectors = basis.reshape(M, S * C, XY, CZ)
    phi = coarse_basis.reshape(K * C, XY, CZ)

    slab = S * C + K * C // 2
    vector, rounded, phi, *slabs = call(
        load_body,
        [
            kept(S * C, XY, CZ),
            kept(S * C, XY, CZ, dtype=jnp.bfloat16),
            kept(K * C, XY, CZ),
            kept(slab, XY, CZ),
            kept(slab, XY, CZ),
        ],
        (in_hbm(vectors), in_hbm(phi)),
        S * C * XY * CZ,
        in_specs=[HBM] * 2,
        scratch=[pltpu.SemaphoreType.DMA((2,))],
    )
    rounded = rounded.reshape(S, C, CX, CY, CZ)
    (rhs,) = call(rhs_body, [kept(n * GATHERED, 128)], (vector, phi), 2 * K * S * C * XY * CZ)
    got = exchange(rhs)
    swapped = [lax.ppermute(x, "gy", pairs) for x, pairs in zip(slabs, pairs_of("gy"))]

    always = lax.axis_index("gx") >= 0

    inverse = inverse_rows.reshape(C, XY, ROWS, CZ)

    def extend(swapped, rounded, phi, vectors, inverse):
        parts = [x[: S * C].reshape(S, C, CX, CY, CZ).astype(rounded.dtype) for x in swapped]
        y_low, y_high = by_side("gy", parts)
        extended = jnp.concatenate([y_low, rounded, y_high], axis=3)
        slabs = swap("gx", extended[:, :, :2], extended[:, :, -2:])
        mine = extended.reshape(S, C, CX * (CY + 4), CZ)
        width = (EXTENT - CX * (CY + 4)) // 2
        low, high = mine[:, :, : SIDE - width], mine[:, :, 2 * SIDE - width :]
        middle = mine[:, :, SIDE - width : 2 * SIDE - width]
        first = lax.axis_index("gx") == 0
        none = jnp.zeros((S, C, width, CZ), rounded.dtype)
        if not two_x:
            ending = jnp.where(
                first, jnp.concatenate([none, low], axis=2), jnp.concatenate([high, none], axis=2)
            )
            middle = jnp.concatenate([middle, ending], axis=2)
        middle = middle.reshape(S, -1, CZ)
        early = call(
            functools.partial(early_body, two_x),
            [kept(BASE, 128), kept(S * C, XY, CZ), kept(*inverse.shape, dtype=inverse.dtype)]
            + [kept(K * C // 4, 8, 128)] * (1 + two_x),
            (phi, in_hbm(vectors), in_hbm(inverse), middle),
            10**10,
            in_specs=[VMEM, HBM, HBM, VMEM],
            scratch=[pltpu.VMEM(vectors.shape, F32), pltpu.SemaphoreType.DMA((C + 1,))],
        )
        slabs, early = lax.optimization_barrier((slabs, early))
        if two_x:
            slabs = [x.reshape(S, C, width, CZ) for x in by_side("gx", slabs)]
            outer = jnp.concatenate([slabs[0], low, high, slabs[1]], axis=2)
        else:
            slab = slabs[0].reshape(S, C, width, CZ)
            outer = jnp.where(
                first, jnp.concatenate([high, slab], axis=2), jnp.concatenate([slab, low], axis=2)
            )
        return [outer.reshape(S, -1, CZ)] + list(early)

    def unused(swapped, rounded, phi, vectors, inverse):
        return [
            jnp.zeros((S, C * SIDE * (1 + two_x), CZ), rounded.dtype),
            jnp.zeros((BASE, 128), F32),
            jnp.zeros((S * C, XY, CZ), F32),
            jnp.zeros_like(inverse),
        ] + [jnp.zeros((K * C // 4, 8, 128), F32)] * (1 + two_x)

    columns, gram, part, inverse, *phi_faces = lax.cond(
        always, extend, unused, swapped, rounded, phi, vectors, inverse
    )
    half, quarter = S * C // 2, (K + S) * C // 4
    sends = [shape(half, 8, 128)] * 2 + [shape(quarter, 8, 128)] * (2 if two_x else 1)
    stride = (len(slots(two_x)) + 1) // 2 + 1
    shares, loc, *sends = call(
        functools.partial(local_body, two_x),
        [kept(n * stride, 128), shape(S * C, XY, CZ)] + sends,
        (inverse, columns, part, got, coarse_factor, *phi_faces),
        2 * S * C * XY * C * SIDE * CZ,
    )

    def trade(*sends):
        x_faces = [lax.ppermute(x, "gx", pairs) for x, pairs in zip(sends[2:], pairs_of("gx"))]
        return [lax.ppermute(x, "gy", pairs) for x, pairs in zip(sends, pairs_of("gy"))] + x_faces

    def untouched(*sends):
        return list(sends)

    coarse = exchange(shares)
    faces = lax.cond(always, trade, untouched, *sends)
    pre, image, sent = call(
        functools.partial(image_body, two_x),
        [kept(S * C, XY, CZ), kept(S * C, XY, CZ), kept(n, 128)],
        (
            loc,
            phi,
            block_diag.reshape(C * C, XY, CZ),
            couple.reshape(6 * C, XY, CZ),
            vectors,
            gram,
            coarse,
            got,
            *swapped,
            *faces,
        ),
        2 * S * C * XY * CZ * 40,
    )
    products = exchange(sent)
    maps, fixed = tables()
    krylov, hessenberg, flag = call(
        functools.partial(finish_body, unknowns),
        [shape(S * C, XY, CZ), shape(S, M + 1), pltpu.SMEM((1,), jnp.int32)],
        (products, image, vectors, jnp.asarray(maps), jnp.asarray(fixed)),
        2 * S * C * XY * CZ * 8,
        out_specs=[VMEM, VMEM, pl.BlockSpec(memory_space=pltpu.SMEM)],
    )

    def exact(image, vectors, krylov, hessenberg):
        h = hessenberg[:, :M]
        left = image.reshape(S, C, XY, CZ) - jnp.sum(
            h.T[:, :, None, None, None] * vectors.reshape(M, S, C, XY, CZ), axis=0
        )
        squares = jnp.zeros((1, 128), F32).at[0, :S].set(jnp.sum(left * left, axis=(1, 2, 3)))
        squares = jnp.sum(exchange(jnp.broadcast_to(squares, (n, 128))), axis=0)[:S]
        norm = jnp.sqrt(squares / unknowns + epsilon)
        return (
            (left / norm[:, None, None, None]).reshape(S * C, XY, CZ),
            jnp.concatenate([h, norm[:, None]], axis=1),
        )

    def as_is(image, vectors, krylov, hessenberg):
        return krylov, hessenberg

    krylov, hessenberg = lax.cond(
        flag[0] > 0, exact, as_is, image, vectors, krylov, hessenberg
    )
    krylov, pre = lax.optimization_barrier((krylov, pre))
    cells = (S, C, CX, CY, CZ)
    return krylov.reshape(cells), pre.reshape(cells), hessenberg


def solution(mesh):
    return jax.shard_map(
        on_device,
        mesh=mesh,
        in_specs=(
            P(None, None, None, "gx", "gy", "gz"),
            P(None, "gx", "gy", None, "gz"),
            P(None, None, "gx", "gy", "gz"),
            P(None, None, "gx", "gy", "gz"),
            P(None, None, "gx", "gy", "gz"),
            P(AXES, None),
        ),
        out_specs=(P(None, None, "gx", "gy", "gz"), P(None, None, "gx", "gy", "gz"), P()),
        check_vma=False,
    )
```
